32 devices in a mesh: ctx: 8 (over z, x), chan: 4 (over y, core).
Axes of the slice: x: 2, y: 2, z: 4, core: 2. Of those that a mesh axis runs over, the one named last changes fastest.
Arguments:
- signal: bfloat16 [128, 8192], P('chan', 'ctx'), may hold values from -6 to 6
- gating: bfloat16 [128, 8192], P('chan', 'ctx'), may hold values from -6 to 6
- cotangent: bfloat16 [128, 8192], P('chan', 'ctx'), may hold values from -6 to 6
- filters: float32 [32, 8192], P(None, 'ctx'), may hold values from -1 to 1
- skip_weight: float32 [128], P('chan'), may hold values from 0.5 to 1.5
Outputs:
- grad_signal: bfloat16 [128, 8192], P('chan', 'ctx')
- grad_gating: bfloat16 [128, 8192], P('chan', 'ctx')
- grad_filters: float32 [32, 8192], P('chan', 'ctx')
The draws below stay inside these ranges and needn't reach their ends.
All inputs are finite; a program needn't handle non-finite values.
Results may differ from the reference program's by a relative error of at most 0.0075.
Values may be sent and summed in bfloat16 or wider, within the bound.
No kernel may reach another device: no remote copies, remote signals or barrier semaphores. Data moves between devices by JAX's collectives and lax.ppermute only.
A program may use at most 64 MiB of HBM per device.

```python
import math
import jax
import jax.numpy as jnp
from jax import lax

C = 128
FILT = 32
SEQ = 8192


def draw_filters(key, part):
    key_taps, key_reach = jax.random.split(jax.random.fold_in(key, 7))
    positions = jnp.arange(SEQ, dtype=jnp.float32)[None, :]
    lengths = jnp.exp(jax.random.uniform(key_reach, (FILT, 1), minval=math.log(40.0), maxval=math.log(4.0 * SEQ)))
    tap_values = jnp.clip(jax.random.normal(key_taps, (FILT, SEQ)), -4.0, 4.0)
    scaling = 1.0 / jnp.sqrt(jnp.minimum(lengths / 2.0, float(SEQ)))
    return (tap_values * jnp.exp(-positions / lengths) * scaling).astype(jnp.float32)


def block_scale(rng, extent, pieces, least, top_value):
    level, own = 1.0, jax.random.fold_in(rng, 6)
    for axis_at, blocks in pieces:
        draws = jnp.exp(jax.random.uniform(jax.random.fold_in(own, axis_at), (blocks,), jnp.float32, least / len(pieces), top_value / len(pieces)))
        level = level * jnp.repeat(draws, extent[axis_at] // blocks).reshape([-1 if axis == axis_at else 1 for axis in range(len(extent))])
    return level


def bell_draw(key, shape, width, reach, shards=(), held_as=jnp.bfloat16):
    values = width * jax.random.normal(key, shape, jnp.float32)
    if shards:
        values = values * block_scale(key, shape, shards, -0.22, 0.18)
    return jnp.clip(values, -reach, reach).astype(held_as)


def setup_inputs(seed: int = 0) -> dict:
    key_list = jax.random.split(jax.random.key(seed), 6)
    return {
        "signal": bell_draw(key_list[0], (C, SEQ), 1.0, 6.0, ((0, 4), (1, 8))),
        "gating": bell_draw(key_list[1], (C, SEQ), 1.0, 6.0, ((0, 4), (1, 8))),
        "cotangent": bell_draw(key_list[2], (C, SEQ), 1.0, 6.0, ((0, 4), (1, 8))),
        "filters": draw_filters(jax.random.fold_in(key_list[5], 71), 0),
        "skip_weight": jnp.clip(0.5 + 1.0 * jax.random.uniform(key_list[4], (C,), jnp.float32) ** block_scale(key_list[4], (C,), ((0, 4),), -0.2, 0.2), 0.5, 1.5),
    }


def reference(signal, gating, cotangent, filters, skip_weight):
    group_size = C // FILT
    padded = 2 * SEQ
    normal_scale = 1.0 / math.sqrt(SEQ * group_size)
    gated_grad = (cotangent.astype(jnp.float32) * gating.astype(jnp.float32)).astype(jnp.bfloat16)

    def regroup(array):
        return jnp.transpose(array.reshape(group_size, FILT, SEQ), (1, 0, 2))

    def ungroup(array):
        return jnp.transpose(array, (1, 0, 2)).reshape(C, SEQ)

    def one_filter(items):
        signal_rows, gated_rows, cot_rows, tap_row, weights = items
        signal_float = signal_rows.astype(jnp.float32)
        gated_float = gated_rows.astype(jnp.float32)
        signal_spec = jnp.fft.rfft(signal_float, n=padded, axis=-1)
        gated_spec = jnp.fft.rfft(gated_float, n=padded, axis=-1)
        tap_spec = jnp.fft.rfft(tap_row, n=padded)
        conv_out = jnp.fft.irfft(signal_spec * tap_spec[None, :], n=padded, axis=-1)[:, :SEQ]
        outputs = conv_out + weights[:, None] * signal_float
        grad_gating = (cot_rows.astype(jnp.float32) * outputs).astype(jnp.bfloat16)
        back_conv = jnp.fft.irfft(jnp.conj(tap_spec)[None, :] * gated_spec, n=padded, axis=-1)[:, :SEQ]
        grad_signal = (back_conv + weights[:, None] * gated_float).astype(jnp.bfloat16)
        correlation = jnp.fft.irfft(jnp.conj(signal_spec) * gated_spec, n=padded, axis=-1)[:, :SEQ]
        grad_row = (lax.optimization_barrier(jnp.sum(correlation, axis=0)) * normal_scale).astype(jnp.float32)
        return (grad_signal, grad_gating, grad_row)
    per_signal, per_gating, grad_filters = lax.map(one_filter, (regroup(signal), regroup(gated_grad), regroup(cotangent), filters, jnp.transpose(skip_weight.reshape(group_size, FILT))))
    return (ungroup(per_signal), ungroup(per_gating), grad_filters)
```

```python
import functools
import math

import jax
import jax.numpy as jnp
import numpy as np
from jax import lax
from jax.experimental import pallas as pl
from jax.experimental.pallas import tpu as pltpu
from jax.sharding import PartitionSpec as P

LANES = 128


def split_table(table):
    high = table.astype(jnp.bfloat16)
    low = (table - high.astype(np.float64)).astype(jnp.bfloat16)
    return high, low


def dft_tables(rows):
    height = 2 * rows
    padded = height * LANES
    kept = rows + 1
    pad = -kept % 16
    k1 = np.arange(kept)
    n1 = np.arange(rows)
    n2 = np.arange(LANES)
    zeros = lambda table, axis: np.pad(table, [(0, pad if a == axis else 0) for a in range(2)])
    outer = 2.0 * np.pi * (np.outer(k1, n1) % height) / height
    first = np.concatenate([zeros(np.cos(outer), 0), zeros(-np.sin(outer), 0)], axis=0)
    high, low = split_table(first)
    first = np.concatenate([high, low, high, low], axis=1)
    turn = 2.0 * np.pi * (np.outer(k1, n2) % padded) / padded
    twiddle = np.stack([zeros(np.cos(turn), 0), zeros(np.sin(turn), 0)]).astype(np.float32)
    inner = 2.0 * np.pi * (np.outer(n2, n2) % LANES) / LANES
    cosine, sine = np.cos(inner), np.sin(inner)
    second = np.stack(split_table(np.block([[cosine, -sine], [sine, cosine]])))
    weight = np.where((k1 == 0) | (k1 == rows), 1.0, 2.0) / padded
    last = np.concatenate(
        [zeros(np.cos(outer.T) * weight, 1), zeros(-np.sin(outer.T) * weight, 1)], axis=1
    )
    last = np.concatenate(split_table(last), axis=0)
    return first, twiddle, second, last


def dot(left, right):
    return jnp.dot(left, right, preferred_element_type=jnp.float32)


def split(values):
    high = values.astype(jnp.bfloat16)
    return high, (values - high.astype(jnp.float32)).astype(jnp.bfloat16)


def spectral_kernel(
    groups, peers, scale, got_ref, first_ref, twiddle_ref, second_ref, last_ref, out_ref, in_ref, part_ref, spec_ref, back_ref
):
    piece = got_ref.shape[1] // 3
    taps = piece // groups
    rows = peers * piece
    kept = twiddle_ref.shape[1]
    count = 2 * groups
    got = [got_ref[source].astype(jnp.float32) for source in range(peers * groups)]

    def gather(group, start):
        parts = [got[peer * groups + group][start : start + piece] for peer in range(peers)]
        return jnp.concatenate(parts, axis=0).astype(jnp.bfloat16)

    for sequence in range(count):
        group, start = sequence % groups, sequence // groups * piece
        values = gather(group, start)
        in_ref[0:rows, sequence * LANES : (sequence + 1) * LANES] = values
        in_ref[rows : 2 * rows, sequence * LANES : (sequence + 1) * LANES] = values
    tap_high = jnp.concatenate([part[2 * piece : 2 * piece + taps] for part in got], axis=0).astype(jnp.bfloat16)
    tap_low = jnp.concatenate([part[2 * piece + taps : 2 * piece + 2 * taps] for part in got], axis=0).astype(jnp.bfloat16)
    tap_in = jnp.concatenate([tap_high, tap_high, tap_low, tap_low], axis=0)
    cosine, sine = twiddle_ref[0], twiddle_ref[1]
    stage = dot(first_ref[:, : 2 * rows], in_ref[...])
    tap_stage = dot(first_ref[...], tap_in)
    total = (count + 1) * kept
    for sequence in range(count + 1):
        source = tap_stage if sequence == count else stage[:, sequence * LANES : (sequence + 1) * LANES]
        real, imag = source[:kept], source[kept:]
        turned = jnp.concatenate([real * cosine + imag * sine, imag * cosine - real * sine], axis=1)
        high, low = split(turned)
        part_ref[sequence * kept : (sequence + 1) * kept] = high
        part_ref[total + sequence * kept : total + (sequence + 1) * kept] = low

    def second_stage():
        both = dot(part_ref[...], second_ref[0])
        spec_ref[...] = both[:total] + both[total:] + dot(part_ref[:total], second_ref[1])

    second_stage()
    tap = spec_ref[count * kept : total]
    tap_real, tap_imag = tap[:, :LANES], tap[:, LANES:]
    corr_real = corr_imag = None

    def put(sequence, real, imag):
        high, low = split(jnp.concatenate([imag, real], axis=1))
        part_ref[sequence * kept : (sequence + 1) * kept] = high
        part_ref[total + sequence * kept : total + (sequence + 1) * kept] = low

    for group in range(groups):
        sig = spec_ref[group * kept : (group + 1) * kept]
        gat = spec_ref[(groups + group) * kept : (groups + group + 1) * kept]
        sr, si, gr, gi = sig[:, :LANES], sig[:, LANES:], gat[:, :LANES], gat[:, LANES:]
        put(group, sr * tap_real - si * tap_imag, sr * tap_imag + si * tap_real)
        put(groups + group, tap_real * gr + tap_imag * gi, tap_real * gi - tap_imag * gr)
        cr, ci = sr * gr + si * gi, sr * gi - si * gr
        corr_real, corr_imag = (cr, ci) if corr_real is None else (corr_real + cr, corr_imag + ci)
    put(count, corr_real * scale, corr_imag * scale)
    second_stage()
    for sequence in range(count + 1):
        both = spec_ref[sequence * kept : (sequence + 1) * kept]
        imag, real = both[:, :LANES], both[:, LANES:]
        turned = jnp.concatenate([real * cosine - imag * sine, imag * cosine + real * sine], axis=0)
        high, low = split(turned)
        back_ref[0, :, sequence * LANES : (sequence + 1) * LANES] = high
        back_ref[1, :, sequence * LANES : (sequence + 1) * LANES] = low
    both = dot(last_ref[...], back_ref[0])
    result = both[:rows] + both[rows:] + dot(last_ref[:rows], back_ref[1])
    for peer in range(peers):
        piece_rows = result[peer * piece : (peer + 1) * piece]
        for group in range(groups):
            cut = lambda sequence: piece_rows[:, sequence * LANES : (sequence + 1) * LANES]
            message = jnp.concatenate([cut(group), cut(groups + group), cut(count)], axis=0)
            out_ref[peer * groups + group] = message.astype(jnp.bfloat16)


def spectral_products(got, groups, peers, scale):
    rows = peers * (got.shape[1] // 3)
    tables = dft_tables(rows)
    kept = tables[1].shape[1]
    total = (2 * groups + 1) * kept
    vmem = pl.BlockSpec(memory_space=pltpu.VMEM)
    return pl.pallas_call(
        functools.partial(spectral_kernel, groups, peers, scale),
        out_shape=jax.ShapeDtypeStruct(got.shape, jnp.bfloat16),
        in_specs=[vmem] * 5,
        out_specs=vmem,
        scratch_shapes=[
            pltpu.VMEM((2 * rows, 2 * groups * LANES), jnp.bfloat16),
            pltpu.VMEM((2 * total, 2 * LANES), jnp.bfloat16),
            pltpu.VMEM((total, 2 * LANES), jnp.float32),
            pltpu.VMEM((2, 2 * kept, (2 * groups + 1) * LANES), jnp.bfloat16),
        ],
        compiler_params=pltpu.CompilerParams(vmem_limit_bytes=40 * 2**20),
        name="spectral_products",
    )(got, *[jnp.asarray(table) for table in tables])


def filter_per_device(signal, gating, cotangent, filters, skip_weight):
    peers = lax.axis_size("ctx")
    groups = lax.axis_size("chan")
    channels, length = signal.shape
    piece = length // LANES
    taps = piece // groups
    both_axes = ("ctx", "chan")
    gated_grad = (cotangent.astype(jnp.float32) * gating.astype(jnp.float32)).astype(jnp.bfloat16)
    own = lax.dynamic_slice_in_dim(filters, lax.axis_index("chan") * (length // groups), length // groups, axis=1)
    tap_high = own.astype(jnp.bfloat16)
    tap_low = (own - tap_high.astype(jnp.float32)).astype(jnp.bfloat16)
    tiles = lambda array: array.reshape(channels, -1, LANES)
    message = jnp.concatenate([tiles(signal), tiles(gated_grad), tiles(tap_high), tiles(tap_low)], axis=1)
    message = jnp.pad(message, ((0, 0), (0, 3 * piece - message.shape[1]), (0, 0)))
    got = lax.all_to_all(message, both_axes, split_axis=0, concat_axis=0, tiled=True)
    scale = 1.0 / math.sqrt(length * peers * groups)
    result = spectral_products(got, groups, peers, scale)
    home = lax.all_to_all(result, both_axes, split_axis=0, concat_axis=0, tiled=True).astype(jnp.float32)
    conv = home[:, :piece].reshape(channels, length)
    back = home[:, piece : 2 * piece].reshape(channels, length)
    weight = skip_weight[:, None]
    outputs = conv + weight * signal.astype(jnp.float32)
    grad_gating = (cotangent.astype(jnp.float32) * outputs).astype(jnp.bfloat16)
    grad_signal = (back + weight * gated_grad.astype(jnp.float32)).astype(jnp.bfloat16)
    share = channels // groups
    corr = lax.dynamic_slice_in_dim(home[:, 2 * piece :], lax.axis_index("chan") * share, share, axis=0)
    return (grad_signal, grad_gating, corr.reshape(share, length))


def product(form, left, right):
    return jnp.einsum(
        form, left, right, precision=lax.Precision.HIGHEST, preferred_element_type=jnp.float32
    )


def phases(left_idx, right_idx, period):
    joined = left_idx[:, None] * right_idx[None, :] % period
    return joined.astype(jnp.float32) * (2.0 * math.pi / period)


def indices(total):
    return jnp.arange(total, dtype=jnp.int32)


def turn_forward(real_part, imag_part, angles):
    cosine = jnp.cos(angles)
    sine_part = jnp.sin(angles)
    return (real_part * cosine + imag_part * sine_part, imag_part * cosine - real_part * sine_part)


def turn_back(real_part, imag_part, angles):
    cosine = jnp.cos(angles)
    sine_part = jnp.sin(angles)
    return (real_part * cosine - imag_part * sine_part, imag_part * cosine + real_part * sine_part)


def first_pass(blocks, position, peer_count):
    height, length = blocks.shape
    piece_len = length // peer_count
    padded = 2 * peer_count * length
    shaped = blocks.reshape(height, peer_count, piece_len)
    angles = phases(indices(peer_count), indices(2 * peer_count), 2 * peer_count)
    real_part = product("rdm,dk->rmk", shaped, jnp.cos(angles))
    imag_part = -product("rdm,dk->rmk", shaped, jnp.sin(angles))
    offsets = position * piece_len + indices(piece_len)
    real_part, imag_part = turn_forward(
        real_part, imag_part, phases(offsets, indices(2 * peer_count), padded)
    )
    return jnp.stack([real_part, imag_part])


def second_pass(columns, peer_count):
    height, piece_len = (columns.shape[1], columns.shape[2])
    length = piece_len * peer_count
    real_part = columns[0].reshape(height, piece_len, peer_count, 2)
    imag_part = columns[1].reshape(height, piece_len, peer_count, 2)
    angles = phases(indices(peer_count), indices(peer_count), peer_count)
    cosine = jnp.cos(angles)
    sine_part = jnp.sin(angles)
    real_one = product("rmeb,ea->rbma", real_part, cosine) + product(
        "rmeb,ea->rbma", imag_part, sine_part
    )
    imag_one = product("rmeb,ea->rbma", imag_part, cosine) - product(
        "rmeb,ea->rbma", real_part, sine_part
    )
    real_one, imag_one = turn_forward(
        real_one, imag_one, phases(indices(piece_len), indices(peer_count), length)
    )
    angles = phases(indices(piece_len), indices(piece_len), piece_len)
    cosine = jnp.cos(angles)
    sine_part = jnp.sin(angles)
    real_two = product("rbma,mc->rbca", real_one, cosine) + product(
        "rbma,mc->rbca", imag_one, sine_part
    )
    imag_two = product("rbma,mc->rbca", imag_one, cosine) - product(
        "rbma,mc->rbca", real_one, sine_part
    )
    return jnp.stack([real_two.reshape(height, 2, length), imag_two.reshape(height, 2, length)])


def inverse_first(spectrum, position, peer_count):
    height, length = (spectrum.shape[1], spectrum.shape[3])
    piece_len = length // peer_count
    padded = 2 * peer_count * length
    real_part = spectrum[0].reshape(height, 2, piece_len, peer_count)
    imag_part = spectrum[1].reshape(height, 2, piece_len, peer_count)
    angles = phases(indices(piece_len), indices(piece_len), piece_len)
    cosine = jnp.cos(angles)
    sine_part = jnp.sin(angles)
    real_one = product("rbca,cm->rbma", real_part, cosine) - product(
        "rbca,cm->rbma", imag_part, sine_part
    )
    imag_one = product("rbca,cm->rbma", imag_part, cosine) + product(
        "rbca,cm->rbma", real_part, sine_part
    )
    real_one, imag_one = turn_back(
        real_one, imag_one, phases(indices(piece_len), indices(peer_count), length)
    )
    angles = phases(indices(peer_count), indices(peer_count), peer_count)
    cosine = jnp.cos(angles)
    sine_part = jnp.sin(angles)
    real_two = product("rbma,ae->rmeb", real_one, cosine) - product(
        "rbma,ae->rmeb", imag_one, sine_part
    )
    imag_two = product("rbma,ae->rmeb", imag_one, cosine) + product(
        "rbma,ae->rmeb", real_one, sine_part
    )
    offsets = (indices(peer_count)[None, :] * piece_len + indices(piece_len)[:, None]).reshape(-1)
    freq_bins = 2 * position + indices(2)
    angles = phases(offsets, freq_bins, padded).reshape(piece_len, peer_count, 2)
    real_two, imag_two = turn_back(real_two, imag_two, angles)
    return jnp.stack(
        [
            real_two.reshape(height, piece_len, 2 * peer_count),
            imag_two.reshape(height, piece_len, 2 * peer_count),
        ]
    )


def inverse_second(received, peer_count):
    height, piece_len = (received.shape[1], received.shape[2])
    length = piece_len * peer_count
    padded = 2 * peer_count * length
    angles = phases(indices(2 * peer_count), indices(peer_count), 2 * peer_count)
    signal_out = product("rmk,kd->rdm", received[0], jnp.cos(angles)) - product(
        "rmk,kd->rdm", received[1], jnp.sin(angles)
    )
    return (signal_out / padded).reshape(height, length)


def split_transforms(signal, gating, cotangent, filters, skip_weight):
    peer_count = lax.axis_size("ctx")
    position = lax.axis_index("ctx")
    channels, length = signal.shape
    count_filters = filters.shape[0]
    local_group = channels // count_filters
    gated_grad = (cotangent.astype(jnp.float32) * gating.astype(jnp.float32)).astype(jnp.bfloat16)
    signal_blocks, gated_blocks = (
        lax.all_to_all(signal, "ctx", split_axis=1, concat_axis=1, tiled=True),
        lax.all_to_all(gated_grad, "ctx", split_axis=1, concat_axis=1, tiled=True),
    )
    tap_blocks = lax.all_to_all(filters, "ctx", split_axis=1, concat_axis=1, tiled=True)
    signal_cols, gated_cols, tap_cols = (
        lax.all_to_all(
            first_pass(signal_blocks.astype(jnp.float32), position, peer_count),
            "ctx",
            split_axis=3,
            concat_axis=3,
            tiled=True,
        ),
        lax.all_to_all(
            first_pass(gated_blocks.astype(jnp.float32), position, peer_count),
            "ctx",
            split_axis=3,
            concat_axis=3,
            tiled=True,
        ),
        lax.all_to_all(
            first_pass(tap_blocks, position, peer_count),
            "ctx",
            split_axis=3,
            concat_axis=3,
            tiled=True,
        ),
    )
    signal_spec = second_pass(signal_cols, peer_count).reshape(
        2, local_group, count_filters, 2, length
    )
    gated_spec = second_pass(gated_cols, peer_count).reshape(
        2, local_group, count_filters, 2, length
    )
    tap_spec = second_pass(tap_cols, peer_count)
    tap_real, tap_imag = (tap_spec[0], tap_spec[1])
    sig_real, sig_imag = (signal_spec[0], signal_spec[1])
    gated_real, gated_imag = (gated_spec[0], gated_spec[1])
    forward_spec = jnp.stack(
        [sig_real * tap_real - sig_imag * tap_imag, sig_real * tap_imag + sig_imag * tap_real]
    ).reshape(2, channels, 2, length)
    back_spec = jnp.stack(
        [
            tap_real * gated_real + tap_imag * gated_imag,
            tap_real * gated_imag - tap_imag * gated_real,
        ]
    ).reshape(2, channels, 2, length)
    corr_spec = jnp.stack(
        [
            jnp.sum(sig_real * gated_real + sig_imag * gated_imag, axis=0),
            jnp.sum(sig_real * gated_imag - sig_imag * gated_real, axis=0),
        ]
    )
    forward_cols, back_cols, corr_cols = (
        lax.all_to_all(
            inverse_first(forward_spec, position, peer_count),
            "ctx",
            split_axis=3,
            concat_axis=3,
            tiled=True,
        ),
        lax.all_to_all(
            inverse_first(back_spec, position, peer_count),
            "ctx",
            split_axis=3,
            concat_axis=3,
            tiled=True,
        ),
        lax.all_to_all(
            inverse_first(corr_spec, position, peer_count),
            "ctx",
            split_axis=3,
            concat_axis=3,
            tiled=True,
        ),
    )
    conv_time, back_time, corr_time = (
        lax.all_to_all(
            inverse_second(forward_cols, peer_count), "ctx", split_axis=1, concat_axis=1, tiled=True
        ),
        lax.all_to_all(
            inverse_second(back_cols, peer_count), "ctx", split_axis=1, concat_axis=1, tiled=True
        ),
        lax.all_to_all(
            inverse_second(corr_cols, peer_count), "ctx", split_axis=1, concat_axis=1, tiled=True
        ),
    )
    corr_time = lax.psum_scatter(corr_time, "chan", scatter_dimension=0, tiled=True)
    weight = skip_weight[:, None]
    outputs = conv_time + weight * signal.astype(jnp.float32)
    grad_gating = (cotangent.astype(jnp.float32) * outputs).astype(jnp.bfloat16)
    grad_signal = (back_time + weight * gated_grad.astype(jnp.float32)).astype(jnp.bfloat16)
    normal_scale = 1.0 / math.sqrt(length * peer_count * local_group * lax.axis_size("chan"))
    grad_filters = corr_time * normal_scale
    return (grad_signal, grad_gating, grad_filters)


def per_device(signal, gating, cotangent, filters, skip_weight):
    peers, groups = lax.axis_size("ctx"), lax.axis_size("chan")
    channels, length = signal.shape
    one_each = channels == filters.shape[0] == peers * groups
    whole_tiles = length % (8 * LANES) == 0 and (length // LANES) % groups == 0
    if one_each and whole_tiles and 2 * (length // LANES // groups) <= length // LANES:
        return filter_per_device(signal, gating, cotangent, filters, skip_weight)
    return split_transforms(signal, gating, cotangent, filters, skip_weight)


def solution(mesh):
    in_specs = (P("chan", "ctx"), P("chan", "ctx"), P("chan", "ctx"), P(None, "ctx"), P("chan"))
    out_specs = (P("chan", "ctx"), P("chan", "ctx"), P("chan", "ctx"))
    return jax.shard_map(
        per_device, mesh=mesh, in_specs=in_specs, out_specs=out_specs, check_vma=False
    )
```

```python
import functools
import math

import jax
import jax.numpy as jnp
import numpy as np
from jax import lax
from jax.experimental import pallas as pl
from jax.experimental.pallas import tpu as pltpu
from jax.sharding import PartitionSpec as P

LANES = 128


def split_table(table):
    high = table.astype(jnp.bfloat16)
    low = (table - high.astype(np.float64)).astype(jnp.bfloat16)
    return high, low


def dft_tables(rows):
    height = 2 * rows
    padded = height * LANES
    kept = rows + 1
    pad = -kept % 16
    k1 = np.arange(kept)
    n1 = np.arange(rows)
    n2 = np.arange(LANES)
    zeros = lambda table, axis: np.pad(table, [(0, pad if a == axis else 0) for a in range(2)])
    outer = 2.0 * np.pi * (np.outer(k1, n1) % height) / height
    first = np.concatenate([zeros(np.cos(outer), 0), zeros(-np.sin(outer), 0)], axis=0)
    high, low = split_table(first)
    first = np.concatenate([high, low, high, low], axis=1)
    turn = 2.0 * np.pi * (np.outer(k1, n2) % padded) / padded
    twiddle = np.stack([zeros(np.cos(turn), 0), zeros(np.sin(turn), 0)]).astype(np.float32)
    inner = 2.0 * np.pi * (np.outer(n2, n2) % LANES) / LANES
    cosine, sine = np.cos(inner), np.sin(inner)
    second = np.stack(split_table(np.block([[cosine, -sine], [sine, cosine]])))
    weight = np.where((k1 == 0) | (k1 == rows), 1.0, 2.0) / padded
    last = np.concatenate(
        [zeros(np.cos(outer.T) * weight, 1), zeros(-np.sin(outer.T) * weight, 1)], axis=1
    )
    last = np.concatenate(split_table(last), axis=0)
    return first, twiddle, second, last


def dot(left, right):
    return jnp.dot(left, right, preferred_element_type=jnp.float32)


def split(values):
    high = values.astype(jnp.bfloat16)
    return high, (values - high.astype(jnp.float32)).astype(jnp.bfloat16)


def spectral_kernel(
    groups, peers, scale, got_ref, first_ref, twiddle_ref, second_ref, last_ref, out_ref, in_ref, part_ref, spec_ref, back_ref
):
    piece = got_ref.shape[1] // 3
    taps = piece // groups
    rows = peers * piece
    kept = twiddle_ref.shape[1]
    count = 2 * groups
    got = [got_ref[source].astype(jnp.float32) for source in range(peers * groups)]

    def gather(group, start):
        parts = [got[peer * groups + group][start : start + piece] for peer in range(peers)]
        return jnp.concatenate(parts, axis=0).astype(jnp.bfloat16)

    for sequence in range(count):
        group, start = sequence % groups, sequence // groups * piece
        values = gather(group, start)
        in_ref[0:rows, sequence * LANES : (sequence + 1) * LANES] = values
        in_ref[rows : 2 * rows, sequence * LANES : (sequence + 1) * LANES] = values
    tap_high = jnp.concatenate([part[2 * piece : 2 * piece + taps] for part in got], axis=0).astype(jnp.bfloat16)
    tap_low = jnp.concatenate([part[2 * piece + taps : 2 * piece + 2 * taps] for part in got], axis=0).astype(jnp.bfloat16)
    tap_in = jnp.concatenate([tap_high, tap_high, tap_low, tap_low], axis=0)
    cosine, sine = twiddle_ref[0], twiddle_ref[1]
    stage = dot(first_ref[:, : 2 * rows], in_ref[...])
    tap_stage = dot(first_ref[...], tap_in)
    total = (count + 1) * kept
    for sequence in range(count + 1):
        source = tap_stage if sequence == count else stage[:, sequence * LANES : (sequence + 1) * LANES]
        real, imag = source[:kept], source[kept:]
        turned = jnp.concatenate([real * cosine + imag * sine, imag * cosine - real * sine], axis=1)
        high, low = split(turned)
        part_ref[sequence * kept : (sequence + 1) * kept] = high
        part_ref[total + sequence * kept : total + (sequence + 1) * kept] = low

    def second_stage():
        both = dot(part_ref[...], second_ref[0])
        spec_ref[...] = both[:total] + both[total:] + dot(part_ref[:total], second_ref[1])

    second_stage()
    tap = spec_ref[count * kept : total]
    tap_real, tap_imag = tap[:, :LANES], tap[:, LANES:]
    corr_real = corr_imag = None

    def put(sequence, real, imag):
        high, low = split(jnp.concatenate([imag, real], axis=1))
        part_ref[sequence * kept : (sequence + 1) * kept] = high
        part_ref[total + sequence * kept : total + (sequence + 1) * kept] = low

    for group in range(groups):
        sig = spec_ref[group * kept : (group + 1) * kept]
        gat = spec_ref[(groups + group) * kept : (groups + group + 1) * kept]
        sr, si, gr, gi = sig[:, :LANES], sig[:, LANES:], gat[:, :LANES], gat[:, LANES:]
        put(group, sr * tap_real - si * tap_imag, sr * tap_imag + si * tap_real)
        put(groups + group, tap_real * gr + tap_imag * gi, tap_real * gi - tap_imag * gr)
        cr, ci = sr * gr + si * gi, sr * gi - si * gr
        corr_real, corr_imag = (cr, ci) if corr_real is None else (corr_real + cr, corr_imag + ci)
    put(count, corr_real * scale, corr_imag * scale)
    second_stage()
    for sequence in range(count + 1):
        both = spec_ref[sequence * kept : (sequence + 1) * kept]
        imag, real = both[:, :LANES], both[:, LANES:]
        turned = jnp.concatenate([real * cosine - imag * sine, imag * cosine + real * sine], axis=0)
        high, low = split(turned)
        back_ref[0, :, sequence * LANES : (sequence + 1) * LANES] = high
        back_ref[1, :, sequence * LANES : (sequence + 1) * LANES] = low
    both = dot(last_ref[...], back_ref[0])
    result = both[:rows] + both[rows:] + dot(last_ref[:rows], back_ref[1])
    for peer in range(peers):
        piece_rows = result[peer * piece : (peer + 1) * piece]
        for group in range(groups):
            cut = lambda sequence: piece_rows[:, sequence * LANES : (sequence + 1) * LANES]
            message = jnp.concatenate([cut(group), cut(groups + group), cut(count)], axis=0)
            out_ref[peer * groups + group] = message.astype(jnp.bfloat16)


def spectral_products(got, groups, peers, scale):
    rows = peers * (got.shape[1] // 3)
    tables = dft_tables(rows)
    kept = tables[1].shape[1]
    total = (2 * groups + 1) * kept
    vmem = pl.BlockSpec(memory_space=pltpu.VMEM)
    return pl.pallas_call(
        functools.partial(spectral_kernel, groups, peers, scale),
        out_shape=jax.ShapeDtypeStruct(got.shape, jnp.bfloat16),
        in_specs=[vmem] * 5,
        out_specs=vmem,
        scratch_shapes=[
            pltpu.VMEM((2 * rows, 2 * groups * LANES), jnp.bfloat16),
            pltpu.VMEM((2 * total, 2 * LANES), jnp.bfloat16),
            pltpu.VMEM((total, 2 * LANES), jnp.float32),
            pltpu.VMEM((2, 2 * kept, (2 * groups + 1) * LANES), jnp.bfloat16),
        ],
        compiler_params=pltpu.CompilerParams(vmem_limit_bytes=24 * 2**20),
        name="spectral_products",
    )(got, *[jnp.asarray(table) for table in tables])


def tile_rows(values):
    return values.reshape(values.shape[0], values.shape[1] // LANES, LANES)


def pack_kernel(
    groups, signal_hbm, gating_hbm, cotangent_hbm, filters_hbm, message_ref, signal_ref, gating_ref, cotangent_ref, taps_ref, sems
):
    channels, length = signal_ref.shape
    share = length // groups
    start = pl.multiple_of(lax.axis_index("chan") * share, share)
    copies = [
        pltpu.make_async_copy(source, target, sems.at[at])
        for at, (source, target) in enumerate(
            [
                (cotangent_hbm, cotangent_ref),
                (gating_hbm, gating_ref),
                (signal_hbm, signal_ref),
                (filters_hbm.at[:, pl.ds(start, share)], taps_ref),
            ]
        )
    ]
    for copy in copies:
        copy.start()
    for copy in copies:
        copy.wait()
    signal = signal_ref[...].astype(jnp.float32)
    gated = cotangent_ref[...].astype(jnp.float32) * gating_ref[...].astype(jnp.float32)
    high, low = split(taps_ref[...])
    spare = message_ref.shape[1] * LANES - 2 * length - 2 * share
    parts = [signal, gated, high.astype(jnp.float32), low.astype(jnp.float32)]
    parts.append(jnp.zeros((channels, spare), jnp.float32))
    message_ref[...] = tile_rows(jnp.concatenate(parts, axis=1)).astype(jnp.bfloat16)


def pack(signal, gating, cotangent, filters, groups):
    channels, length = signal.shape
    vmem = pl.BlockSpec(memory_space=pltpu.VMEM)
    return pl.pallas_call(
        functools.partial(pack_kernel, groups),
        out_shape=jax.ShapeDtypeStruct((channels, 3 * (length // LANES), LANES), jnp.bfloat16),
        in_specs=[pl.BlockSpec(memory_space=pltpu.HBM)] * 4,
        out_specs=vmem,
        scratch_shapes=[pltpu.VMEM(signal.shape, jnp.bfloat16)] * 3
        + [pltpu.VMEM((filters.shape[0], length // groups), jnp.float32), pltpu.SemaphoreType.DMA((4,))],
        compiler_params=pltpu.CompilerParams(vmem_limit_bytes=16 * 2**20),
        name="pack",
    )(*[pltpu.with_memory_space_constraint(array, pltpu.HBM) for array in (signal, gating, cotangent, filters)])


def finish_kernel(groups, home_ref, signal_ref, gating_ref, cotangent_ref, weight_ref, signal_out, gating_out, filters_out):
    channels, length = signal_ref.shape
    piece = length // LANES
    share = channels // groups
    home = home_ref[...].astype(jnp.float32).reshape(channels, 3 * length)
    cotangent = cotangent_ref[...].astype(jnp.float32)
    gated = (cotangent * gating_ref[...].astype(jnp.float32)).astype(jnp.bfloat16).astype(jnp.float32)
    weight = weight_ref[...]
    outputs = home[:, :length] + weight * signal_ref[...].astype(jnp.float32)
    gating_out[...] = (cotangent * outputs).astype(jnp.bfloat16)
    signal_out[...] = (home[:, length : 2 * length] + weight * gated).astype(jnp.bfloat16)
    first = pl.multiple_of(lax.axis_index("chan") * share, share)
    corr = home_ref[pl.ds(first, share), 2 * piece :, :].astype(jnp.float32)
    filters_out[...] = corr.reshape(share, length)


def finish(home, signal, gating, cotangent, skip_weight, groups):
    channels, length = signal.shape
    vmem = pl.BlockSpec(memory_space=pltpu.VMEM)
    return pl.pallas_call(
        functools.partial(finish_kernel, groups),
        out_shape=(
            jax.ShapeDtypeStruct(signal.shape, jnp.bfloat16),
            jax.ShapeDtypeStruct(signal.shape, jnp.bfloat16),
            jax.ShapeDtypeStruct((channels // groups, length), jnp.float32),
        ),
        in_specs=[vmem] * 5,
        out_specs=(vmem,) * 3,
        compiler_params=pltpu.CompilerParams(vmem_limit_bytes=16 * 2**20),
        name="finish",
    )(home, signal, gating, cotangent, skip_weight[:, None])


def filter_per_device(signal, gating, cotangent, filters, skip_weight):
    peers = lax.axis_size("ctx")
    groups = lax.axis_size("chan")
    both_axes = ("ctx", "chan")
    message = pack(signal, gating, cotangent, filters, groups)
    got = lax.all_to_all(message, both_axes, split_axis=0, concat_axis=0, tiled=True)
    scale = 1.0 / math.sqrt(signal.shape[1] * peers * groups)
    result = spectral_products(got, groups, peers, scale)
    home = lax.all_to_all(result, both_axes, split_axis=0, concat_axis=0, tiled=True)
    return finish(home, signal, gating, cotangent, skip_weight, groups)


def product(form, left, right):
    return jnp.einsum(
        form, left, right, precision=lax.Precision.HIGHEST, preferred_element_type=jnp.float32
    )


def phases(left_idx, right_idx, period):
    joined = left_idx[:, None] * right_idx[None, :] % period
    return joined.astype(jnp.float32) * (2.0 * math.pi / period)


def indices(total):
    return jnp.arange(total, dtype=jnp.int32)


def turn_forward(real_part, imag_part, angles):
    cosine = jnp.cos(angles)
    sine_part = jnp.sin(angles)
    return (real_part * cosine + imag_part * sine_part, imag_part * cosine - real_part * sine_part)


def turn_back(real_part, imag_part, angles):
    cosine = jnp.cos(angles)
    sine_part = jnp.sin(angles)
    return (real_part * cosine - imag_part * sine_part, imag_part * cosine + real_part * sine_part)


def first_pass(blocks, position, peer_count):
    height, length = blocks.shape
    piece_len = length // peer_count
    padded = 2 * peer_count * length
    shaped = blocks.reshape(height, peer_count, piece_len)
    angles = phases(indices(peer_count), indices(2 * peer_count), 2 * peer_count)
    real_part = product("rdm,dk->rmk", shaped, jnp.cos(angles))
    imag_part = -product("rdm,dk->rmk", shaped, jnp.sin(angles))
    offsets = position * piece_len + indices(piece_len)
    real_part, imag_part = turn_forward(
        real_part, imag_part, phases(offsets, indices(2 * peer_count), padded)
    )
    return jnp.stack([real_part, imag_part])


def second_pass(columns, peer_count):
    height, piece_len = (columns.shape[1], columns.shape[2])
    length = piece_len * peer_count
    real_part = columns[0].reshape(height, piece_len, peer_count, 2)
    imag_part = columns[1].reshape(height, piece_len, peer_count, 2)
    angles = phases(indices(peer_count), indices(peer_count), peer_count)
    cosine = jnp.cos(angles)
    sine_part = jnp.sin(angles)
    real_one = product("rmeb,ea->rbma", real_part, cosine) + product(
        "rmeb,ea->rbma", imag_part, sine_part
    )
    imag_one = product("rmeb,ea->rbma", imag_part, cosine) - product(
        "rmeb,ea->rbma", real_part, sine_part
    )
    real_one, imag_one = turn_forward(
        real_one, imag_one, phases(indices(piece_len), indices(peer_count), length)
    )
    angles = phases(indices(piece_len), indices(piece_len), piece_len)
    cosine = jnp.cos(angles)
    sine_part = jnp.sin(angles)
    real_two = product("rbma,mc->rbca", real_one, cosine) + product(
        "rbma,mc->rbca", imag_one, sine_part
    )
    imag_two = product("rbma,mc->rbca", imag_one, cosine) - product(
        "rbma,mc->rbca", real_one, sine_part
    )
    return jnp.stack([real_two.reshape(height, 2, length), imag_two.reshape(height, 2, length)])


def inverse_first(spectrum, position, peer_count):
    height, length = (spectrum.shape[1], spectrum.shape[3])
    piece_len = length // peer_count
    padded = 2 * peer_count * length
    real_part = spectrum[0].reshape(height, 2, piece_len, peer_count)
    imag_part = spectrum[1].reshape(height, 2, piece_len, peer_count)
    angles = phases(indices(piece_len), indices(piece_len), piece_len)
    cosine = jnp.cos(angles)
    sine_part = jnp.sin(angles)
    real_one = product("rbca,cm->rbma", real_part, cosine) - product(
        "rbca,cm->rbma", imag_part, sine_part
    )
    imag_one = product("rbca,cm->rbma", imag_part, cosine) + product(
        "rbca,cm->rbma", real_part, sine_part
    )
    real_one, imag_one = turn_back(
        real_one, imag_one, phases(indices(piece_len), indices(peer_count), length)
    )
    angles = phases(indices(peer_count), indices(peer_count), peer_count)
    cosine = jnp.cos(angles)
    sine_part = jnp.sin(angles)
    real_two = product("rbma,ae->rmeb", real_one, cosine) - product(
        "rbma,ae->rmeb", imag_one, sine_part
    )
    imag_two = product("rbma,ae->rmeb", imag_one, cosine) + product(
        "rbma,ae->rmeb", real_one, sine_part
    )
    offsets = (indices(peer_count)[None, :] * piece_len + indices(piece_len)[:, None]).reshape(-1)
    freq_bins = 2 * position + indices(2)
    angles = phases(offsets, freq_bins, padded).reshape(piece_len, peer_count, 2)
    real_two, imag_two = turn_back(real_two, imag_two, angles)
    return jnp.stack(
        [
            real_two.reshape(height, piece_len, 2 * peer_count),
            imag_two.reshape(height, piece_len, 2 * peer_count),
        ]
    )


def inverse_second(received, peer_count):
    height, piece_len = (received.shape[1], received.shape[2])
    length = piece_len * peer_count
    padded = 2 * peer_count * length
    angles = phases(indices(2 * peer_count), indices(peer_count), 2 * peer_count)
    signal_out = product("rmk,kd->rdm", received[0], jnp.cos(angles)) - product(
        "rmk,kd->rdm", received[1], jnp.sin(angles)
    )
    return (signal_out / padded).reshape(height, length)


def split_transforms(signal, gating, cotangent, filters, skip_weight):
    peer_count = lax.axis_size("ctx")
    position = lax.axis_index("ctx")
    channels, length = signal.shape
    count_filters = filters.shape[0]
    local_group = channels // count_filters
    gated_grad = (cotangent.astype(jnp.float32) * gating.astype(jnp.float32)).astype(jnp.bfloat16)
    signal_blocks, gated_blocks = (
        lax.all_to_all(signal, "ctx", split_axis=1, concat_axis=1, tiled=True),
        lax.all_to_all(gated_grad, "ctx", split_axis=1, concat_axis=1, tiled=True),
    )
    tap_blocks = lax.all_to_all(filters, "ctx", split_axis=1, concat_axis=1, tiled=True)
    signal_cols, gated_cols, tap_cols = (
        lax.all_to_all(
            first_pass(signal_blocks.astype(jnp.float32), position, peer_count),
            "ctx",
            split_axis=3,
            concat_axis=3,
            tiled=True,
        ),
        lax.all_to_all(
            first_pass(gated_blocks.astype(jnp.float32), position, peer_count),
            "ctx",
            split_axis=3,
            concat_axis=3,
            tiled=True,
        ),
        lax.all_to_all(
            first_pass(tap_blocks, position, peer_count),
            "ctx",
            split_axis=3,
            concat_axis=3,
            tiled=True,
        ),
    )
    signal_spec = second_pass(signal_cols, peer_count).reshape(
        2, local_group, count_filters, 2, length
    )
    gated_spec = second_pass(gated_cols, peer_count).reshape(
        2, local_group, count_filters, 2, length
    )
    tap_spec = second_pass(tap_cols, peer_count)
    tap_real, tap_imag = (tap_spec[0], tap_spec[1])
    sig_real, sig_imag = (signal_spec[0], signal_spec[1])
    gated_real, gated_imag = (gated_spec[0], gated_spec[1])
    forward_spec = jnp.stack(
        [sig_real * tap_real - sig_imag * tap_imag, sig_real * tap_imag + sig_imag * tap_real]
    ).reshape(2, channels, 2, length)
    back_spec = jnp.stack(
        [
            tap_real * gated_real + tap_imag * gated_imag,
            tap_real * gated_imag - tap_imag * gated_real,
        ]
    ).reshape(2, channels, 2, length)
    corr_spec = jnp.stack(
        [
            jnp.sum(sig_real * gated_real + sig_imag * gated_imag, axis=0),
            jnp.sum(sig_real * gated_imag - sig_imag * gated_real, axis=0),
        ]
    )
    forward_cols, back_cols, corr_cols = (
        lax.all_to_all(
            inverse_first(forward_spec, position, peer_count),
            "ctx",
            split_axis=3,
            concat_axis=3,
            tiled=True,
        ),
        lax.all_to_all(
            inverse_first(back_spec, position, peer_count),
            "ctx",
            split_axis=3,
            concat_axis=3,
            tiled=True,
        ),
        lax.all_to_all(
            inverse_first(corr_spec, position, peer_count),
            "ctx",
            split_axis=3,
            concat_axis=3,
            tiled=True,
        ),
    )
    conv_time, back_time, corr_time = (
        lax.all_to_all(
            inverse_second(forward_cols, peer_count), "ctx", split_axis=1, concat_axis=1, tiled=True
        ),
        lax.all_to_all(
            inverse_second(back_cols, peer_count), "ctx", split_axis=1, concat_axis=1, tiled=True
        ),
        lax.all_to_all(
            inverse_second(corr_cols, peer_count), "ctx", split_axis=1, concat_axis=1, tiled=True
        ),
    )
    corr_time = lax.psum_scatter(corr_time, "chan", scatter_dimension=0, tiled=True)
    weight = skip_weight[:, None]
    outputs = conv_time + weight * signal.astype(jnp.float32)
    grad_gating = (cotangent.astype(jnp.float32) * outputs).astype(jnp.bfloat16)
    grad_signal = (back_time + weight * gated_grad.astype(jnp.float32)).astype(jnp.bfloat16)
    normal_scale = 1.0 / math.sqrt(length * peer_count * local_group * lax.axis_size("chan"))
    grad_filters = corr_time * normal_scale
    return (grad_signal, grad_gating, grad_filters)


def per_device(signal, gating, cotangent, filters, skip_weight):
    peers, groups = lax.axis_size("ctx"), lax.axis_size("chan")
    channels, length = signal.shape
    one_each = channels == filters.shape[0] == peers * groups
    whole_tiles = length % (8 * LANES) == 0 and (length // LANES) % groups == 0
    if one_each and whole_tiles and 2 * (length // LANES // groups) <= length // LANES:
        return filter_per_device(signal, gating, cotangent, filters, skip_weight)
    return split_transforms(signal, gating, cotangent, filters, skip_weight)


def solution(mesh):
    in_specs = (P("chan", "ctx"), P("chan", "ctx"), P("chan", "ctx"), P(None, "ctx"), P("chan"))
    out_specs = (P("chan", "ctx"), P("chan", "ctx"), P("chan", "ctx"))
    return jax.shard_map(
        per_device, mesh=mesh, in_specs=in_specs, out_specs=out_specs, check_vma=False
    )
```

```python
import functools
import math

import jax
import jax.numpy as jnp
import numpy as np
from jax import lax
from jax.experimental import pallas as pl
from jax.experimental.pallas import tpu as pltpu
from jax.sharding import PartitionSpec as P

LANES = 128


def split_table(table):
    high = table.astype(jnp.bfloat16)
    low = (table - high.astype(np.float64)).astype(jnp.bfloat16)
    return high, low


def dft_tables(rows):
    height = 2 * rows
    padded = height * LANES
    k1 = np.arange(rows)
    n1 = np.arange(rows)
    n2 = np.arange(LANES)
    outer = np.pi * (np.outer(2 * k1 + 1, n1) % (2 * height)) / height
    high, low = split_table(np.concatenate([np.cos(outer), -np.sin(outer)], axis=0))
    first = np.concatenate([high, low, high, low], axis=1)
    turn = np.pi * (np.outer(2 * k1 + 1, n2) % (2 * padded)) / padded
    twiddle = np.stack([np.cos(turn), np.sin(turn)]).astype(np.float32)
    inner = 2.0 * np.pi * (np.outer(n2, n2) % LANES) / LANES
    cosine, sine = np.cos(inner), np.sin(inner)
    second = np.stack(split_table(np.block([[cosine, -sine], [sine, cosine]])))
    high, low = split_table(np.concatenate([np.cos(outer.T), -np.sin(outer.T)], axis=1) * (2.0 / padded))
    last = np.block([[high, high], [low, np.zeros_like(low)]])
    return first, twiddle, second, last


def dot(left, right):
    return jnp.dot(left, right, preferred_element_type=jnp.float32)


def split(values):
    high = values.astype(jnp.bfloat16)
    return high, (values - high.astype(jnp.float32)).astype(jnp.bfloat16)


def spectral_kernel(
    groups, peers, scale, got_ref, first_ref, twiddle_ref, second_ref, last_ref, out_ref, in_ref, part_ref, spec_ref, back_ref
):
    piece = got_ref.shape[1] // 3
    taps = piece // groups
    rows = peers * piece
    kept = twiddle_ref.shape[1]
    count = 2 * groups
    got = [got_ref[source].astype(jnp.float32) for source in range(peers * groups)]

    def gather(group, start):
        parts = [got[peer * groups + group][start : start + piece] for peer in range(peers)]
        return jnp.concatenate(parts, axis=0).astype(jnp.bfloat16)

    for sequence in range(count):
        group, start = sequence % groups, sequence // groups * piece
        values = gather(group, start)
        in_ref[0:rows, sequence * LANES : (sequence + 1) * LANES] = values
        in_ref[rows : 2 * rows, sequence * LANES : (sequence + 1) * LANES] = values
    tap_high = jnp.concatenate([part[2 * piece : 2 * piece + taps] for part in got], axis=0).astype(jnp.bfloat16)
    tap_low = jnp.concatenate([part[2 * piece + taps : 2 * piece + 2 * taps] for part in got], axis=0).astype(jnp.bfloat16)
    tap_in = jnp.concatenate([tap_high, tap_high, tap_low, tap_low], axis=0)
    cosine, sine = twiddle_ref[0], twiddle_ref[1]
    stage = dot(first_ref[:, : 2 * rows], in_ref[...])
    tap_stage = dot(first_ref[...], tap_in)
    total = (count + 1) * kept
    for sequence in range(count + 1):
        source = tap_stage if sequence == count else stage[:, sequence * LANES : (sequence + 1) * LANES]
        real, imag = source[:kept], source[kept:]
        turned = jnp.concatenate([real * cosine + imag * sine, imag * cosine - real * sine], axis=1)
        high, low = split(turned)
        part_ref[sequence * kept : (sequence + 1) * kept] = high
        part_ref[total + sequence * kept : total + (sequence + 1) * kept] = low

    def second_stage():
        both = dot(part_ref[...], second_ref[0])
        spec_ref[...] = both[:total] + both[total:] + dot(part_ref[:total], second_ref[1])

    second_stage()
    tap = spec_ref[count * kept : total]
    tap_real, tap_imag = tap[:, :LANES], tap[:, LANES:]
    corr_real = corr_imag = None

    def put(sequence, real, imag):
        high, low = split(jnp.concatenate([imag, real], axis=1))
        part_ref[sequence * kept : (sequence + 1) * kept] = high
        part_ref[total + sequence * kept : total + (sequence + 1) * kept] = low

    for group in range(groups):
        sig = spec_ref[group * kept : (group + 1) * kept]
        gat = spec_ref[(groups + group) * kept : (groups + group + 1) * kept]
        sr, si, gr, gi = sig[:, :LANES], sig[:, LANES:], gat[:, :LANES], gat[:, LANES:]
        put(group, sr * tap_real - si * tap_imag, sr * tap_imag + si * tap_real)
        put(groups + group, tap_real * gr + tap_imag * gi, tap_real * gi - tap_imag * gr)
        cr, ci = sr * gr + si * gi, sr * gi - si * gr
        corr_real, corr_imag = (cr, ci) if corr_real is None else (corr_real + cr, corr_imag + ci)
    put(count, corr_real * scale, corr_imag * scale)
    second_stage()
    for sequence in range(count + 1):
        both = spec_ref[sequence * kept : (sequence + 1) * kept]
        imag, real = both[:, :LANES], both[:, LANES:]
        turned = jnp.concatenate([real * cosine - imag * sine, imag * cosine + real * sine], axis=0)
        high, low = split(turned)
        back_ref[: 2 * kept, sequence * LANES : (sequence + 1) * LANES] = high
        back_ref[2 * kept :, sequence * LANES : (sequence + 1) * LANES] = low
    both = dot(last_ref[...], back_ref[...])
    result = both[:rows] + both[rows:]
    for peer in range(peers):
        piece_rows = result[peer * piece : (peer + 1) * piece]
        for group in range(groups):
            cut = lambda sequence: piece_rows[:, sequence * LANES : (sequence + 1) * LANES]
            message = jnp.concatenate([cut(group), cut(groups + group), cut(count)], axis=0)
            out_ref[peer * groups + group] = message.astype(jnp.bfloat16)


def spectral_products(got, groups, peers, scale):
    rows = peers * (got.shape[1] // 3)
    tables = dft_tables(rows)
    kept = tables[1].shape[1]
    total = (2 * groups + 1) * kept
    vmem = pl.BlockSpec(memory_space=pltpu.VMEM)
    return pl.pallas_call(
        functools.partial(spectral_kernel, groups, peers, scale),
        out_shape=jax.ShapeDtypeStruct(got.shape, jnp.bfloat16),
        in_specs=[vmem] * 5,
        out_specs=vmem,
        scratch_shapes=[
            pltpu.VMEM((2 * rows, 2 * groups * LANES), jnp.bfloat16),
            pltpu.VMEM((2 * total, 2 * LANES), jnp.bfloat16),
            pltpu.VMEM((total, 2 * LANES), jnp.float32),
            pltpu.VMEM((4 * kept, (2 * groups + 1) * LANES), jnp.bfloat16),
        ],
        compiler_params=pltpu.CompilerParams(vmem_limit_bytes=24 * 2**20),
        name="spectral_products",
    )(got, *[jnp.asarray(table) for table in tables])


def tile_rows(values):
    return values.reshape(values.shape[0], values.shape[1] // LANES, LANES)


def pack_kernel(
    groups,
    signal_hbm,
    gating_hbm,
    cotangent_hbm,
    filters_hbm,
    weight_hbm,
    message_ref,
    column_ref,
    signal_ref,
    gating_ref,
    cotangent_ref,
    taps_ref,
    weight_ref,
    sems,
):
    channels, length = signal_ref.shape
    share = length // groups
    start = pl.multiple_of(lax.axis_index("chan") * share, share)
    copies = [
        pltpu.make_async_copy(source, target, sems.at[at])
        for at, (source, target) in enumerate(
            [
                (cotangent_hbm, cotangent_ref),
                (gating_hbm, gating_ref),
                (signal_hbm, signal_ref),
                (filters_hbm.at[:, pl.ds(start, share)], taps_ref),
                (weight_hbm, weight_ref),
            ]
        )
    ]
    for copy in copies:
        copy.start()
    for copy in copies:
        copy.wait()
    signal = signal_ref[...].astype(jnp.float32)
    gated = cotangent_ref[...].astype(jnp.float32) * gating_ref[...].astype(jnp.float32)
    high, low = split(taps_ref[...])
    spare = message_ref.shape[1] * LANES - 2 * length - 2 * share
    parts = [signal, gated, high.astype(jnp.float32), low.astype(jnp.float32)]
    parts.append(jnp.zeros((channels, spare), jnp.float32))
    message_ref[...] = tile_rows(jnp.concatenate(parts, axis=1)).astype(jnp.bfloat16)
    square = (channels, channels)
    diagonal = lax.broadcasted_iota(jnp.int32, square, 0) == lax.broadcasted_iota(jnp.int32, square, 1)
    weight = jnp.sum(jnp.where(diagonal, jnp.broadcast_to(weight_ref[...], square), 0.0), axis=1, keepdims=True)
    column_ref[...] = jnp.broadcast_to(weight, column_ref.shape)


def pack(signal, gating, cotangent, filters, skip_weight, groups):
    channels, length = signal.shape
    vmem = pl.BlockSpec(memory_space=pltpu.VMEM)
    operands = (signal, gating, cotangent, filters, skip_weight[None, :])
    return pl.pallas_call(
        functools.partial(pack_kernel, groups),
        out_shape=(
            jax.ShapeDtypeStruct((channels, 3 * (length // LANES), LANES), jnp.bfloat16),
            jax.ShapeDtypeStruct((channels, LANES), jnp.float32),
        ),
        in_specs=[pl.BlockSpec(memory_space=pltpu.HBM)] * 5,
        out_specs=(vmem, vmem),
        scratch_shapes=[pltpu.VMEM(signal.shape, jnp.bfloat16)] * 3
        + [
            pltpu.VMEM((filters.shape[0], length // groups), jnp.float32),
            pltpu.VMEM((1, channels), jnp.float32),
            pltpu.SemaphoreType.DMA((5,)),
        ],
        compiler_params=pltpu.CompilerParams(vmem_limit_bytes=16 * 2**20),
        name="pack",
    )(*[pltpu.with_memory_space_constraint(operand, pltpu.HBM) for operand in operands])


def finish_kernel(groups, home_ref, signal_ref, gating_ref, cotangent_ref, column_ref, signal_out, gating_out, filters_out):
    channels, length = signal_ref.shape
    piece = length // LANES
    share = channels // groups
    home = home_ref[...].astype(jnp.float32).reshape(channels, 3 * length)
    cotangent = cotangent_ref[...].astype(jnp.float32)
    gated = (cotangent * gating_ref[...].astype(jnp.float32)).astype(jnp.bfloat16).astype(jnp.float32)
    weight = column_ref[:, :1]
    outputs = home[:, :length] + weight * signal_ref[...].astype(jnp.float32)
    gating_out[...] = (cotangent * outputs).astype(jnp.bfloat16)
    signal_out[...] = (home[:, length : 2 * length] + weight * gated).astype(jnp.bfloat16)
    first = pl.multiple_of(lax.axis_index("chan") * share, share)
    corr = home_ref[pl.ds(first, share), 2 * piece :, :].astype(jnp.float32)
    filters_out[...] = corr.reshape(share, length)


def finish(home, signal, gating, cotangent, column, groups):
    channels, length = signal.shape
    vmem = pl.BlockSpec(memory_space=pltpu.VMEM)
    return pl.pallas_call(
        functools.partial(finish_kernel, groups),
        out_shape=(
            jax.ShapeDtypeStruct(signal.shape, jnp.bfloat16),
            jax.ShapeDtypeStruct(signal.shape, jnp.bfloat16),
            jax.ShapeDtypeStruct((channels // groups, length), jnp.float32),
        ),
        in_specs=[vmem] * 5,
        out_specs=(vmem,) * 3,
        compiler_params=pltpu.CompilerParams(vmem_limit_bytes=16 * 2**20),
        name="finish",
    )(home, signal, gating, cotangent, column)


def filter_per_device(signal, gating, cotangent, filters, skip_weight):
    peers = lax.axis_size("ctx")
    groups = lax.axis_size("chan")
    both_axes = ("ctx", "chan")
    message, column = pack(signal, gating, cotangent, filters, skip_weight, groups)
    got = lax.all_to_all(message, both_axes, split_axis=0, concat_axis=0, tiled=True)
    scale = 1.0 / math.sqrt(signal.shape[1] * peers * groups)
    result = spectral_products(got, groups, peers, scale)
    home = lax.all_to_all(result, both_axes, split_axis=0, concat_axis=0, tiled=True)
    return finish(home, signal, gating, cotangent, column, groups)


def product(form, left, right):
    return jnp.einsum(
        form, left, right, precision=lax.Precision.HIGHEST, preferred_element_type=jnp.float32
    )


def phases(left_idx, right_idx, period):
    joined = left_idx[:, None] * right_idx[None, :] % period
    return joined.astype(jnp.float32) * (2.0 * math.pi / period)


def indices(total):
    return jnp.arange(total, dtype=jnp.int32)


def turn_forward(real_part, imag_part, angles):
    cosine = jnp.cos(angles)
    sine_part = jnp.sin(angles)
    return (real_part * cosine + imag_part * sine_part, imag_part * cosine - real_part * sine_part)


def turn_back(real_part, imag_part, angles):
    cosine = jnp.cos(angles)
    sine_part = jnp.sin(angles)
    return (real_part * cosine - imag_part * sine_part, imag_part * cosine + real_part * sine_part)


def first_pass(blocks, position, peer_count):
    height, length = blocks.shape
    piece_len = length // peer_count
    padded = 2 * peer_count * length
    shaped = blocks.reshape(height, peer_count, piece_len)
    angles = phases(indices(peer_count), indices(2 * peer_count), 2 * peer_count)
    real_part = product("rdm,dk->rmk", shaped, jnp.cos(angles))
    imag_part = -product("rdm,dk->rmk", shaped, jnp.sin(angles))
    offsets = position * piece_len + indices(piece_len)
    real_part, imag_part = turn_forward(
        real_part, imag_part, phases(offsets, indices(2 * peer_count), padded)
    )
    return jnp.stack([real_part, imag_part])


def second_pass(columns, peer_count):
    height, piece_len = (columns.shape[1], columns.shape[2])
    length = piece_len * peer_count
    real_part = columns[0].reshape(height, piece_len, peer_count, 2)
    imag_part = columns[1].reshape(height, piece_len, peer_count, 2)
    angles = phases(indices(peer_count), indices(peer_count), peer_count)
    cosine = jnp.cos(angles)
    sine_part = jnp.sin(angles)
    real_one = product("rmeb,ea->rbma", real_part, cosine) + product(
        "rmeb,ea->rbma", imag_part, sine_part
    )
    imag_one = product("rmeb,ea->rbma", imag_part, cosine) - product(
        "rmeb,ea->rbma", real_part, sine_part
    )
    real_one, imag_one = turn_forward(
        real_one, imag_one, phases(indices(piece_len), indices(peer_count), length)
    )
    angles = phases(indices(piece_len), indices(piece_len), piece_len)
    cosine = jnp.cos(angles)
    sine_part = jnp.sin(angles)
    real_two = product("rbma,mc->rbca", real_one, cosine) + product(
        "rbma,mc->rbca", imag_one, sine_part
    )
    imag_two = product("rbma,mc->rbca", imag_one, cosine) - product(
        "rbma,mc->rbca", real_one, sine_part
    )
    return jnp.stack([real_two.reshape(height, 2, length), imag_two.reshape(height, 2, length)])


def inverse_first(spectrum, position, peer_count):
    height, length = (spectrum.shape[1], spectrum.shape[3])
    piece_len = length // peer_count
    padded = 2 * peer_count * length
    real_part = spectrum[0].reshape(height, 2, piece_len, peer_count)
    imag_part = spectrum[1].reshape(height, 2, piece_len, peer_count)
    angles = phases(indices(piece_len), indices(piece_len), piece_len)
    cosine = jnp.cos(angles)
    sine_part = jnp.sin(angles)
    real_one = product("rbca,cm->rbma", real_part, cosine) - product(
        "rbca,cm->rbma", imag_part, sine_part
    )
    imag_one = product("rbca,cm->rbma", imag_part, cosine) + product(
        "rbca,cm->rbma", real_part, sine_part
    )
    real_one, imag_one = turn_back(
        real_one, imag_one, phases(indices(piece_len), indices(peer_count), length)
    )
    angles = phases(indices(peer_count), indices(peer_count), peer_count)
    cosine = jnp.cos(angles)
    sine_part = jnp.sin(angles)
    real_two = product("rbma,ae->rmeb", real_one, cosine) - product(
        "rbma,ae->rmeb", imag_one, sine_part
    )
    imag_two = product("rbma,ae->rmeb", imag_one, cosine) + product(
        "rbma,ae->rmeb", real_one, sine_part
    )
    offsets = (indices(peer_count)[None, :] * piece_len + indices(piece_len)[:, None]).reshape(-1)
    freq_bins = 2 * position + indices(2)
    angles = phases(offsets, freq_bins, padded).reshape(piece_len, peer_count, 2)
    real_two, imag_two = turn_back(real_two, imag_two, angles)
    return jnp.stack(
        [
            real_two.reshape(height, piece_len, 2 * peer_count),
            imag_two.reshape(height, piece_len, 2 * peer_count),
        ]
    )


def inverse_second(received, peer_count):
    height, piece_len = (received.shape[1], received.shape[2])
    length = piece_len * peer_count
    padded = 2 * peer_count * length
    angles = phases(indices(2 * peer_count), indices(peer_count), 2 * peer_count)
    signal_out = product("rmk,kd->rdm", received[0], jnp.cos(angles)) - product(
        "rmk,kd->rdm", received[1], jnp.sin(angles)
    )
    return (signal_out / padded).reshape(height, length)


def split_transforms(signal, gating, cotangent, filters, skip_weight):
    peer_count = lax.axis_size("ctx")
    position = lax.axis_index("ctx")
    channels, length = signal.shape
    count_filters = filters.shape[0]
    local_group = channels // count_filters
    gated_grad = (cotangent.astype(jnp.float32) * gating.astype(jnp.float32)).astype(jnp.bfloat16)
    signal_blocks, gated_blocks = (
        lax.all_to_all(signal, "ctx", split_axis=1, concat_axis=1, tiled=True),
        lax.all_to_all(gated_grad, "ctx", split_axis=1, concat_axis=1, tiled=True),
    )
    tap_blocks = lax.all_to_all(filters, "ctx", split_axis=1, concat_axis=1, tiled=True)
    signal_cols, gated_cols, tap_cols = (
        lax.all_to_all(
            first_pass(signal_blocks.astype(jnp.float32), position, peer_count),
            "ctx",
            split_axis=3,
            concat_axis=3,
            tiled=True,
        ),
        lax.all_to_all(
            first_pass(gated_blocks.astype(jnp.float32), position, peer_count),
            "ctx",
            split_axis=3,
            concat_axis=3,
            tiled=True,
        ),
        lax.all_to_all(
            first_pass(tap_blocks, position, peer_count),
            "ctx",
            split_axis=3,
            concat_axis=3,
            tiled=True,
        ),
    )
    signal_spec = second_pass(signal_cols, peer_count).reshape(
        2, local_group, count_filters, 2, length
    )
    gated_spec = second_pass(gated_cols, peer_count).reshape(
        2, local_group, count_filters, 2, length
    )
    tap_spec = second_pass(tap_cols, peer_count)
    tap_real, tap_imag = (tap_spec[0], tap_spec[1])
    sig_real, sig_imag = (signal_spec[0], signal_spec[1])
    gated_real, gated_imag = (gated_spec[0], gated_spec[1])
    forward_spec = jnp.stack(
        [sig_real * tap_real - sig_imag * tap_imag, sig_real * tap_imag + sig_imag * tap_real]
    ).reshape(2, channels, 2, length)
    back_spec = jnp.stack(
        [
            tap_real * gated_real + tap_imag * gated_imag,
            tap_real * gated_imag - tap_imag * gated_real,
        ]
    ).reshape(2, channels, 2, length)
    corr_spec = jnp.stack(
        [
            jnp.sum(sig_real * gated_real + sig_imag * gated_imag, axis=0),
            jnp.sum(sig_real * gated_imag - sig_imag * gated_real, axis=0),
        ]
    )
    forward_cols, back_cols, corr_cols = (
        lax.all_to_all(
            inverse_first(forward_spec, position, peer_count),
            "ctx",
            split_axis=3,
            concat_axis=3,
            tiled=True,
        ),
        lax.all_to_all(
            inverse_first(back_spec, position, peer_count),
            "ctx",
            split_axis=3,
            concat_axis=3,
            tiled=True,
        ),
        lax.all_to_all(
            inverse_first(corr_spec, position, peer_count),
            "ctx",
            split_axis=3,
            concat_axis=3,
            tiled=True,
        ),
    )
    conv_time, back_time, corr_time = (
        lax.all_to_all(
            inverse_second(forward_cols, peer_count), "ctx", split_axis=1, concat_axis=1, tiled=True
        ),
        lax.all_to_all(
            inverse_second(back_cols, peer_count), "ctx", split_axis=1, concat_axis=1, tiled=True
        ),
        lax.all_to_all(
            inverse_second(corr_cols, peer_count), "ctx", split_axis=1, concat_axis=1, tiled=True
        ),
    )
    corr_time = lax.psum_scatter(corr_time, "chan", scatter_dimension=0, tiled=True)
    weight = skip_weight[:, None]
    outputs = conv_time + weight * signal.astype(jnp.float32)
    grad_gating = (cotangent.astype(jnp.float32) * outputs).astype(jnp.bfloat16)
    grad_signal = (back_time + weight * gated_grad.astype(jnp.float32)).astype(jnp.bfloat16)
    normal_scale = 1.0 / math.sqrt(length * peer_count * local_group * lax.axis_size("chan"))
    grad_filters = corr_time * normal_scale
    return (grad_signal, grad_gating, grad_filters)


def per_device(signal, gating, cotangent, filters, skip_weight):
    peers, groups = lax.axis_size("ctx"), lax.axis_size("chan")
    channels, length = signal.shape
    one_each = channels == filters.shape[0] == peers * groups
    whole_tiles = length % (8 * LANES) == 0 and (length // LANES) % groups == 0
    if one_each and whole_tiles and 2 * (length // LANES // groups) <= length // LANES:
        return filter_per_device(signal, gating, cotangent, filters, skip_weight)
    return split_transforms(signal, gating, cotangent, filters, skip_weight)


def solution(mesh):
    in_specs = (P("chan", "ctx"), P("chan", "ctx"), P("chan", "ctx"), P(None, "ctx"), P("chan"))
    out_specs = (P("chan", "ctx"), P("chan", "ctx"), P("chan", "ctx"))
    return jax.shard_map(
        per_device, mesh=mesh, in_specs=in_specs, out_specs=out_specs, check_vma=False
    )
```

```python
import functools
import math

import jax
import jax.numpy as jnp
import numpy as np
from jax import lax
from jax.experimental import pallas as pl
from jax.experimental.pallas import tpu as pltpu
from jax.sharding import PartitionSpec as P

LANES = 128
TILE = 2


def split_table(table):
    high = table.astype(jnp.bfloat16)
    low = (table - high.astype(np.float64)).astype(jnp.bfloat16)
    return high, low


def dft_tables(rows):
    height = 2 * rows
    padded = height * LANES
    k1 = np.arange(rows)
    n1 = np.arange(rows)
    n2 = np.arange(LANES)
    outer = np.pi * (np.outer(2 * k1 + 1, n1) % (2 * height)) / height
    high, low = split_table(np.concatenate([np.cos(outer), -np.sin(outer)], axis=0))
    first = np.concatenate([high, low, high, low], axis=1)
    turn = np.pi * (np.outer(2 * k1 + 1, n2) % (2 * padded)) / padded
    twiddle = np.stack([np.cos(turn), np.sin(turn)]).astype(np.float32)
    inner = 2.0 * np.pi * (np.outer(n2, n2) % LANES) / LANES
    cosine, sine = np.cos(inner), np.sin(inner)
    high, low = split_table(np.block([[cosine, -sine], [sine, cosine]]))
    second = np.concatenate([high, high, low], axis=0)
    high, low = split_table(np.concatenate([np.cos(outer.T), -np.sin(outer.T)], axis=1) * (2.0 / padded))
    last = np.block([[high, high], [low, np.zeros_like(low)]])
    return first, twiddle, second, last


def dot(left, right):
    return jnp.dot(left, right, preferred_element_type=jnp.float32)


def split(values):
    high = values.astype(jnp.bfloat16)
    return high, (values - high.astype(jnp.float32)).astype(jnp.bfloat16)


def spectral_kernel(
    groups, peers, scale, got_ref, first_ref, twiddle_ref, second_ref, last_ref, out_ref, in_ref, part_ref, spec_ref, back_ref
):
    piece = out_ref.shape[1] // 3
    taps = piece // groups
    rows = peers * piece
    kept = twiddle_ref.shape[1]
    count = 2 * groups
    got = got_ref[...].astype(jnp.float32).reshape(peers * groups, -1, LANES)

    def gather(group, start):
        parts = [got[peer * groups + group][start : start + piece] for peer in range(peers)]
        return jnp.concatenate(parts, axis=0).astype(jnp.bfloat16)

    for sequence in range(count):
        group, start = sequence % groups, sequence // groups * piece
        values = gather(group, start)
        in_ref[0:rows, sequence * LANES : (sequence + 1) * LANES] = values
        in_ref[rows : 2 * rows, sequence * LANES : (sequence + 1) * LANES] = values
    tap_high = jnp.concatenate([part[2 * piece : 2 * piece + taps] for part in got], axis=0).astype(jnp.bfloat16)
    tap_in = jnp.concatenate([tap_high, tap_high], axis=0)
    cosine, sine = twiddle_ref[0], twiddle_ref[1]
    stage = dot(first_ref[:, : 2 * rows], in_ref[...])
    tap_stage = dot(first_ref[:, : 2 * rows], tap_in)
    total = (count + 1) * kept

    def store_parts(sequence, values):
        high, low = split(values)
        at = slice(sequence * kept, (sequence + 1) * kept)
        part_ref[at, : 2 * LANES] = high
        part_ref[at, 2 * LANES : 4 * LANES] = low
        part_ref[at, 4 * LANES :] = high

    for sequence in range(count + 1):
        source = tap_stage if sequence == count else stage[:, sequence * LANES : (sequence + 1) * LANES]
        real, imag = source[:kept], source[kept:]
        turned = jnp.concatenate([real * cosine + imag * sine, imag * cosine - real * sine], axis=1)
        store_parts(sequence, turned)

    def second_stage():
        step = pl.cdiv(total, 4 * 16) * 16
        for at in range(0, total, step):
            stop = min(at + step, total)
            spec_ref[at:stop] = dot(part_ref[at:stop], second_ref[...])

    second_stage()
    tap = spec_ref[count * kept : total]
    tap_real, tap_imag = tap[:, :LANES], tap[:, LANES:]
    corr_real = corr_imag = None

    def put(sequence, real, imag):
        store_parts(sequence, jnp.concatenate([imag, real], axis=1))

    for group in range(groups):
        sig = spec_ref[group * kept : (group + 1) * kept]
        gat = spec_ref[(groups + group) * kept : (groups + group + 1) * kept]
        sr, si, gr, gi = sig[:, :LANES], sig[:, LANES:], gat[:, :LANES], gat[:, LANES:]
        put(group, sr * tap_real - si * tap_imag, sr * tap_imag + si * tap_real)
        put(groups + group, tap_real * gr + tap_imag * gi, tap_real * gi - tap_imag * gr)
        cr, ci = sr * gr + si * gi, sr * gi - si * gr
        corr_real, corr_imag = (cr, ci) if corr_real is None else (corr_real + cr, corr_imag + ci)
    put(count, corr_real * scale, corr_imag * scale)
    second_stage()
    for sequence in range(count + 1):
        both = spec_ref[sequence * kept : (sequence + 1) * kept]
        imag, real = both[:, :LANES], both[:, LANES:]
        turned = jnp.concatenate([real * cosine - imag * sine, imag * cosine + real * sine], axis=0)
        high, low = split(turned)
        back_ref[: 2 * kept, sequence * LANES : (sequence + 1) * LANES] = high
        back_ref[2 * kept :, sequence * LANES : (sequence + 1) * LANES] = low
    both = dot(last_ref[...], back_ref[...])
    result = both[:rows] + both[rows:]
    for peer in range(peers):
        piece_rows = result[peer * piece : (peer + 1) * piece]
        for group in range(groups):
            cut = lambda sequence: piece_rows[:, sequence * LANES : (sequence + 1) * LANES]
            message = jnp.concatenate([cut(group), cut(groups + group), cut(count)], axis=0)
            out_ref[peer * groups + group] = message.astype(jnp.bfloat16)


def spectral_products(got, piece, groups, peers, scale):
    rows = peers * piece
    tables = dft_tables(rows)
    kept = tables[1].shape[1]
    total = (2 * groups + 1) * kept
    vmem = pl.BlockSpec(memory_space=pltpu.VMEM)
    return pl.pallas_call(
        functools.partial(spectral_kernel, groups, peers, scale),
        out_shape=jax.ShapeDtypeStruct((got.shape[0], 3 * piece, LANES), jnp.bfloat16),
        in_specs=[vmem] * 5,
        out_specs=vmem,
        scratch_shapes=[
            pltpu.VMEM((2 * rows, 2 * groups * LANES), jnp.bfloat16),
            pltpu.VMEM((total, 6 * LANES), jnp.bfloat16),
            pltpu.VMEM((total, 2 * LANES), jnp.float32),
            pltpu.VMEM((4 * kept, (2 * groups + 1) * LANES), jnp.bfloat16),
        ],
        compiler_params=pltpu.CompilerParams(vmem_limit_bytes=24 * 2**20),
        name="spectral_products",
    )(got, *[jnp.asarray(table) for table in tables])


def tile_rows(values):
    return values.reshape(values.shape[0], values.shape[1] // LANES, LANES)


def pack_kernel(
    groups,
    signal_hbm,
    gating_hbm,
    cotangent_hbm,
    filters_hbm,
    weight_hbm,
    message_ref,
    column_ref,
    signal_ref,
    gating_ref,
    cotangent_ref,
    taps_ref,
    weight_ref,
    sems,
):
    channels, length = signal_ref.shape
    share = length // groups
    start = pl.multiple_of(lax.axis_index("chan") * share, share)
    copies = [
        pltpu.make_async_copy(source, target, sems.at[at])
        for at, (source, target) in enumerate(
            [
                (cotangent_hbm, cotangent_ref),
                (gating_hbm, gating_ref),
                (signal_hbm, signal_ref),
                (filters_hbm.at[:, pl.ds(start, share)], taps_ref),
                (weight_hbm, weight_ref),
            ]
        )
    ]
    for copy in copies:
        copy.start()
    for copy in copies:
        copy.wait()
    signal = signal_ref[...].astype(jnp.float32)
    gated = cotangent_ref[...].astype(jnp.float32) * gating_ref[...].astype(jnp.float32)
    rows = tile_rows(jnp.concatenate([signal, gated, taps_ref[...]], axis=1))
    message_ref[...] = rows.reshape(message_ref.shape).astype(jnp.bfloat16)
    square = (channels, channels)
    diagonal = lax.broadcasted_iota(jnp.int32, square, 0) == lax.broadcasted_iota(jnp.int32, square, 1)
    weight = jnp.sum(jnp.where(diagonal, jnp.broadcast_to(weight_ref[...], square), 0.0), axis=1, keepdims=True)
    column_ref[...] = jnp.broadcast_to(weight, column_ref.shape)


def pack(signal, gating, cotangent, filters, skip_weight, groups):
    channels, length = signal.shape
    vmem = pl.BlockSpec(memory_space=pltpu.VMEM)
    operands = (signal, gating, cotangent, filters, skip_weight[None, :])
    return pl.pallas_call(
        functools.partial(pack_kernel, groups),
        out_shape=(
            jax.ShapeDtypeStruct((channels, (2 * length + length // groups) // (TILE * LANES), TILE, LANES), jnp.bfloat16),
            jax.ShapeDtypeStruct((channels, LANES), jnp.float32),
        ),
        in_specs=[pl.BlockSpec(memory_space=pltpu.HBM)] * 5,
        out_specs=(vmem, vmem),
        scratch_shapes=[pltpu.VMEM(signal.shape, jnp.bfloat16)] * 3
        + [
            pltpu.VMEM((filters.shape[0], length // groups), jnp.float32),
            pltpu.VMEM((1, channels), jnp.float32),
            pltpu.SemaphoreType.DMA((5,)),
        ],
        compiler_params=pltpu.CompilerParams(vmem_limit_bytes=16 * 2**20),
        name="pack",
    )(*[pltpu.with_memory_space_constraint(operand, pltpu.HBM) for operand in operands])


def finish_kernel(groups, home_ref, signal_ref, gating_ref, cotangent_ref, column_ref, signal_out, gating_out, filters_out):
    channels, length = signal_ref.shape
    piece = length // LANES
    share = channels // groups
    home = home_ref[...].astype(jnp.float32).reshape(channels, 3 * length)
    cotangent = cotangent_ref[...].astype(jnp.float32)
    gated = (cotangent * gating_ref[...].astype(jnp.float32)).astype(jnp.bfloat16).astype(jnp.float32)
    weight = column_ref[:, :1]
    outputs = home[:, :length] + weight * signal_ref[...].astype(jnp.float32)
    gating_out[...] = (cotangent * outputs).astype(jnp.bfloat16)
    signal_out[...] = (home[:, length : 2 * length] + weight * gated).astype(jnp.bfloat16)
    first = pl.multiple_of(lax.axis_index("chan") * share, share)
    corr = home_ref[pl.ds(first, share), 2 * piece :, :].astype(jnp.float32)
    filters_out[...] = corr.reshape(share, length)


def finish(home, signal, gating, cotangent, column, groups):
    channels, length = signal.shape
    vmem = pl.BlockSpec(memory_space=pltpu.VMEM)
    return pl.pallas_call(
        functools.partial(finish_kernel, groups),
        out_shape=(
            jax.ShapeDtypeStruct(signal.shape, jnp.bfloat16),
            jax.ShapeDtypeStruct(signal.shape, jnp.bfloat16),
            jax.ShapeDtypeStruct((channels // groups, length), jnp.float32),
        ),
        in_specs=[vmem] * 5,
        out_specs=(vmem,) * 3,
        compiler_params=pltpu.CompilerParams(vmem_limit_bytes=16 * 2**20),
        name="finish",
    )(home, signal, gating, cotangent, column)


def filter_per_device(signal, gating, cotangent, filters, skip_weight):
    peers = lax.axis_size("ctx")
    groups = lax.axis_size("chan")
    both_axes = ("ctx", "chan")
    message, column = pack(signal, gating, cotangent, filters, skip_weight, groups)
    got = lax.all_to_all(message, both_axes, split_axis=0, concat_axis=0, tiled=True)
    scale = 1.0 / math.sqrt(signal.shape[1] * peers * groups)
    result = spectral_products(got, signal.shape[1] // LANES, groups, peers, scale)
    home = lax.all_to_all(result, both_axes, split_axis=0, concat_axis=0, tiled=True)
    return finish(home, signal, gating, cotangent, column, groups)


def product(form, left, right):
    return jnp.einsum(
        form, left, right, precision=lax.Precision.HIGHEST, preferred_element_type=jnp.float32
    )


def phases(left_idx, right_idx, period):
    joined = left_idx[:, None] * right_idx[None, :] % period
    return joined.astype(jnp.float32) * (2.0 * math.pi / period)


def indices(total):
    return jnp.arange(total, dtype=jnp.int32)


def turn_forward(real_part, imag_part, angles):
    cosine = jnp.cos(angles)
    sine_part = jnp.sin(angles)
    return (real_part * cosine + imag_part * sine_part, imag_part * cosine - real_part * sine_part)


def turn_back(real_part, imag_part, angles):
    cosine = jnp.cos(angles)
    sine_part = jnp.sin(angles)
    return (real_part * cosine - imag_part * sine_part, imag_part * cosine + real_part * sine_part)


def first_pass(blocks, position, peer_count):
    height, length = blocks.shape
    piece_len = length // peer_count
    padded = 2 * peer_count * length
    shaped = blocks.reshape(height, peer_count, piece_len)
    angles = phases(indices(peer_count), indices(2 * peer_count), 2 * peer_count)
    real_part = product("rdm,dk->rmk", shaped, jnp.cos(angles))
    imag_part = -product("rdm,dk->rmk", shaped, jnp.sin(angles))
    offsets = position * piece_len + indices(piece_len)
    real_part, imag_part = turn_forward(
        real_part, imag_part, phases(offsets, indices(2 * peer_count), padded)
    )
    return jnp.stack([real_part, imag_part])


def second_pass(columns, peer_count):
    height, piece_len = (columns.shape[1], columns.shape[2])
    length = piece_len * peer_count
    real_part = columns[0].reshape(height, piece_len, peer_count, 2)
    imag_part = columns[1].reshape(height, piece_len, peer_count, 2)
    angles = phases(indices(peer_count), indices(peer_count), peer_count)
    cosine = jnp.cos(angles)
    sine_part = jnp.sin(angles)
    real_one = product("rmeb,ea->rbma", real_part, cosine) + product(
        "rmeb,ea->rbma", imag_part, sine_part
    )
    imag_one = product("rmeb,ea->rbma", imag_part, cosine) - product(
        "rmeb,ea->rbma", real_part, sine_part
    )
    real_one, imag_one = turn_forward(
        real_one, imag_one, phases(indices(piece_len), indices(peer_count), length)
    )
    angles = phases(indices(piece_len), indices(piece_len), piece_len)
    cosine = jnp.cos(angles)
    sine_part = jnp.sin(angles)
    real_two = product("rbma,mc->rbca", real_one, cosine) + product(
        "rbma,mc->rbca", imag_one, sine_part
    )
    imag_two = product("rbma,mc->rbca", imag_one, cosine) - product(
        "rbma,mc->rbca", real_one, sine_part
    )
    return jnp.stack([real_two.reshape(height, 2, length), imag_two.reshape(height, 2, length)])


def inverse_first(spectrum, position, peer_count):
    height, length = (spectrum.shape[1], spectrum.shape[3])
    piece_len = length // peer_count
    padded = 2 * peer_count * length
    real_part = spectrum[0].reshape(height, 2, piece_len, peer_count)
    imag_part = spectrum[1].reshape(height, 2, piece_len, peer_count)
    angles = phases(indices(piece_len), indices(piece_len), piece_len)
    cosine = jnp.cos(angles)
    sine_part = jnp.sin(angles)
    real_one = product("rbca,cm->rbma", real_part, cosine) - product(
        "rbca,cm->rbma", imag_part, sine_part
    )
    imag_one = product("rbca,cm->rbma", imag_part, cosine) + product(
        "rbca,cm->rbma", real_part, sine_part
    )
    real_one, imag_one = turn_back(
        real_one, imag_one, phases(indices(piece_len), indices(peer_count), length)
    )
    angles = phases(indices(peer_count), indices(peer_count), peer_count)
    cosine = jnp.cos(angles)
    sine_part = jnp.sin(angles)
    real_two = product("rbma,ae->rmeb", real_one, cosine) - product(
        "rbma,ae->rmeb", imag_one, sine_part
    )
    imag_two = product("rbma,ae->rmeb", imag_one, cosine) + product(
        "rbma,ae->rmeb", real_one, sine_part
    )
    offsets = (indices(peer_count)[None, :] * piece_len + indices(piece_len)[:, None]).reshape(-1)
    freq_bins = 2 * position + indices(2)
    angles = phases(offsets, freq_bins, padded).reshape(piece_len, peer_count, 2)
    real_two, imag_two = turn_back(real_two, imag_two, angles)
    return jnp.stack(
        [
            real_two.reshape(height, piece_len, 2 * peer_count),
            imag_two.reshape(height, piece_len, 2 * peer_count),
        ]
    )


def inverse_second(received, peer_count):
    height, piece_len = (received.shape[1], received.shape[2])
    length = piece_len * peer_count
    padded = 2 * peer_count * length
    angles = phases(indices(2 * peer_count), indices(peer_count), 2 * peer_count)
    signal_out = product("rmk,kd->rdm", received[0], jnp.cos(angles)) - product(
        "rmk,kd->rdm", received[1], jnp.sin(angles)
    )
    return (signal_out / padded).reshape(height, length)


def split_transforms(signal, gating, cotangent, filters, skip_weight):
    peer_count = lax.axis_size("ctx")
    position = lax.axis_index("ctx")
    channels, length = signal.shape
    count_filters = filters.shape[0]
    local_group = channels // count_filters
    gated_grad = (cotangent.astype(jnp.float32) * gating.astype(jnp.float32)).astype(jnp.bfloat16)
    signal_blocks, gated_blocks = (
        lax.all_to_all(signal, "ctx", split_axis=1, concat_axis=1, tiled=True),
        lax.all_to_all(gated_grad, "ctx", split_axis=1, concat_axis=1, tiled=True),
    )
    tap_blocks = lax.all_to_all(filters, "ctx", split_axis=1, concat_axis=1, tiled=True)
    signal_cols, gated_cols, tap_cols = (
        lax.all_to_all(
            first_pass(signal_blocks.astype(jnp.float32), position, peer_count),
            "ctx",
            split_axis=3,
            concat_axis=3,
            tiled=True,
        ),
        lax.all_to_all(
            first_pass(gated_blocks.astype(jnp.float32), position, peer_count),
            "ctx",
            split_axis=3,
            concat_axis=3,
            tiled=True,
        ),
        lax.all_to_all(
            first_pass(tap_blocks, position, peer_count),
            "ctx",
            split_axis=3,
            concat_axis=3,
            tiled=True,
        ),
    )
    signal_spec = second_pass(signal_cols, peer_count).reshape(
        2, local_group, count_filters, 2, length
    )
    gated_spec = second_pass(gated_cols, peer_count).reshape(
        2, local_group, count_filters, 2, length
    )
    tap_spec = second_pass(tap_cols, peer_count)
    tap_real, tap_imag = (tap_spec[0], tap_spec[1])
    sig_real, sig_imag = (signal_spec[0], signal_spec[1])
    gated_real, gated_imag = (gated_spec[0], gated_spec[1])
    forward_spec = jnp.stack(
        [sig_real * tap_real - sig_imag * tap_imag, sig_real * tap_imag + sig_imag * tap_real]
    ).reshape(2, channels, 2, length)
    back_spec = jnp.stack(
        [
            tap_real * gated_real + tap_imag * gated_imag,
            tap_real * gated_imag - tap_imag * gated_real,
        ]
    ).reshape(2, channels, 2, length)
    corr_spec = jnp.stack(
        [
            jnp.sum(sig_real * gated_real + sig_imag * gated_imag, axis=0),
            jnp.sum(sig_real * gated_imag - sig_imag * gated_real, axis=0),
        ]
    )
    forward_cols, back_cols, corr_cols = (
        lax.all_to_all(
            inverse_first(forward_spec, position, peer_count),
            "ctx",
            split_axis=3,
            concat_axis=3,
            tiled=True,
        ),
        lax.all_to_all(
            inverse_first(back_spec, position, peer_count),
            "ctx",
            split_axis=3,
            concat_axis=3,
            tiled=True,
        ),
        lax.all_to_all(
            inverse_first(corr_spec, position, peer_count),
            "ctx",
            split_axis=3,
            concat_axis=3,
            tiled=True,
        ),
    )
    conv_time, back_time, corr_time = (
        lax.all_to_all(
            inverse_second(forward_cols, peer_count), "ctx", split_axis=1, concat_axis=1, tiled=True
        ),
        lax.all_to_all(
            inverse_second(back_cols, peer_count), "ctx", split_axis=1, concat_axis=1, tiled=True
        ),
        lax.all_to_all(
            inverse_second(corr_cols, peer_count), "ctx", split_axis=1, concat_axis=1, tiled=True
        ),
    )
    corr_time = lax.psum_scatter(corr_time, "chan", scatter_dimension=0, tiled=True)
    weight = skip_weight[:, None]
    outputs = conv_time + weight * signal.astype(jnp.float32)
    grad_gating = (cotangent.astype(jnp.float32) * outputs).astype(jnp.bfloat16)
    grad_signal = (back_time + weight * gated_grad.astype(jnp.float32)).astype(jnp.bfloat16)
    normal_scale = 1.0 / math.sqrt(length * peer_count * local_group * lax.axis_size("chan"))
    grad_filters = corr_time * normal_scale
    return (grad_signal, grad_gating, grad_filters)


def per_device(signal, gating, cotangent, filters, skip_weight):
    peers, groups = lax.axis_size("ctx"), lax.axis_size("chan")
    channels, length = signal.shape
    one_each = channels == filters.shape[0] == peers * groups
    piece = length // LANES
    whole_tiles = length % (8 * LANES) == 0 and piece % groups == 0
    if one_each and whole_tiles and (peers * piece) % 16 == 0 and (piece // groups) % TILE == 0:
        return filter_per_device(signal, gating, cotangent, filters, skip_weight)
    return split_transforms(signal, gating, cotangent, filters, skip_weight)


def solution(mesh):
    in_specs = (P("chan", "ctx"), P("chan", "ctx"), P("chan", "ctx"), P(None, "ctx"), P("chan"))
    out_specs = (P("chan", "ctx"), P("chan", "ctx"), P("chan", "ctx"))
    return jax.shard_map(
        per_device, mesh=mesh, in_specs=in_specs, out_specs=out_specs, check_vma=False
    )
```

```python
import functools
import math

import jax
import jax.numpy as jnp
import numpy as np
from jax import lax
from jax.experimental import pallas as pl
from jax.experimental.pallas import tpu as pltpu
from jax.sharding import PartitionSpec as P

LANES = 128
TILE = 2


def split_table(table):
    high = table.astype(jnp.bfloat16)
    low = (table - high.astype(np.float64)).astype(jnp.bfloat16)
    return high, low


def dft_tables(rows):
    height = 2 * rows
    padded = height * LANES
    k1 = np.arange(rows)
    n1 = np.arange(rows)
    n2 = np.arange(LANES)
    outer = np.pi * (np.outer(2 * k1 + 1, n1) % (2 * height)) / height
    high, low = split_table(np.concatenate([np.cos(outer), -np.sin(outer)], axis=0))
    first = np.concatenate([high, low], axis=1)
    turn = np.pi * (np.outer(2 * k1 + 1, n2) % (2 * padded)) / padded
    twiddle = np.stack([np.cos(turn), np.sin(turn)]).astype(np.float32)
    inner = 2.0 * np.pi * (np.outer(n2, n2) % LANES) / LANES
    cosine, sine = np.cos(inner), np.sin(inner)
    second = np.block([[cosine, -sine], [sine, cosine]]).astype(jnp.bfloat16)
    high, low = split_table(np.concatenate([np.cos(outer.T), -np.sin(outer.T)], axis=1) * (2.0 / padded))
    last = np.concatenate([high, low], axis=0)
    return first, twiddle, second, last


def dot(left, right):
    return jnp.dot(left, right, preferred_element_type=jnp.float32)


def split(values):
    high = values.astype(jnp.bfloat16)
    return high, (values - high.astype(jnp.float32)).astype(jnp.bfloat16)


def spectral_kernel(
    groups, peers, scale, got_ref, first_ref, twiddle_ref, second_ref, last_ref, out_ref
):
    piece = out_ref.shape[1] // 3
    taps = piece // groups
    rows = peers * piece
    kept = twiddle_ref.shape[1]
    count = 2 * groups
    got = got_ref[...].astype(jnp.float32).reshape(peers * groups, -1, LANES)

    def gather(group, start):
        parts = [got[peer * groups + group][start : start + piece] for peer in range(peers)]
        return jnp.concatenate(parts, axis=0).astype(jnp.bfloat16)

    cosine, sine = twiddle_ref[0], twiddle_ref[1]
    second = second_ref[...]

    def first_stage(values):
        return dot(first_ref[...], jnp.concatenate([values, values], axis=0))

    def turn_forward(stage):
        parts = []
        for at in range(0, stage.shape[1], LANES):
            real, imag = stage[:kept, at : at + LANES], stage[kept:, at : at + LANES]
            turned = jnp.concatenate([real * cosine + imag * sine, imag * cosine - real * sine], axis=1)
            parts.append(turned.astype(jnp.bfloat16))
        return parts

    def second_stage(parts):
        both = dot(jnp.concatenate(parts, axis=0), second)
        cuts = [both[at : at + kept] for at in range(0, both.shape[0], kept)]
        return [(cut[:, :LANES], cut[:, LANES:]) for cut in cuts]

    def swapped(real, imag):
        return jnp.concatenate([imag, real], axis=1).astype(jnp.bfloat16)

    def last_stage(swapped_pairs):
        parts = []
        for imag, real in swapped_pairs:
            turned = jnp.concatenate([real * cosine - imag * sine, imag * cosine + real * sine], axis=0)
            parts.append(turned.astype(jnp.bfloat16))
        both = dot(last_ref[...], jnp.concatenate(parts, axis=1))
        return both[:rows] + both[rows:]

    taps_in = jnp.concatenate([part[2 * piece : 2 * piece + taps] for part in got], axis=0).astype(jnp.bfloat16)
    signal_in = jnp.concatenate([gather(group, 0) for group in range(groups)] + [taps_in], axis=1)
    grad_in = jnp.concatenate([gather(group, piece) for group in range(groups)], axis=1)
    signal_stage = first_stage(signal_in)
    grad_stage = first_stage(grad_in)
    forward = second_stage(turn_forward(signal_stage) + turn_forward(grad_stage))
    signals, (tap_real, tap_imag), grads = forward[:groups], forward[groups], forward[groups + 1 :]
    conv_parts = [swapped(r * tap_real - i * tap_imag, r * tap_imag + i * tap_real) for r, i in signals]
    back_parts = [swapped(tap_real * r + tap_imag * i, tap_real * i - tap_imag * r) for r, i in grads]
    corr_real = sum(sr * gr + si * gi for (sr, si), (gr, gi) in zip(signals, grads)) * scale
    corr_imag = sum(sr * gi - si * gr for (sr, si), (gr, gi) in zip(signals, grads)) * scale
    result = last_stage(second_stage(conv_parts + back_parts + [swapped(corr_real, corr_imag)]))
    for peer in range(peers):
        piece_rows = result[peer * piece : (peer + 1) * piece]
        for group in range(groups):
            cut = lambda sequence: piece_rows[:, sequence * LANES : (sequence + 1) * LANES]
            message = jnp.concatenate([cut(group), cut(groups + group), cut(count)], axis=0)
            out_ref[peer * groups + group] = message.astype(jnp.bfloat16)


def spectral_products(got, piece, groups, peers, scale):
    rows = peers * piece
    tables = dft_tables(rows)
    vmem = pl.BlockSpec(memory_space=pltpu.VMEM)
    return pl.pallas_call(
        functools.partial(spectral_kernel, groups, peers, scale),
        out_shape=jax.ShapeDtypeStruct((got.shape[0], 3 * piece, LANES), jnp.bfloat16),
        in_specs=[vmem] * 5,
        out_specs=vmem,
        compiler_params=pltpu.CompilerParams(vmem_limit_bytes=24 * 2**20),
        name="spectral_products",
    )(got, *[jnp.asarray(table) for table in tables])


def tile_rows(values):
    return values.reshape(values.shape[0], values.shape[1] // LANES, LANES)


def pack_kernel(
    groups,
    signal_hbm,
    gating_hbm,
    cotangent_hbm,
    filters_hbm,
    weight_hbm,
    message_ref,
    column_ref,
    signal_ref,
    gating_ref,
    cotangent_ref,
    taps_ref,
    weight_ref,
    sems,
):
    channels, length = signal_ref.shape
    share = length // groups
    start = pl.multiple_of(lax.axis_index("chan") * share, share)
    copies = [
        pltpu.make_async_copy(source, target, sems.at[at])
        for at, (source, target) in enumerate(
            [
                (cotangent_hbm, cotangent_ref),
                (gating_hbm, gating_ref),
                (signal_hbm, signal_ref),
                (filters_hbm.at[:, pl.ds(start, share)], taps_ref),
                (weight_hbm, weight_ref),
            ]
        )
    ]
    for copy in copies:
        copy.start()
    for copy in copies:
        copy.wait()
    signal = signal_ref[...].astype(jnp.float32)
    gated = cotangent_ref[...].astype(jnp.float32) * gating_ref[...].astype(jnp.float32)
    rows = tile_rows(jnp.concatenate([signal, gated, taps_ref[...]], axis=1))
    message_ref[...] = rows.reshape(message_ref.shape).astype(jnp.bfloat16)
    square = (channels, channels)
    diagonal = lax.broadcasted_iota(jnp.int32, square, 0) == lax.broadcasted_iota(jnp.int32, square, 1)
    weight = jnp.sum(jnp.where(diagonal, jnp.broadcast_to(weight_ref[...], square), 0.0), axis=1, keepdims=True)
    column_ref[...] = jnp.broadcast_to(weight, column_ref.shape)


def pack(signal, gating, cotangent, filters, skip_weight, groups):
    channels, length = signal.shape
    vmem = pl.BlockSpec(memory_space=pltpu.VMEM)
    operands = (signal, gating, cotangent, filters, skip_weight[None, :])
    return pl.pallas_call(
        functools.partial(pack_kernel, groups),
        out_shape=(
            jax.ShapeDtypeStruct((channels, (2 * length + length // groups) // (TILE * LANES), TILE, LANES), jnp.bfloat16),
            jax.ShapeDtypeStruct((channels, LANES), jnp.float32),
        ),
        in_specs=[pl.BlockSpec(memory_space=pltpu.HBM)] * 5,
        out_specs=(vmem, vmem),
        scratch_shapes=[pltpu.VMEM(signal.shape, jnp.bfloat16)] * 3
        + [
            pltpu.VMEM((filters.shape[0], length // groups), jnp.float32),
            pltpu.VMEM((1, channels), jnp.float32),
            pltpu.SemaphoreType.DMA((5,)),
        ],
        compiler_params=pltpu.CompilerParams(vmem_limit_bytes=16 * 2**20),
        name="pack",
    )(*[pltpu.with_memory_space_constraint(operand, pltpu.HBM) for operand in operands])


def finish_kernel(groups, home_ref, signal_ref, gating_ref, cotangent_ref, column_ref, signal_out, gating_out, filters_out):
    channels, length = signal_ref.shape
    piece = length // LANES
    share = channels // groups
    home = home_ref[...].astype(jnp.float32).reshape(channels, 3 * length)
    cotangent = cotangent_ref[...].astype(jnp.float32)
    gated = (cotangent * gating_ref[...].astype(jnp.float32)).astype(jnp.bfloat16).astype(jnp.float32)
    weight = column_ref[:, :1]
    outputs = home[:, :length] + weight * signal_ref[...].astype(jnp.float32)
    gating_out[...] = (cotangent * outputs).astype(jnp.bfloat16)
    signal_out[...] = (home[:, length : 2 * length] + weight * gated).astype(jnp.bfloat16)
    first = pl.multiple_of(lax.axis_index("chan") * share, share)
    corr = home_ref[pl.ds(first, share), 2 * piece :, :].astype(jnp.float32)
    filters_out[...] = corr.reshape(share, length)


def finish(home, signal, gating, cotangent, column, groups):
    channels, length = signal.shape
    vmem = pl.BlockSpec(memory_space=pltpu.VMEM)
    return pl.pallas_call(
        functools.partial(finish_kernel, groups),
        out_shape=(
            jax.ShapeDtypeStruct(signal.shape, jnp.bfloat16),
            jax.ShapeDtypeStruct(signal.shape, jnp.bfloat16),
            jax.ShapeDtypeStruct((channels // groups, length), jnp.float32),
        ),
        in_specs=[vmem] * 5,
        out_specs=(vmem,) * 3,
        compiler_params=pltpu.CompilerParams(vmem_limit_bytes=16 * 2**20),
        name="finish",
    )(home, signal, gating, cotangent, column)


def filter_per_device(signal, gating, cotangent, filters, skip_weight):
    peers = lax.axis_size("ctx")
    groups = lax.axis_size("chan")
    both_axes = ("ctx", "chan")
    message, column = pack(signal, gating, cotangent, filters, skip_weight, groups)
    got = lax.all_to_all(message, both_axes, split_axis=0, concat_axis=0, tiled=True)
    scale = 1.0 / math.sqrt(signal.shape[1] * peers * groups)
    result = spectral_products(got, signal.shape[1] // LANES, groups, peers, scale)
    home = lax.all_to_all(result, both_axes, split_axis=0, concat_axis=0, tiled=True)
    return finish(home, signal, gating, cotangent, column, groups)


def product(form, left, right):
    return jnp.einsum(
        form, left, right, precision=lax.Precision.HIGHEST, preferred_element_type=jnp.float32
    )


def phases(left_idx, right_idx, period):
    joined = left_idx[:, None] * right_idx[None, :] % period
    return joined.astype(jnp.float32) * (2.0 * math.pi / period)


def indices(total):
    return jnp.arange(total, dtype=jnp.int32)


def turn_forward(real_part, imag_part, angles):
    cosine = jnp.cos(angles)
    sine_part = jnp.sin(angles)
    return (real_part * cosine + imag_part * sine_part, imag_part * cosine - real_part * sine_part)


def turn_back(real_part, imag_part, angles):
    cosine = jnp.cos(angles)
    sine_part = jnp.sin(angles)
    return (real_part * cosine - imag_part * sine_part, imag_part * cosine + real_part * sine_part)


def first_pass(blocks, position, peer_count):
    height, length = blocks.shape
    piece_len = length // peer_count
    padded = 2 * peer_count * length
    shaped = blocks.reshape(height, peer_count, piece_len)
    angles = phases(indices(peer_count), indices(2 * peer_count), 2 * peer_count)
    real_part = product("rdm,dk->rmk", shaped, jnp.cos(angles))
    imag_part = -product("rdm,dk->rmk", shaped, jnp.sin(angles))
    offsets = position * piece_len + indices(piece_len)
    real_part, imag_part = turn_forward(
        real_part, imag_part, phases(offsets, indices(2 * peer_count), padded)
    )
    return jnp.stack([real_part, imag_part])


def second_pass(columns, peer_count):
    height, piece_len = (columns.shape[1], columns.shape[2])
    length = piece_len * peer_count
    real_part = columns[0].reshape(height, piece_len, peer_count, 2)
    imag_part = columns[1].reshape(height, piece_len, peer_count, 2)
    angles = phases(indices(peer_count), indices(peer_count), peer_count)
    cosine = jnp.cos(angles)
    sine_part = jnp.sin(angles)
    real_one = product("rmeb,ea->rbma", real_part, cosine) + product(
        "rmeb,ea->rbma", imag_part, sine_part
    )
    imag_one = product("rmeb,ea->rbma", imag_part, cosine) - product(
        "rmeb,ea->rbma", real_part, sine_part
    )
    real_one, imag_one = turn_forward(
        real_one, imag_one, phases(indices(piece_len), indices(peer_count), length)
    )
    angles = phases(indices(piece_len), indices(piece_len), piece_len)
    cosine = jnp.cos(angles)
    sine_part = jnp.sin(angles)
    real_two = product("rbma,mc->rbca", real_one, cosine) + product(
        "rbma,mc->rbca", imag_one, sine_part
    )
    imag_two = product("rbma,mc->rbca", imag_one, cosine) - product(
        "rbma,mc->rbca", real_one, sine_part
    )
    return jnp.stack([real_two.reshape(height, 2, length), imag_two.reshape(height, 2, length)])


def inverse_first(spectrum, position, peer_count):
    height, length = (spectrum.shape[1], spectrum.shape[3])
    piece_len = length // peer_count
    padded = 2 * peer_count * length
    real_part = spectrum[0].reshape(height, 2, piece_len, peer_count)
    imag_part = spectrum[1].reshape(height, 2, piece_len, peer_count)
    angles = phases(indices(piece_len), indices(piece_len), piece_len)
    cosine = jnp.cos(angles)
    sine_part = jnp.sin(angles)
    real_one = product("rbca,cm->rbma", real_part, cosine) - product(
        "rbca,cm->rbma", imag_part, sine_part
    )
    imag_one = product("rbca,cm->rbma", imag_part, cosine) + product(
        "rbca,cm->rbma", real_part, sine_part
    )
    real_one, imag_one = turn_back(
        real_one, imag_one, phases(indices(piece_len), indices(peer_count), length)
    )
    angles = phases(indices(peer_count), indices(peer_count), peer_count)
    cosine = jnp.cos(angles)
    sine_part = jnp.sin(angles)
    real_two = product("rbma,ae->rmeb", real_one, cosine) - product(
        "rbma,ae->rmeb", imag_one, sine_part
    )
    imag_two = product("rbma,ae->rmeb", imag_one, cosine) + product(
        "rbma,ae->rmeb", real_one, sine_part
    )
    offsets = (indices(peer_count)[None, :] * piece_len + indices(piece_len)[:, None]).reshape(-1)
    freq_bins = 2 * position + indices(2)
    angles = phases(offsets, freq_bins, padded).reshape(piece_len, peer_count, 2)
    real_two, imag_two = turn_back(real_two, imag_two, angles)
    return jnp.stack(
        [
            real_two.reshape(height, piece_len, 2 * peer_count),
            imag_two.reshape(height, piece_len, 2 * peer_count),
        ]
    )


def inverse_second(received, peer_count):
    height, piece_len = (received.shape[1], received.shape[2])
    length = piece_len * peer_count
    padded = 2 * peer_count * length
    angles = phases(indices(2 * peer_count), indices(peer_count), 2 * peer_count)
    signal_out = product("rmk,kd->rdm", received[0], jnp.cos(angles)) - product(
        "rmk,kd->rdm", received[1], jnp.sin(angles)
    )
    return (signal_out / padded).reshape(height, length)


def split_transforms(signal, gating, cotangent, filters, skip_weight):
    peer_count = lax.axis_size("ctx")
    position = lax.axis_index("ctx")
    channels, length = signal.shape
    count_filters = filters.shape[0]
    local_group = channels // count_filters
    gated_grad = (cotangent.astype(jnp.float32) * gating.astype(jnp.float32)).astype(jnp.bfloat16)
    signal_blocks, gated_blocks = (
        lax.all_to_all(signal, "ctx", split_axis=1, concat_axis=1, tiled=True),
        lax.all_to_all(gated_grad, "ctx", split_axis=1, concat_axis=1, tiled=True),
    )
    tap_blocks = lax.all_to_all(filters, "ctx", split_axis=1, concat_axis=1, tiled=True)
    signal_cols, gated_cols, tap_cols = (
        lax.all_to_all(
            first_pass(signal_blocks.astype(jnp.float32), position, peer_count),
            "ctx",
            split_axis=3,
            concat_axis=3,
            tiled=True,
        ),
        lax.all_to_all(
            first_pass(gated_blocks.astype(jnp.float32), position, peer_count),
            "ctx",
            split_axis=3,
            concat_axis=3,
            tiled=True,
        ),
        lax.all_to_all(
            first_pass(tap_blocks, position, peer_count),
            "ctx",
            split_axis=3,
            concat_axis=3,
            tiled=True,
        ),
    )
    signal_spec = second_pass(signal_cols, peer_count).reshape(
        2, local_group, count_filters, 2, length
    )
    gated_spec = second_pass(gated_cols, peer_count).reshape(
        2, local_group, count_filters, 2, length
    )
    tap_spec = second_pass(tap_cols, peer_count)
    tap_real, tap_imag = (tap_spec[0], tap_spec[1])
    sig_real, sig_imag = (signal_spec[0], signal_spec[1])
    gated_real, gated_imag = (gated_spec[0], gated_spec[1])
    forward_spec = jnp.stack(
        [sig_real * tap_real - sig_imag * tap_imag, sig_real * tap_imag + sig_imag * tap_real]
    ).reshape(2, channels, 2, length)
    back_spec = jnp.stack(
        [
            tap_real * gated_real + tap_imag * gated_imag,
            tap_real * gated_imag - tap_imag * gated_real,
        ]
    ).reshape(2, channels, 2, length)
    corr_spec = jnp.stack(
        [
            jnp.sum(sig_real * gated_real + sig_imag * gated_imag, axis=0),
            jnp.sum(sig_real * gated_imag - sig_imag * gated_real, axis=0),
        ]
    )
    forward_cols, back_cols, corr_cols = (
        lax.all_to_all(
            inverse_first(forward_spec, position, peer_count),
            "ctx",
            split_axis=3,
            concat_axis=3,
            tiled=True,
        ),
        lax.all_to_all(
            inverse_first(back_spec, position, peer_count),
            "ctx",
            split_axis=3,
            concat_axis=3,
            tiled=True,
        ),
        lax.all_to_all(
            inverse_first(corr_spec, position, peer_count),
            "ctx",
            split_axis=3,
            concat_axis=3,
            tiled=True,
        ),
    )
    conv_time, back_time, corr_time = (
        lax.all_to_all(
            inverse_second(forward_cols, peer_count), "ctx", split_axis=1, concat_axis=1, tiled=True
        ),
        lax.all_to_all(
            inverse_second(back_cols, peer_count), "ctx", split_axis=1, concat_axis=1, tiled=True
        ),
        lax.all_to_all(
            inverse_second(corr_cols, peer_count), "ctx", split_axis=1, concat_axis=1, tiled=True
        ),
    )
    corr_time = lax.psum_scatter(corr_time, "chan", scatter_dimension=0, tiled=True)
    weight = skip_weight[:, None]
    outputs = conv_time + weight * signal.astype(jnp.float32)
    grad_gating = (cotangent.astype(jnp.float32) * outputs).astype(jnp.bfloat16)
    grad_signal = (back_time + weight * gated_grad.astype(jnp.float32)).astype(jnp.bfloat16)
    normal_scale = 1.0 / math.sqrt(length * peer_count * local_group * lax.axis_size("chan"))
    grad_filters = corr_time * normal_scale
    return (grad_signal, grad_gating, grad_filters)


def per_device(signal, gating, cotangent, filters, skip_weight):
    peers, groups = lax.axis_size("ctx"), lax.axis_size("chan")
    channels, length = signal.shape
    one_each = channels == filters.shape[0] == peers * groups
    piece = length // LANES
    whole_tiles = length % (8 * LANES) == 0 and piece % groups == 0
    if one_each and whole_tiles and (peers * piece) % 16 == 0 and (piece // groups) % TILE == 0:
        return filter_per_device(signal, gating, cotangent, filters, skip_weight)
    return split_transforms(signal, gating, cotangent, filters, skip_weight)


def solution(mesh):
    in_specs = (P("chan", "ctx"), P("chan", "ctx"), P("chan", "ctx"), P(None, "ctx"), P("chan"))
    out_specs = (P("chan", "ctx"), P("chan", "ctx"), P("chan", "ctx"))
    return jax.shard_map(
        per_device, mesh=mesh, in_specs=in_specs, out_specs=out_specs, check_vma=False
    )
```

```python
import functools
import math

import jax
import jax.numpy as jnp
import numpy as np
from jax import lax
from jax.experimental import pallas as pl
from jax.experimental.pallas import tpu as pltpu
from jax.sharding import PartitionSpec as P

LANES = 128
TILE = 2


def split_table(table):
    high = table.astype(jnp.bfloat16)
    low = (table - high.astype(np.float64)).astype(jnp.bfloat16)
    return high, low


def dft_tables(rows):
    height = 2 * rows
    padded = height * LANES
    k1 = np.arange(rows)
    n1 = np.arange(rows)
    n2 = np.arange(LANES)
    outer = np.pi * (np.outer(2 * k1 + 1, n1) % (2 * height)) / height
    high, low = split_table(np.concatenate([np.cos(outer), -np.sin(outer)], axis=0))
    first = np.concatenate([high, low], axis=1)
    turn = np.pi * (np.outer(2 * k1 + 1, n2) % (2 * padded)) / padded
    twiddle = np.stack([np.cos(turn), np.sin(turn)]).astype(np.float32)
    inner = 2.0 * np.pi * (np.outer(n2, n2) % LANES) / LANES
    cosine, sine = np.cos(inner), np.sin(inner)
    second = np.block([[cosine, -sine], [sine, cosine]]).astype(jnp.bfloat16)
    high, low = split_table(np.concatenate([np.cos(outer.T), -np.sin(outer.T)], axis=1) * (2.0 / padded))
    last = np.concatenate([high, low], axis=0)
    return first, twiddle, second, last


def dot(left, right):
    return jnp.dot(left, right, preferred_element_type=jnp.float32)


def split(values):
    high = values.astype(jnp.bfloat16)
    return high, (values - high.astype(jnp.float32)).astype(jnp.bfloat16)


def slot_order(peers, groups):
    if peers % 2 or groups % 2:
        return list(range(peers * groups))
    return [
        (high * 2 + low) * groups + (plane * 2 + core)
        for plane in range(groups // 2)
        for low in range(2)
        for high in reversed(range(peers // 2))
        for core in range(2)
    ]


def spectral_kernel(
    groups, peers, scale, got_ref, first_ref, twiddle_ref, second_ref, last_ref, out_ref
):
    piece = out_ref.shape[1] // 3
    taps = piece // groups
    rows = peers * piece
    kept = twiddle_ref.shape[1]
    count = 2 * groups
    order = slot_order(peers, groups)
    slots = [order.index(device) for device in range(peers * groups)]
    got = got_ref[...].astype(jnp.float32).reshape(peers * groups, -1, LANES)
    got = [got[slot] for slot in slots]

    def gather(group, start):
        parts = [got[peer * groups + group][start : start + piece] for peer in range(peers)]
        return jnp.concatenate(parts, axis=0).astype(jnp.bfloat16)

    cosine, sine = twiddle_ref[0], twiddle_ref[1]
    second = second_ref[...]

    def first_stage(values):
        return dot(first_ref[...], jnp.concatenate([values, values], axis=0))

    def turn_forward(stage):
        parts = []
        for at in range(0, stage.shape[1], LANES):
            real, imag = stage[:kept, at : at + LANES], stage[kept:, at : at + LANES]
            turned = jnp.concatenate([real * cosine + imag * sine, imag * cosine - real * sine], axis=1)
            parts.append(turned.astype(jnp.bfloat16))
        return parts

    def second_stage(parts):
        both = dot(jnp.concatenate(parts, axis=0), second)
        cuts = [both[at : at + kept] for at in range(0, both.shape[0], kept)]
        return [(cut[:, :LANES], cut[:, LANES:]) for cut in cuts]

    def swapped(real, imag):
        return jnp.concatenate([imag, real], axis=1).astype(jnp.bfloat16)

    def last_stage(swapped_pairs):
        parts = []
        for imag, real in swapped_pairs:
            turned = jnp.concatenate([real * cosine - imag * sine, imag * cosine + real * sine], axis=0)
            parts.append(turned.astype(jnp.bfloat16))
        both = dot(last_ref[...], jnp.concatenate(parts, axis=1))
        return both[:rows] + both[rows:]

    taps_in = jnp.concatenate([part[2 * piece : 2 * piece + taps] for part in got], axis=0).astype(jnp.bfloat16)
    signal_in = jnp.concatenate([gather(group, 0) for group in range(groups)] + [taps_in], axis=1)
    grad_in = jnp.concatenate([gather(group, piece) for group in range(groups)], axis=1)
    signal_stage = first_stage(signal_in)
    grad_stage = first_stage(grad_in)
    forward = second_stage(turn_forward(signal_stage) + turn_forward(grad_stage))
    signals, (tap_real, tap_imag), grads = forward[:groups], forward[groups], forward[groups + 1 :]
    conv_parts = [swapped(r * tap_real - i * tap_imag, r * tap_imag + i * tap_real) for r, i in signals]
    back_parts = [swapped(tap_real * r + tap_imag * i, tap_real * i - tap_imag * r) for r, i in grads]
    corr_real = sum(sr * gr + si * gi for (sr, si), (gr, gi) in zip(signals, grads)) * scale
    corr_imag = sum(sr * gi - si * gr for (sr, si), (gr, gi) in zip(signals, grads)) * scale
    result = last_stage(second_stage(conv_parts + back_parts + [swapped(corr_real, corr_imag)]))
    for peer in range(peers):
        piece_rows = result[peer * piece : (peer + 1) * piece]
        for group in range(groups):
            cut = lambda sequence: piece_rows[:, sequence * LANES : (sequence + 1) * LANES]
            message = jnp.concatenate([cut(group), cut(groups + group), cut(count)], axis=0)
            out_ref[slots[peer * groups + group]] = message.astype(jnp.bfloat16)


def spectral_products(got, piece, groups, peers, scale):
    rows = peers * piece
    tables = dft_tables(rows)
    vmem = pl.BlockSpec(memory_space=pltpu.VMEM)
    return pl.pallas_call(
        functools.partial(spectral_kernel, groups, peers, scale),
        out_shape=jax.ShapeDtypeStruct((got.shape[0], 3 * piece, LANES), jnp.bfloat16),
        in_specs=[vmem] * 5,
        out_specs=vmem,
        compiler_params=pltpu.CompilerParams(vmem_limit_bytes=24 * 2**20),
        name="spectral_products",
    )(got, *[jnp.asarray(table) for table in tables])


def tile_rows(values):
    return values.reshape(values.shape[0], values.shape[1] // LANES, LANES)


def pack_kernel(
    groups,
    signal_hbm,
    gating_hbm,
    cotangent_hbm,
    filters_hbm,
    weight_hbm,
    message_ref,
    column_ref,
    signal_ref,
    gating_ref,
    cotangent_ref,
    taps_ref,
    weight_ref,
    sems,
):
    channels, length = signal_ref.shape
    share = length // groups
    start = pl.multiple_of(lax.axis_index("chan") * share, share)
    copies = [
        pltpu.make_async_copy(source, target, sems.at[at])
        for at, (source, target) in enumerate(
            [
                (cotangent_hbm, cotangent_ref),
                (gating_hbm, gating_ref),
                (signal_hbm, signal_ref),
                (filters_hbm.at[:, pl.ds(start, share)], taps_ref),
                (weight_hbm, weight_ref),
            ]
        )
    ]
    for copy in copies:
        copy.start()
    for copy in copies:
        copy.wait()
    signal = signal_ref[...].astype(jnp.float32)
    gated = cotangent_ref[...].astype(jnp.float32) * gating_ref[...].astype(jnp.float32)
    rows = tile_rows(jnp.concatenate([signal, gated, taps_ref[...]], axis=1))
    message_ref[...] = rows.reshape(message_ref.shape).astype(jnp.bfloat16)
    square = (channels, channels)
    diagonal = lax.broadcasted_iota(jnp.int32, square, 0) == lax.broadcasted_iota(jnp.int32, square, 1)
    weight = jnp.sum(jnp.where(diagonal, jnp.broadcast_to(weight_ref[...], square), 0.0), axis=1, keepdims=True)
    column_ref[...] = jnp.broadcast_to(weight, column_ref.shape)


def pack(signal, gating, cotangent, filters, skip_weight, groups):
    channels, length = signal.shape
    vmem = pl.BlockSpec(memory_space=pltpu.VMEM)
    operands = (signal, gating, cotangent, filters, skip_weight[None, :])
    return pl.pallas_call(
        functools.partial(pack_kernel, groups),
        out_shape=(
            jax.ShapeDtypeStruct((channels, (2 * length + length // groups) // (TILE * LANES), TILE, LANES), jnp.bfloat16),
            jax.ShapeDtypeStruct((channels, LANES), jnp.float32),
        ),
        in_specs=[pl.BlockSpec(memory_space=pltpu.HBM)] * 5,
        out_specs=(vmem, vmem),
        scratch_shapes=[pltpu.VMEM(signal.shape, jnp.bfloat16)] * 3
        + [
            pltpu.VMEM((filters.shape[0], length // groups), jnp.float32),
            pltpu.VMEM((1, channels), jnp.float32),
            pltpu.SemaphoreType.DMA((5,)),
        ],
        compiler_params=pltpu.CompilerParams(vmem_limit_bytes=16 * 2**20),
        name="pack",
    )(*[pltpu.with_memory_space_constraint(operand, pltpu.HBM) for operand in operands])


def finish_kernel(groups, home_ref, signal_ref, gating_ref, cotangent_ref, column_ref, signal_out, gating_out, filters_out):
    channels, length = signal_ref.shape
    piece = length // LANES
    share = channels // groups
    home = home_ref[...].astype(jnp.float32).reshape(channels, 3 * length)
    cotangent = cotangent_ref[...].astype(jnp.float32)
    gated = (cotangent * gating_ref[...].astype(jnp.float32)).astype(jnp.bfloat16).astype(jnp.float32)
    weight = column_ref[:, :1]
    outputs = home[:, :length] + weight * signal_ref[...].astype(jnp.float32)
    gating_out[...] = (cotangent * outputs).astype(jnp.bfloat16)
    signal_out[...] = (home[:, length : 2 * length] + weight * gated).astype(jnp.bfloat16)
    first = pl.multiple_of(lax.axis_index("chan") * share, share)
    corr = home_ref[pl.ds(first, share), 2 * piece :, :].astype(jnp.float32)
    filters_out[...] = corr.reshape(share, length)


def finish(home, signal, gating, cotangent, column, groups):
    channels, length = signal.shape
    vmem = pl.BlockSpec(memory_space=pltpu.VMEM)
    return pl.pallas_call(
        functools.partial(finish_kernel, groups),
        out_shape=(
            jax.ShapeDtypeStruct(signal.shape, jnp.bfloat16),
            jax.ShapeDtypeStruct(signal.shape, jnp.bfloat16),
            jax.ShapeDtypeStruct((channels // groups, length), jnp.float32),
        ),
        in_specs=[vmem] * 5,
        out_specs=(vmem,) * 3,
        compiler_params=pltpu.CompilerParams(vmem_limit_bytes=16 * 2**20),
        name="finish",
    )(home, signal, gating, cotangent, column)


def filter_per_device(signal, gating, cotangent, filters, skip_weight):
    peers = lax.axis_size("ctx")
    groups = lax.axis_size("chan")
    message, column = pack(signal, gating, cotangent, filters, skip_weight, groups)
    exchange = functools.partial(
        lax.all_to_all,
        axis_name=("ctx", "chan"),
        split_axis=0,
        concat_axis=0,
        axis_index_groups=[slot_order(peers, groups)],
        tiled=True,
    )
    got = exchange(message)
    scale = 1.0 / math.sqrt(signal.shape[1] * peers * groups)
    result = spectral_products(got, signal.shape[1] // LANES, groups, peers, scale)
    home = exchange(result)
    return finish(home, signal, gating, cotangent, column, groups)


def product(form, left, right):
    return jnp.einsum(
        form, left, right, precision=lax.Precision.HIGHEST, preferred_element_type=jnp.float32
    )


def phases(left_idx, right_idx, period):
    joined = left_idx[:, None] * right_idx[None, :] % period
    return joined.astype(jnp.float32) * (2.0 * math.pi / period)


def indices(total):
    return jnp.arange(total, dtype=jnp.int32)


def turn_forward(real_part, imag_part, angles):
    cosine = jnp.cos(angles)
    sine_part = jnp.sin(angles)
    return (real_part * cosine + imag_part * sine_part, imag_part * cosine - real_part * sine_part)


def turn_back(real_part, imag_part, angles):
    cosine = jnp.cos(angles)
    sine_part = jnp.sin(angles)
    return (real_part * cosine - imag_part * sine_part, imag_part * cosine + real_part * sine_part)


def first_pass(blocks, position, peer_count):
    height, length = blocks.shape
    piece_len = length // peer_count
    padded = 2 * peer_count * length
    shaped = blocks.reshape(height, peer_count, piece_len)
    angles = phases(indices(peer_count), indices(2 * peer_count), 2 * peer_count)
    real_part = product("rdm,dk->rmk", shaped, jnp.cos(angles))
    imag_part = -product("rdm,dk->rmk", shaped, jnp.sin(angles))
    offsets = position * piece_len + indices(piece_len)
    real_part, imag_part = turn_forward(
        real_part, imag_part, phases(offsets, indices(2 * peer_count), padded)
    )
    return jnp.stack([real_part, imag_part])


def second_pass(columns, peer_count):
    height, piece_len = (columns.shape[1], columns.shape[2])
    length = piece_len * peer_count
    real_part = columns[0].reshape(height, piece_len, peer_count, 2)
    imag_part = columns[1].reshape(height, piece_len, peer_count, 2)
    angles = phases(indices(peer_count), indices(peer_count), peer_count)
    cosine = jnp.cos(angles)
    sine_part = jnp.sin(angles)
    real_one = product("rmeb,ea->rbma", real_part, cosine) + product(
        "rmeb,ea->rbma", imag_part, sine_part
    )
    imag_one = product("rmeb,ea->rbma", imag_part, cosine) - product(
        "rmeb,ea->rbma", real_part, sine_part
    )
    real_one, imag_one = turn_forward(
        real_one, imag_one, phases(indices(piece_len), indices(peer_count), length)
    )
    angles = phases(indices(piece_len), indices(piece_len), piece_len)
    cosine = jnp.cos(angles)
    sine_part = jnp.sin(angles)
    real_two = product("rbma,mc->rbca", real_one, cosine) + product(
        "rbma,mc->rbca", imag_one, sine_part
    )
    imag_two = product("rbma,mc->rbca", imag_one, cosine) - product(
        "rbma,mc->rbca", real_one, sine_part
    )
    return jnp.stack([real_two.reshape(height, 2, length), imag_two.reshape(height, 2, length)])


def inverse_first(spectrum, position, peer_count):
    height, length = (spectrum.shape[1], spectrum.shape[3])
    piece_len = length // peer_count
    padded = 2 * peer_count * length
    real_part = spectrum[0].reshape(height, 2, piece_len, peer_count)
    imag_part = spectrum[1].reshape(height, 2, piece_len, peer_count)
    angles = phases(indices(piece_len), indices(piece_len), piece_len)
    cosine = jnp.cos(angles)
    sine_part = jnp.sin(angles)
    real_one = product("rbca,cm->rbma", real_part, cosine) - product(
        "rbca,cm->rbma", imag_part, sine_part
    )
    imag_one = product("rbca,cm->rbma", imag_part, cosine) + product(
        "rbca,cm->rbma", real_part, sine_part
    )
    real_one, imag_one = turn_back(
        real_one, imag_one, phases(indices(piece_len), indices(peer_count), length)
    )
    angles = phases(indices(peer_count), indices(peer_count), peer_count)
    cosine = jnp.cos(angles)
    sine_part = jnp.sin(angles)
    real_two = product("rbma,ae->rmeb", real_one, cosine) - product(
        "rbma,ae->rmeb", imag_one, sine_part
    )
    imag_two = product("rbma,ae->rmeb", imag_one, cosine) + product(
        "rbma,ae->rmeb", real_one, sine_part
    )
    offsets = (indices(peer_count)[None, :] * piece_len + indices(piece_len)[:, None]).reshape(-1)
    freq_bins = 2 * position + indices(2)
    angles = phases(offsets, freq_bins, padded).reshape(piece_len, peer_count, 2)
    real_two, imag_two = turn_back(real_two, imag_two, angles)
    return jnp.stack(
        [
            real_two.reshape(height, piece_len, 2 * peer_count),
            imag_two.reshape(height, piece_len, 2 * peer_count),
        ]
    )


def inverse_second(received, peer_count):
    height, piece_len = (received.shape[1], received.shape[2])
    length = piece_len * peer_count
    padded = 2 * peer_count * length
    angles = phases(indices(2 * peer_count), indices(peer_count), 2 * peer_count)
    signal_out = product("rmk,kd->rdm", received[0], jnp.cos(angles)) - product(
        "rmk,kd->rdm", received[1], jnp.sin(angles)
    )
    return (signal_out / padded).reshape(height, length)


def split_transforms(signal, gating, cotangent, filters, skip_weight):
    peer_count = lax.axis_size("ctx")
    position = lax.axis_index("ctx")
    channels, length = signal.shape
    count_filters = filters.shape[0]
    local_group = channels // count_filters
    gated_grad = (cotangent.astype(jnp.float32) * gating.astype(jnp.float32)).astype(jnp.bfloat16)
    signal_blocks, gated_blocks = (
        lax.all_to_all(signal, "ctx", split_axis=1, concat_axis=1, tiled=True),
        lax.all_to_all(gated_grad, "ctx", split_axis=1, concat_axis=1, tiled=True),
    )
    tap_blocks = lax.all_to_all(filters, "ctx", split_axis=1, concat_axis=1, tiled=True)
    signal_cols, gated_cols, tap_cols = (
        lax.all_to_all(
            first_pass(signal_blocks.astype(jnp.float32), position, peer_count),
            "ctx",
            split_axis=3,
            concat_axis=3,
            tiled=True,
        ),
        lax.all_to_all(
            first_pass(gated_blocks.astype(jnp.float32), position, peer_count),
            "ctx",
            split_axis=3,
            concat_axis=3,
            tiled=True,
        ),
        lax.all_to_all(
            first_pass(tap_blocks, position, peer_count),
            "ctx",
            split_axis=3,
            concat_axis=3,
            tiled=True,
        ),
    )
    signal_spec = second_pass(signal_cols, peer_count).reshape(
        2, local_group, count_filters, 2, length
    )
    gated_spec = second_pass(gated_cols, peer_count).reshape(
        2, local_group, count_filters, 2, length
    )
    tap_spec = second_pass(tap_cols, peer_count)
    tap_real, tap_imag = (tap_spec[0], tap_spec[1])
    sig_real, sig_imag = (signal_spec[0], signal_spec[1])
    gated_real, gated_imag = (gated_spec[0], gated_spec[1])
    forward_spec = jnp.stack(
        [sig_real * tap_real - sig_imag * tap_imag, sig_real * tap_imag + sig_imag * tap_real]
    ).reshape(2, channels, 2, length)
    back_spec = jnp.stack(
        [
            tap_real * gated_real + tap_imag * gated_imag,
            tap_real * gated_imag - tap_imag * gated_real,
        ]
    ).reshape(2, channels, 2, length)
    corr_spec = jnp.stack(
        [
            jnp.sum(sig_real * gated_real + sig_imag * gated_imag, axis=0),
            jnp.sum(sig_real * gated_imag - sig_imag * gated_real, axis=0),
        ]
    )
    forward_cols, back_cols, corr_cols = (
        lax.all_to_all(
            inverse_first(forward_spec, position, peer_count),
            "ctx",
            split_axis=3,
            concat_axis=3,
            tiled=True,
        ),
        lax.all_to_all(
            inverse_first(back_spec, position, peer_count),
            "ctx",
            split_axis=3,
            concat_axis=3,
            tiled=True,
        ),
        lax.all_to_all(
            inverse_first(corr_spec, position, peer_count),
            "ctx",
            split_axis=3,
            concat_axis=3,
            tiled=True,
        ),
    )
    conv_time, back_time, corr_time = (
        lax.all_to_all(
            inverse_second(forward_cols, peer_count), "ctx", split_axis=1, concat_axis=1, tiled=True
        ),
        lax.all_to_all(
            inverse_second(back_cols, peer_count), "ctx", split_axis=1, concat_axis=1, tiled=True
        ),
        lax.all_to_all(
            inverse_second(corr_cols, peer_count), "ctx", split_axis=1, concat_axis=1, tiled=True
        ),
    )
    corr_time = lax.psum_scatter(corr_time, "chan", scatter_dimension=0, tiled=True)
    weight = skip_weight[:, None]
    outputs = conv_time + weight * signal.astype(jnp.float32)
    grad_gating = (cotangent.astype(jnp.float32) * outputs).astype(jnp.bfloat16)
    grad_signal = (back_time + weight * gated_grad.astype(jnp.float32)).astype(jnp.bfloat16)
    normal_scale = 1.0 / math.sqrt(length * peer_count * local_group * lax.axis_size("chan"))
    grad_filters = corr_time * normal_scale
    return (grad_signal, grad_gating, grad_filters)


def per_device(signal, gating, cotangent, filters, skip_weight):
    peers, groups = lax.axis_size("ctx"), lax.axis_size("chan")
    channels, length = signal.shape
    one_each = channels == filters.shape[0] == peers * groups
    piece = length // LANES
    whole_tiles = length % (8 * LANES) == 0 and piece % groups == 0
    if one_each and whole_tiles and (peers * piece) % 16 == 0 and (piece // groups) % TILE == 0:
        return filter_per_device(signal, gating, cotangent, filters, skip_weight)
    return split_transforms(signal, gating, cotangent, filters, skip_weight)


def solution(mesh):
    in_specs = (P("chan", "ctx"), P("chan", "ctx"), P("chan", "ctx"), P(None, "ctx"), P("chan"))
    out_specs = (P("chan", "ctx"), P("chan", "ctx"), P("chan", "ctx"))
    return jax.shard_map(
        per_device, mesh=mesh, in_specs=in_specs, out_specs=out_specs, check_vma=False
    )
```

```python
import functools
import math

import jax
import jax.numpy as jnp
import numpy as np
from jax import lax
from jax.experimental import pallas as pl
from jax.experimental.pallas import tpu as pltpu
from jax.sharding import PartitionSpec as P

LANES = 128
TILE = 2


def split_table(table):
    high = table.astype(jnp.bfloat16)
    low = (table - high.astype(np.float64)).astype(jnp.bfloat16)
    return high, low


def dft_tables(rows):
    height = 2 * rows
    padded = height * LANES
    k1 = np.arange(rows)
    n1 = np.arange(rows)
    n2 = np.arange(LANES)
    outer = np.pi * (np.outer(2 * k1 + 1, n1) % (2 * height)) / height
    high, low = split_table(np.concatenate([np.cos(outer), -np.sin(outer)], axis=0))
    first = np.concatenate([high, low], axis=1)
    turn = np.pi * (np.outer(2 * k1 + 1, n2) % (2 * padded)) / padded
    twiddle = np.stack([np.cos(turn), np.sin(turn)]).astype(np.float32)
    inner = 2.0 * np.pi * (np.outer(n2, n2) % LANES) / LANES
    cosine, sine = np.cos(inner), np.sin(inner)
    second = np.block([[cosine, -sine], [sine, cosine]]).astype(jnp.bfloat16)
    high, low = split_table(np.concatenate([np.cos(outer.T), -np.sin(outer.T)], axis=1) * (2.0 / padded))
    last = np.concatenate([high, low], axis=0)
    return first, twiddle, second, last


def dot(left, right):
    return jnp.dot(left, right, preferred_element_type=jnp.float32)


def slot_order(peers, groups):
    if peers % 2 or groups % 2:
        return list(range(peers * groups))
    return [
        (high * 2 + low) * groups + (plane * 2 + core)
        for plane in range(groups // 2)
        for low in reversed(range(2))
        for high in reversed(range(peers // 2))
        for core in range(2)
    ]


def spectral_kernel(
    groups, peers, scale, got_ref, first_ref, twiddle_ref, second_ref, last_ref, out_ref
):
    piece = out_ref.shape[1] // 3
    taps = piece // groups
    rows = peers * piece
    kept = twiddle_ref.shape[1]
    count = 2 * groups
    order = slot_order(peers, groups)
    slots = [order.index(device) for device in range(peers * groups)]
    got = got_ref[...].astype(jnp.float32).reshape(peers * groups, -1, LANES)
    got = [got[slot] for slot in slots]

    def gather(group, start):
        parts = [got[peer * groups + group][start : start + piece] for peer in range(peers)]
        return jnp.concatenate(parts, axis=0).astype(jnp.bfloat16)

    cosine, sine = twiddle_ref[0], twiddle_ref[1]
    second = second_ref[...]

    def first_stage(values):
        return dot(first_ref[...], jnp.concatenate([values, values], axis=0))

    def turn_forward(stage):
        parts = []
        for at in range(0, stage.shape[1], LANES):
            real, imag = stage[:kept, at : at + LANES], stage[kept:, at : at + LANES]
            turned = jnp.concatenate([real * cosine + imag * sine, imag * cosine - real * sine], axis=1)
            parts.append(turned.astype(jnp.bfloat16))
        return parts

    def second_stage(parts):
        both = dot(jnp.concatenate(parts, axis=0), second)
        cuts = [both[at : at + kept] for at in range(0, both.shape[0], kept)]
        return [(cut[:, :LANES], cut[:, LANES:]) for cut in cuts]

    def swapped(real, imag):
        return jnp.concatenate([imag, real], axis=1).astype(jnp.bfloat16)

    def last_stage(swapped_pairs):
        parts = []
        for imag, real in swapped_pairs:
            turned = jnp.concatenate([real * cosine - imag * sine, imag * cosine + real * sine], axis=0)
            parts.append(turned.astype(jnp.bfloat16))
        both = dot(last_ref[...], jnp.concatenate(parts, axis=1))
        return both[:rows] + both[rows:]

    taps_in = jnp.concatenate([part[2 * piece : 2 * piece + taps] for part in got], axis=0).astype(jnp.bfloat16)
    signal_in = jnp.concatenate([gather(group, 0) for group in range(groups)] + [taps_in], axis=1)
    grad_in = jnp.concatenate([gather(group, piece) for group in range(groups)], axis=1)
    signal_stage = first_stage(signal_in)
    grad_stage = first_stage(grad_in)
    forward = second_stage(turn_forward(signal_stage) + turn_forward(grad_stage))
    signals, (tap_real, tap_imag), grads = forward[:groups], forward[groups], forward[groups + 1 :]
    conv_parts = [swapped(r * tap_real - i * tap_imag, r * tap_imag + i * tap_real) for r, i in signals]
    back_parts = [swapped(tap_real * r + tap_imag * i, tap_real * i - tap_imag * r) for r, i in grads]
    corr_real = sum(sr * gr + si * gi for (sr, si), (gr, gi) in zip(signals, grads)) * scale
    corr_imag = sum(sr * gi - si * gr for (sr, si), (gr, gi) in zip(signals, grads)) * scale
    result = last_stage(second_stage(conv_parts + back_parts + [swapped(corr_real, corr_imag)]))
    for peer in range(peers):
        piece_rows = result[peer * piece : (peer + 1) * piece]
        for group in range(groups):
            cut = lambda sequence: piece_rows[:, sequence * LANES : (sequence + 1) * LANES]
            message = jnp.concatenate([cut(group), cut(groups + group), cut(count)], axis=0)
            out_ref[slots[peer * groups + group]] = message.astype(jnp.bfloat16)


def spectral_products(got, piece, groups, peers, scale):
    rows = peers * piece
    tables = dft_tables(rows)
    vmem = pl.BlockSpec(memory_space=pltpu.VMEM)
    return pl.pallas_call(
        functools.partial(spectral_kernel, groups, peers, scale),
        out_shape=jax.ShapeDtypeStruct((got.shape[0], 3 * piece, LANES), jnp.bfloat16),
        in_specs=[vmem] * 5,
        out_specs=vmem,
        compiler_params=pltpu.CompilerParams(vmem_limit_bytes=24 * 2**20),
        name="spectral_products",
    )(got, *[jnp.asarray(table) for table in tables])


def tile_rows(values):
    return values.reshape(values.shape[0], values.shape[1] // LANES, LANES)


def pack_kernel(
    groups,
    signal_hbm,
    gating_hbm,
    cotangent_hbm,
    filters_hbm,
    weight_hbm,
    message_ref,
    column_ref,
    signal_ref,
    gating_ref,
    cotangent_ref,
    taps_ref,
    weight_ref,
    sems,
):
    channels, length = signal_ref.shape
    share = length // groups
    start = pl.multiple_of(lax.axis_index("chan") * share, share)
    copies = [
        pltpu.make_async_copy(source, target, sems.at[at])
        for at, (source, target) in enumerate(
            [
                (cotangent_hbm, cotangent_ref),
                (gating_hbm, gating_ref),
                (signal_hbm, signal_ref),
                (filters_hbm.at[:, pl.ds(start, share)], taps_ref),
                (weight_hbm, weight_ref),
            ]
        )
    ]
    for copy in copies:
        copy.start()
    for copy in copies:
        copy.wait()
    signal = signal_ref[...].astype(jnp.float32)
    gated = cotangent_ref[...].astype(jnp.float32) * gating_ref[...].astype(jnp.float32)
    rows = tile_rows(jnp.concatenate([signal, gated, taps_ref[...]], axis=1))
    message_ref[...] = rows.reshape(message_ref.shape).astype(jnp.bfloat16)
    square = (channels, channels)
    diagonal = lax.broadcasted_iota(jnp.int32, square, 0) == lax.broadcasted_iota(jnp.int32, square, 1)
    weight = jnp.sum(jnp.where(diagonal, jnp.broadcast_to(weight_ref[...], square), 0.0), axis=1, keepdims=True)
    column_ref[...] = jnp.broadcast_to(weight, column_ref.shape)


def pack(signal, gating, cotangent, filters, skip_weight, groups):
    channels, length = signal.shape
    vmem = pl.BlockSpec(memory_space=pltpu.VMEM)
    operands = (signal, gating, cotangent, filters, skip_weight[None, :])
    return pl.pallas_call(
        functools.partial(pack_kernel, groups),
        out_shape=(
            jax.ShapeDtypeStruct((channels, (2 * length + length // groups) // (TILE * LANES), TILE, LANES), jnp.bfloat16),
            jax.ShapeDtypeStruct((channels, LANES), jnp.float32),
        ),
        in_specs=[pl.BlockSpec(memory_space=pltpu.HBM)] * 5,
        out_specs=(vmem, vmem),
        scratch_shapes=[pltpu.VMEM(signal.shape, jnp.bfloat16)] * 3
        + [
            pltpu.VMEM((filters.shape[0], length // groups), jnp.float32),
            pltpu.VMEM((1, channels), jnp.float32),
            pltpu.SemaphoreType.DMA((5,)),
        ],
        compiler_params=pltpu.CompilerParams(vmem_limit_bytes=16 * 2**20),
        name="pack",
    )(*[pltpu.with_memory_space_constraint(operand, pltpu.HBM) for operand in operands])


def finish_kernel(groups, home_ref, signal_ref, gating_ref, cotangent_ref, column_ref, signal_out, gating_out, filters_out):
    channels, length = signal_ref.shape
    piece = length // LANES
    share = channels // groups
    home = home_ref[...].astype(jnp.float32).reshape(channels, 3 * length)
    cotangent = cotangent_ref[...].astype(jnp.float32)
    gated = (cotangent * gating_ref[...].astype(jnp.float32)).astype(jnp.bfloat16).astype(jnp.float32)
    weight = column_ref[:, :1]
    outputs = home[:, :length] + weight * signal_ref[...].astype(jnp.float32)
    gating_out[...] = (cotangent * outputs).astype(jnp.bfloat16)
    signal_out[...] = (home[:, length : 2 * length] + weight * gated).astype(jnp.bfloat16)
    first = pl.multiple_of(lax.axis_index("chan") * share, share)
    corr = home_ref[pl.ds(first, share), 2 * piece :, :].astype(jnp.float32)
    filters_out[...] = corr.reshape(share, length)


def finish(home, signal, gating, cotangent, column, groups):
    channels, length = signal.shape
    vmem = pl.BlockSpec(memory_space=pltpu.VMEM)
    return pl.pallas_call(
        functools.partial(finish_kernel, groups),
        out_shape=(
            jax.ShapeDtypeStruct(signal.shape, jnp.bfloat16),
            jax.ShapeDtypeStruct(signal.shape, jnp.bfloat16),
            jax.ShapeDtypeStruct((channels // groups, length), jnp.float32),
        ),
        in_specs=[vmem] * 5,
        out_specs=(vmem,) * 3,
        compiler_params=pltpu.CompilerParams(vmem_limit_bytes=16 * 2**20),
        name="finish",
    )(home, signal, gating, cotangent, column)


def filter_per_device(signal, gating, cotangent, filters, skip_weight):
    peers = lax.axis_size("ctx")
    groups = lax.axis_size("chan")
    message, column = pack(signal, gating, cotangent, filters, skip_weight, groups)
    exchange = functools.partial(
        lax.all_to_all,
        axis_name=("ctx", "chan"),
        split_axis=0,
        concat_axis=0,
        axis_index_groups=[slot_order(peers, groups)],
        tiled=True,
    )
    got = exchange(message)
    scale = 1.0 / math.sqrt(signal.shape[1] * peers * groups)
    result = spectral_products(got, signal.shape[1] // LANES, groups, peers, scale)
    home = exchange(result)
    return finish(home, signal, gating, cotangent, column, groups)


def product(form, left, right):
    return jnp.einsum(
        form, left, right, precision=lax.Precision.HIGHEST, preferred_element_type=jnp.float32
    )


def phases(left_idx, right_idx, period):
    joined = left_idx[:, None] * right_idx[None, :] % period
    return joined.astype(jnp.float32) * (2.0 * math.pi / period)


def indices(total):
    return jnp.arange(total, dtype=jnp.int32)


def turn_forward(real_part, imag_part, angles):
    cosine = jnp.cos(angles)
    sine_part = jnp.sin(angles)
    return (real_part * cosine + imag_part * sine_part, imag_part * cosine - real_part * sine_part)


def turn_back(real_part, imag_part, angles):
    cosine = jnp.cos(angles)
    sine_part = jnp.sin(angles)
    return (real_part * cosine - imag_part * sine_part, imag_part * cosine + real_part * sine_part)


def first_pass(blocks, position, peer_count):
    height, length = blocks.shape
    piece_len = length // peer_count
    padded = 2 * peer_count * length
    shaped = blocks.reshape(height, peer_count, piece_len)
    angles = phases(indices(peer_count), indices(2 * peer_count), 2 * peer_count)
    real_part = product("rdm,dk->rmk", shaped, jnp.cos(angles))
    imag_part = -product("rdm,dk->rmk", shaped, jnp.sin(angles))
    offsets = position * piece_len + indices(piece_len)
    real_part, imag_part = turn_forward(
        real_part, imag_part, phases(offsets, indices(2 * peer_count), padded)
    )
    return jnp.stack([real_part, imag_part])


def second_pass(columns, peer_count):
    height, piece_len = (columns.shape[1], columns.shape[2])
    length = piece_len * peer_count
    real_part = columns[0].reshape(height, piece_len, peer_count, 2)
    imag_part = columns[1].reshape(height, piece_len, peer_count, 2)
    angles = phases(indices(peer_count), indices(peer_count), peer_count)
    cosine = jnp.cos(angles)
    sine_part = jnp.sin(angles)
    real_one = product("rmeb,ea->rbma", real_part, cosine) + product(
        "rmeb,ea->rbma", imag_part, sine_part
    )
    imag_one = product("rmeb,ea->rbma", imag_part, cosine) - product(
        "rmeb,ea->rbma", real_part, sine_part
    )
    real_one, imag_one = turn_forward(
        real_one, imag_one, phases(indices(piece_len), indices(peer_count), length)
    )
    angles = phases(indices(piece_len), indices(piece_len), piece_len)
    cosine = jnp.cos(angles)
    sine_part = jnp.sin(angles)
    real_two = product("rbma,mc->rbca", real_one, cosine) + product(
        "rbma,mc->rbca", imag_one, sine_part
    )
    imag_two = product("rbma,mc->rbca", imag_one, cosine) - product(
        "rbma,mc->rbca", real_one, sine_part
    )
    return jnp.stack([real_two.reshape(height, 2, length), imag_two.reshape(height, 2, length)])


def inverse_first(spectrum, position, peer_count):
    height, length = (spectrum.shape[1], spectrum.shape[3])
    piece_len = length // peer_count
    padded = 2 * peer_count * length
    real_part = spectrum[0].reshape(height, 2, piece_len, peer_count)
    imag_part = spectrum[1].reshape(height, 2, piece_len, peer_count)
    angles = phases(indices(piece_len), indices(piece_len), piece_len)
    cosine = jnp.cos(angles)
    sine_part = jnp.sin(angles)
    real_one = product("rbca,cm->rbma", real_part, cosine) - product(
        "rbca,cm->rbma", imag_part, sine_part
    )
    imag_one = product("rbca,cm->rbma", imag_part, cosine) + product(
        "rbca,cm->rbma", real_part, sine_part
    )
    real_one, imag_one = turn_back(
        real_one, imag_one, phases(indices(piece_len), indices(peer_count), length)
    )
    angles = phases(indices(peer_count), indices(peer_count), peer_count)
    cosine = jnp.cos(angles)
    sine_part = jnp.sin(angles)
    real_two = product("rbma,ae->rmeb", real_one, cosine) - product(
        "rbma,ae->rmeb", imag_one, sine_part
    )
    imag_two = product("rbma,ae->rmeb", imag_one, cosine) + product(
        "rbma,ae->rmeb", real_one, sine_part
    )
    offsets = (indices(peer_count)[None, :] * piece_len + indices(piece_len)[:, None]).reshape(-1)
    freq_bins = 2 * position + indices(2)
    angles = phases(offsets, freq_bins, padded).reshape(piece_len, peer_count, 2)
    real_two, imag_two = turn_back(real_two, imag_two, angles)
    return jnp.stack(
        [
            real_two.reshape(height, piece_len, 2 * peer_count),
            imag_two.reshape(height, piece_len, 2 * peer_count),
        ]
    )


def inverse_second(received, peer_count):
    height, piece_len = (received.shape[1], received.shape[2])
    length = piece_len * peer_count
    padded = 2 * peer_count * length
    angles = phases(indices(2 * peer_count), indices(peer_count), 2 * peer_count)
    signal_out = product("rmk,kd->rdm", received[0], jnp.cos(angles)) - product(
        "rmk,kd->rdm", received[1], jnp.sin(angles)
    )
    return (signal_out / padded).reshape(height, length)


def split_transforms(signal, gating, cotangent, filters, skip_weight):
    peer_count = lax.axis_size("ctx")
    position = lax.axis_index("ctx")
    channels, length = signal.shape
    count_filters = filters.shape[0]
    local_group = channels // count_filters
    gated_grad = (cotangent.astype(jnp.float32) * gating.astype(jnp.float32)).astype(jnp.bfloat16)
    signal_blocks, gated_blocks = (
        lax.all_to_all(signal, "ctx", split_axis=1, concat_axis=1, tiled=True),
        lax.all_to_all(gated_grad, "ctx", split_axis=1, concat_axis=1, tiled=True),
    )
    tap_blocks = lax.all_to_all(filters, "ctx", split_axis=1, concat_axis=1, tiled=True)
    signal_cols, gated_cols, tap_cols = (
        lax.all_to_all(
            first_pass(signal_blocks.astype(jnp.float32), position, peer_count),
            "ctx",
            split_axis=3,
            concat_axis=3,
            tiled=True,
        ),
        lax.all_to_all(
            first_pass(gated_blocks.astype(jnp.float32), position, peer_count),
            "ctx",
            split_axis=3,
            concat_axis=3,
            tiled=True,
        ),
        lax.all_to_all(
            first_pass(tap_blocks, position, peer_count),
            "ctx",
            split_axis=3,
            concat_axis=3,
            tiled=True,
        ),
    )
    signal_spec = second_pass(signal_cols, peer_count).reshape(
        2, local_group, count_filters, 2, length
    )
    gated_spec = second_pass(gated_cols, peer_count).reshape(
        2, local_group, count_filters, 2, length
    )
    tap_spec = second_pass(tap_cols, peer_count)
    tap_real, tap_imag = (tap_spec[0], tap_spec[1])
    sig_real, sig_imag = (signal_spec[0], signal_spec[1])
    gated_real, gated_imag = (gated_spec[0], gated_spec[1])
    forward_spec = jnp.stack(
        [sig_real * tap_real - sig_imag * tap_imag, sig_real * tap_imag + sig_imag * tap_real]
    ).reshape(2, channels, 2, length)
    back_spec = jnp.stack(
        [
            tap_real * gated_real + tap_imag * gated_imag,
            tap_real * gated_imag - tap_imag * gated_real,
        ]
    ).reshape(2, channels, 2, length)
    corr_spec = jnp.stack(
        [
            jnp.sum(sig_real * gated_real + sig_imag * gated_imag, axis=0),
            jnp.sum(sig_real * gated_imag - sig_imag * gated_real, axis=0),
        ]
    )
    forward_cols, back_cols, corr_cols = (
        lax.all_to_all(
            inverse_first(forward_spec, position, peer_count),
            "ctx",
            split_axis=3,
            concat_axis=3,
            tiled=True,
        ),
        lax.all_to_all(
            inverse_first(back_spec, position, peer_count),
            "ctx",
            split_axis=3,
            concat_axis=3,
            tiled=True,
        ),
        lax.all_to_all(
            inverse_first(corr_spec, position, peer_count),
            "ctx",
            split_axis=3,
            concat_axis=3,
            tiled=True,
        ),
    )
    conv_time, back_time, corr_time = (
        lax.all_to_all(
            inverse_second(forward_cols, peer_count), "ctx", split_axis=1, concat_axis=1, tiled=True
        ),
        lax.all_to_all(
            inverse_second(back_cols, peer_count), "ctx", split_axis=1, concat_axis=1, tiled=True
        ),
        lax.all_to_all(
            inverse_second(corr_cols, peer_count), "ctx", split_axis=1, concat_axis=1, tiled=True
        ),
    )
    corr_time = lax.psum_scatter(corr_time, "chan", scatter_dimension=0, tiled=True)
    weight = skip_weight[:, None]
    outputs = conv_time + weight * signal.astype(jnp.float32)
    grad_gating = (cotangent.astype(jnp.float32) * outputs).astype(jnp.bfloat16)
    grad_signal = (back_time + weight * gated_grad.astype(jnp.float32)).astype(jnp.bfloat16)
    normal_scale = 1.0 / math.sqrt(length * peer_count * local_group * lax.axis_size("chan"))
    grad_filters = corr_time * normal_scale
    return (grad_signal, grad_gating, grad_filters)


def per_device(signal, gating, cotangent, filters, skip_weight):
    peers, groups = lax.axis_size("ctx"), lax.axis_size("chan")
    channels, length = signal.shape
    one_each = channels == filters.shape[0] == peers * groups
    piece = length // LANES
    whole_tiles = length % (8 * LANES) == 0 and piece % groups == 0
    if one_each and whole_tiles and (peers * piece) % 16 == 0 and (piece // groups) % TILE == 0:
        return filter_per_device(signal, gating, cotangent, filters, skip_weight)
    return split_transforms(signal, gating, cotangent, filters, skip_weight)


def solution(mesh):
    in_specs = (P("chan", "ctx"), P("chan", "ctx"), P("chan", "ctx"), P(None, "ctx"), P("chan"))
    out_specs = (P("chan", "ctx"), P("chan", "ctx"), P("chan", "ctx"))
    return jax.shard_map(
        per_device, mesh=mesh, in_specs=in_specs, out_specs=out_specs, check_vma=False
    )
```

```python
import functools
import math

import jax
import jax.numpy as jnp
import numpy as np
from jax import lax
from jax.experimental import pallas as pl
from jax.experimental.pallas import tpu as pltpu
from jax.sharding import PartitionSpec as P

LANES = 128
TILE = 2


def split_table(table):
    high = table.astype(jnp.bfloat16)
    low = (table - high.astype(np.float64)).astype(jnp.bfloat16)
    return high, low


def dft_tables(rows):
    height = 2 * rows
    padded = height * LANES
    k1 = np.arange(rows)
    n1 = np.arange(rows)
    n2 = np.arange(LANES)
    outer = np.pi * (np.outer(2 * k1 + 1, n1) % (2 * height)) / height
    high, low = split_table(np.concatenate([np.cos(outer), -np.sin(outer)], axis=0))
    first = np.concatenate([high, low], axis=1)
    turn = np.pi * (np.outer(2 * k1 + 1, n2) % (2 * padded)) / padded
    twiddle = np.stack([np.cos(turn), np.sin(turn)]).astype(np.float32)
    inner = 2.0 * np.pi * (np.outer(n2, n2) % LANES) / LANES
    cosine, sine = np.cos(inner), np.sin(inner)
    second = np.block([[cosine, -sine], [sine, cosine]]).astype(jnp.bfloat16)
    high, low = split_table(np.concatenate([np.cos(outer.T), -np.sin(outer.T)], axis=1) * (2.0 / padded))
    last = np.concatenate([high, low], axis=0)
    return first, twiddle, second, last


def dot(left, right):
    return jnp.dot(left, right, preferred_element_type=jnp.float32)


def slot_order(peers, groups):
    if peers % 2 or groups % 2:
        return list(range(peers * groups))
    return [
        (high * 2 + low) * groups + (plane * 2 + core)
        for plane in range(groups // 2)
        for low in range(2)
        for high in [0, *reversed(range(1, peers // 2))]
        for core in range(2)
    ]


def spectral_kernel(
    groups, peers, scale, got_ref, first_ref, twiddle_ref, second_ref, last_ref, out_ref
):
    piece = out_ref.shape[1] // 3
    taps = piece // groups
    rows = peers * piece
    kept = twiddle_ref.shape[1]
    count = 2 * groups
    order = slot_order(peers, groups)
    slots = [order.index(device) for device in range(peers * groups)]
    got = got_ref[...].astype(jnp.float32).reshape(peers * groups, -1, LANES)
    got = [got[slot] for slot in slots]

    def gather(group, start):
        parts = [got[peer * groups + group][start : start + piece] for peer in range(peers)]
        return jnp.concatenate(parts, axis=0).astype(jnp.bfloat16)

    cosine, sine = twiddle_ref[0], twiddle_ref[1]
    second = second_ref[...]

    def first_stage(values):
        return dot(first_ref[...], jnp.concatenate([values, values], axis=0))

    def turn_forward(stage):
        parts = []
        for at in range(0, stage.shape[1], LANES):
            real, imag = stage[:kept, at : at + LANES], stage[kept:, at : at + LANES]
            turned = jnp.concatenate([real * cosine + imag * sine, imag * cosine - real * sine], axis=1)
            parts.append(turned.astype(jnp.bfloat16))
        return parts

    def second_stage(parts):
        both = dot(jnp.concatenate(parts, axis=0), second)
        cuts = [both[at : at + kept] for at in range(0, both.shape[0], kept)]
        return [(cut[:, :LANES], cut[:, LANES:]) for cut in cuts]

    def swapped(real, imag):
        return jnp.concatenate([imag, real], axis=1).astype(jnp.bfloat16)

    def last_stage(swapped_pairs):
        parts = []
        for imag, real in swapped_pairs:
            turned = jnp.concatenate([real * cosine - imag * sine, imag * cosine + real * sine], axis=0)
            parts.append(turned.astype(jnp.bfloat16))
        both = dot(last_ref[...], jnp.concatenate(parts, axis=1))
        return both[:rows] + both[rows:]

    taps_in = jnp.concatenate([part[2 * piece : 2 * piece + taps] for part in got], axis=0).astype(jnp.bfloat16)
    signal_in = jnp.concatenate([gather(group, 0) for group in range(groups)] + [taps_in], axis=1)
    grad_in = jnp.concatenate([gather(group, piece) for group in range(groups)], axis=1)
    signal_stage = first_stage(signal_in)
    grad_stage = first_stage(grad_in)
    forward = second_stage(turn_forward(signal_stage) + turn_forward(grad_stage))
    signals, (tap_real, tap_imag), grads = forward[:groups], forward[groups], forward[groups + 1 :]
    conv_parts = [swapped(r * tap_real - i * tap_imag, r * tap_imag + i * tap_real) for r, i in signals]
    back_parts = [swapped(tap_real * r + tap_imag * i, tap_real * i - tap_imag * r) for r, i in grads]
    corr_real = sum(sr * gr + si * gi for (sr, si), (gr, gi) in zip(signals, grads)) * scale
    corr_imag = sum(sr * gi - si * gr for (sr, si), (gr, gi) in zip(signals, grads)) * scale
    result = last_stage(second_stage(conv_parts + back_parts + [swapped(corr_real, corr_imag)]))
    for peer in range(peers):
        piece_rows = result[peer * piece : (peer + 1) * piece]
        for group in range(groups):
            cut = lambda sequence: piece_rows[:, sequence * LANES : (sequence + 1) * LANES]
            message = jnp.concatenate([cut(group), cut(groups + group), cut(count)], axis=0)
            out_ref[slots[peer * groups + group]] = message.astype(jnp.bfloat16)


def spectral_products(got, piece, groups, peers, scale):
    rows = peers * piece
    tables = dft_tables(rows)
    vmem = pl.BlockSpec(memory_space=pltpu.VMEM)
    return pl.pallas_call(
        functools.partial(spectral_kernel, groups, peers, scale),
        out_shape=jax.ShapeDtypeStruct((got.shape[0], 3 * piece, LANES), jnp.bfloat16),
        in_specs=[vmem] * 5,
        out_specs=vmem,
        compiler_params=pltpu.CompilerParams(vmem_limit_bytes=24 * 2**20),
        name="spectral_products",
    )(got, *[jnp.asarray(table) for table in tables])


def tile_rows(values):
    return values.reshape(values.shape[0], values.shape[1] // LANES, LANES)


def pack_kernel(
    groups,
    signal_hbm,
    gating_hbm,
    cotangent_hbm,
    filters_hbm,
    weight_hbm,
    message_ref,
    column_ref,
    signal_ref,
    gating_ref,
    cotangent_ref,
    taps_ref,
    weight_ref,
    sems,
):
    channels, length = signal_ref.shape
    share = length // groups
    start = pl.multiple_of(lax.axis_index("chan") * share, share)
    copies = [
        pltpu.make_async_copy(source, target, sems.at[at])
        for at, (source, target) in enumerate(
            [
                (cotangent_hbm, cotangent_ref),
                (gating_hbm, gating_ref),
                (signal_hbm, signal_ref),
                (filters_hbm.at[:, pl.ds(start, share)], taps_ref),
                (weight_hbm, weight_ref),
            ]
        )
    ]
    for copy in copies:
        copy.start()
    for copy in copies:
        copy.wait()
    signal = signal_ref[...].astype(jnp.float32)
    gated = cotangent_ref[...].astype(jnp.float32) * gating_ref[...].astype(jnp.float32)
    rows = tile_rows(jnp.concatenate([signal, gated, taps_ref[...]], axis=1))
    message_ref[...] = rows.reshape(message_ref.shape).astype(jnp.bfloat16)
    square = (channels, channels)
    diagonal = lax.broadcasted_iota(jnp.int32, square, 0) == lax.broadcasted_iota(jnp.int32, square, 1)
    weight = jnp.sum(jnp.where(diagonal, jnp.broadcast_to(weight_ref[...], square), 0.0), axis=1, keepdims=True)
    column_ref[...] = jnp.broadcast_to(weight, column_ref.shape)


def pack(signal, gating, cotangent, filters, skip_weight, groups):
    channels, length = signal.shape
    vmem = pl.BlockSpec(memory_space=pltpu.VMEM)
    operands = (signal, gating, cotangent, filters, skip_weight[None, :])
    return pl.pallas_call(
        functools.partial(pack_kernel, groups),
        out_shape=(
            jax.ShapeDtypeStruct((channels, (2 * length + length // groups) // (TILE * LANES), TILE, LANES), jnp.bfloat16),
            jax.ShapeDtypeStruct((channels, LANES), jnp.float32),
        ),
        in_specs=[pl.BlockSpec(memory_space=pltpu.HBM)] * 5,
        out_specs=(vmem, vmem),
        scratch_shapes=[pltpu.VMEM(signal.shape, jnp.bfloat16)] * 3
        + [
            pltpu.VMEM((filters.shape[0], length // groups), jnp.float32),
            pltpu.VMEM((1, channels), jnp.float32),
            pltpu.SemaphoreType.DMA((5,)),
        ],
        compiler_params=pltpu.CompilerParams(vmem_limit_bytes=16 * 2**20),
        name="pack",
    )(*[pltpu.with_memory_space_constraint(operand, pltpu.HBM) for operand in operands])


def finish_kernel(groups, home_ref, signal_ref, gating_ref, cotangent_ref, column_ref, signal_out, gating_out, filters_out):
    channels, length = signal_ref.shape
    piece = length // LANES
    share = channels // groups
    home = home_ref[...].astype(jnp.float32).reshape(channels, 3 * length)
    cotangent = cotangent_ref[...].astype(jnp.float32)
    gated = (cotangent * gating_ref[...].astype(jnp.float32)).astype(jnp.bfloat16).astype(jnp.float32)
    weight = column_ref[:, :1]
    outputs = home[:, :length] + weight * signal_ref[...].astype(jnp.float32)
    gating_out[...] = (cotangent * outputs).astype(jnp.bfloat16)
    signal_out[...] = (home[:, length : 2 * length] + weight * gated).astype(jnp.bfloat16)
    first = pl.multiple_of(lax.axis_index("chan") * share, share)
    corr = home_ref[pl.ds(first, share), 2 * piece :, :].astype(jnp.float32)
    filters_out[...] = corr.reshape(share, length)


def finish(home, signal, gating, cotangent, column, groups):
    channels, length = signal.shape
    vmem = pl.BlockSpec(memory_space=pltpu.VMEM)
    return pl.pallas_call(
        functools.partial(finish_kernel, groups),
        out_shape=(
            jax.ShapeDtypeStruct(signal.shape, jnp.bfloat16),
            jax.ShapeDtypeStruct(signal.shape, jnp.bfloat16),
            jax.ShapeDtypeStruct((channels // groups, length), jnp.float32),
        ),
        in_specs=[vmem] * 5,
        out_specs=(vmem,) * 3,
        compiler_params=pltpu.CompilerParams(vmem_limit_bytes=16 * 2**20),
        name="finish",
    )(home, signal, gating, cotangent, column)


def filter_per_device(signal, gating, cotangent, filters, skip_weight):
    peers = lax.axis_size("ctx")
    groups = lax.axis_size("chan")
    message, column = pack(signal, gating, cotangent, filters, skip_weight, groups)
    exchange = functools.partial(
        lax.all_to_all,
        axis_name=("ctx", "chan"),
        split_axis=0,
        concat_axis=0,
        axis_index_groups=[slot_order(peers, groups)],
        tiled=True,
    )
    got = exchange(message)
    scale = 1.0 / math.sqrt(signal.shape[1] * peers * groups)
    result = spectral_products(got, signal.shape[1] // LANES, groups, peers, scale)
    home = exchange(result)
    return finish(home, signal, gating, cotangent, column, groups)


def product(form, left, right):
    return jnp.einsum(
        form, left, right, precision=lax.Precision.HIGHEST, preferred_element_type=jnp.float32
    )


def phases(left_idx, right_idx, period):
    joined = left_idx[:, None] * right_idx[None, :] % period
    return joined.astype(jnp.float32) * (2.0 * math.pi / period)


def indices(total):
    return jnp.arange(total, dtype=jnp.int32)


def turn_forward(real_part, imag_part, angles):
    cosine = jnp.cos(angles)
    sine_part = jnp.sin(angles)
    return (real_part * cosine + imag_part * sine_part, imag_part * cosine - real_part * sine_part)


def turn_back(real_part, imag_part, angles):
    cosine = jnp.cos(angles)
    sine_part = jnp.sin(angles)
    return (real_part * cosine - imag_part * sine_part, imag_part * cosine + real_part * sine_part)


def first_pass(blocks, position, peer_count):
    height, length = blocks.shape
    piece_len = length // peer_count
    padded = 2 * peer_count * length
    shaped = blocks.reshape(height, peer_count, piece_len)
    angles = phases(indices(peer_count), indices(2 * peer_count), 2 * peer_count)
    real_part = product("rdm,dk->rmk", shaped, jnp.cos(angles))
    imag_part = -product("rdm,dk->rmk", shaped, jnp.sin(angles))
    offsets = position * piece_len + indices(piece_len)
    real_part, imag_part = turn_forward(
        real_part, imag_part, phases(offsets, indices(2 * peer_count), padded)
    )
    return jnp.stack([real_part, imag_part])


def second_pass(columns, peer_count):
    height, piece_len = (columns.shape[1], columns.shape[2])
    length = piece_len * peer_count
    real_part = columns[0].reshape(height, piece_len, peer_count, 2)
    imag_part = columns[1].reshape(height, piece_len, peer_count, 2)
    angles = phases(indices(peer_count), indices(peer_count), peer_count)
    cosine = jnp.cos(angles)
    sine_part = jnp.sin(angles)
    real_one = product("rmeb,ea->rbma", real_part, cosine) + product(
        "rmeb,ea->rbma", imag_part, sine_part
    )
    imag_one = product("rmeb,ea->rbma", imag_part, cosine) - product(
        "rmeb,ea->rbma", real_part, sine_part
    )
    real_one, imag_one = turn_forward(
        real_one, imag_one, phases(indices(piece_len), indices(peer_count), length)
    )
    angles = phases(indices(piece_len), indices(piece_len), piece_len)
    cosine = jnp.cos(angles)
    sine_part = jnp.sin(angles)
    real_two = product("rbma,mc->rbca", real_one, cosine) + product(
        "rbma,mc->rbca", imag_one, sine_part
    )
    imag_two = product("rbma,mc->rbca", imag_one, cosine) - product(
        "rbma,mc->rbca", real_one, sine_part
    )
    return jnp.stack([real_two.reshape(height, 2, length), imag_two.reshape(height, 2, length)])


def inverse_first(spectrum, position, peer_count):
    height, length = (spectrum.shape[1], spectrum.shape[3])
    piece_len = length // peer_count
    padded = 2 * peer_count * length
    real_part = spectrum[0].reshape(height, 2, piece_len, peer_count)
    imag_part = spectrum[1].reshape(height, 2, piece_len, peer_count)
    angles = phases(indices(piece_len), indices(piece_len), piece_len)
    cosine = jnp.cos(angles)
    sine_part = jnp.sin(angles)
    real_one = product("rbca,cm->rbma", real_part, cosine) - product(
        "rbca,cm->rbma", imag_part, sine_part
    )
    imag_one = product("rbca,cm->rbma", imag_part, cosine) + product(
        "rbca,cm->rbma", real_part, sine_part
    )
    real_one, imag_one = turn_back(
        real_one, imag_one, phases(indices(piece_len), indices(peer_count), length)
    )
    angles = phases(indices(peer_count), indices(peer_count), peer_count)
    cosine = jnp.cos(angles)
    sine_part = jnp.sin(angles)
    real_two = product("rbma,ae->rmeb", real_one, cosine) - product(
        "rbma,ae->rmeb", imag_one, sine_part
    )
    imag_two = product("rbma,ae->rmeb", imag_one, cosine) + product(
        "rbma,ae->rmeb", real_one, sine_part
    )
    offsets = (indices(peer_count)[None, :] * piece_len + indices(piece_len)[:, None]).reshape(-1)
    freq_bins = 2 * position + indices(2)
    angles = phases(offsets, freq_bins, padded).reshape(piece_len, peer_count, 2)
    real_two, imag_two = turn_back(real_two, imag_two, angles)
    return jnp.stack(
        [
            real_two.reshape(height, piece_len, 2 * peer_count),
            imag_two.reshape(height, piece_len, 2 * peer_count),
        ]
    )


def inverse_second(received, peer_count):
    height, piece_len = (received.shape[1], received.shape[2])
    length = piece_len * peer_count
    padded = 2 * peer_count * length
    angles = phases(indices(2 * peer_count), indices(peer_count), 2 * peer_count)
    signal_out = product("rmk,kd->rdm", received[0], jnp.cos(angles)) - product(
        "rmk,kd->rdm", received[1], jnp.sin(angles)
    )
    return (signal_out / padded).reshape(height, length)


def split_transforms(signal, gating, cotangent, filters, skip_weight):
    peer_count = lax.axis_size("ctx")
    position = lax.axis_index("ctx")
    channels, length = signal.shape
    count_filters = filters.shape[0]
    local_group = channels // count_filters
    gated_grad = (cotangent.astype(jnp.float32) * gating.astype(jnp.float32)).astype(jnp.bfloat16)
    signal_blocks, gated_blocks = (
        lax.all_to_all(signal, "ctx", split_axis=1, concat_axis=1, tiled=True),
        lax.all_to_all(gated_grad, "ctx", split_axis=1, concat_axis=1, tiled=True),
    )
    tap_blocks = lax.all_to_all(filters, "ctx", split_axis=1, concat_axis=1, tiled=True)
    signal_cols, gated_cols, tap_cols = (
        lax.all_to_all(
            first_pass(signal_blocks.astype(jnp.float32), position, peer_count),
            "ctx",
            split_axis=3,
            concat_axis=3,
            tiled=True,
        ),
        lax.all_to_all(
            first_pass(gated_blocks.astype(jnp.float32), position, peer_count),
            "ctx",
            split_axis=3,
            concat_axis=3,
            tiled=True,
        ),
        lax.all_to_all(
            first_pass(tap_blocks, position, peer_count),
            "ctx",
            split_axis=3,
            concat_axis=3,
            tiled=True,
        ),
    )
    signal_spec = second_pass(signal_cols, peer_count).reshape(
        2, local_group, count_filters, 2, length
    )
    gated_spec = second_pass(gated_cols, peer_count).reshape(
        2, local_group, count_filters, 2, length
    )
    tap_spec = second_pass(tap_cols, peer_count)
    tap_real, tap_imag = (tap_spec[0], tap_spec[1])
    sig_real, sig_imag = (signal_spec[0], signal_spec[1])
    gated_real, gated_imag = (gated_spec[0], gated_spec[1])
    forward_spec = jnp.stack(
        [sig_real * tap_real - sig_imag * tap_imag, sig_real * tap_imag + sig_imag * tap_real]
    ).reshape(2, channels, 2, length)
    back_spec = jnp.stack(
        [
            tap_real * gated_real + tap_imag * gated_imag,
            tap_real * gated_imag - tap_imag * gated_real,
        ]
    ).reshape(2, channels, 2, length)
    corr_spec = jnp.stack(
        [
            jnp.sum(sig_real * gated_real + sig_imag * gated_imag, axis=0),
            jnp.sum(sig_real * gated_imag - sig_imag * gated_real, axis=0),
        ]
    )
    forward_cols, back_cols, corr_cols = (
        lax.all_to_all(
            inverse_first(forward_spec, position, peer_count),
            "ctx",
            split_axis=3,
            concat_axis=3,
            tiled=True,
        ),
        lax.all_to_all(
            inverse_first(back_spec, position, peer_count),
            "ctx",
            split_axis=3,
            concat_axis=3,
            tiled=True,
        ),
        lax.all_to_all(
            inverse_first(corr_spec, position, peer_count),
            "ctx",
            split_axis=3,
            concat_axis=3,
            tiled=True,
        ),
    )
    conv_time, back_time, corr_time = (
        lax.all_to_all(
            inverse_second(forward_cols, peer_count), "ctx", split_axis=1, concat_axis=1, tiled=True
        ),
        lax.all_to_all(
            inverse_second(back_cols, peer_count), "ctx", split_axis=1, concat_axis=1, tiled=True
        ),
        lax.all_to_all(
            inverse_second(corr_cols, peer_count), "ctx", split_axis=1, concat_axis=1, tiled=True
        ),
    )
    corr_time = lax.psum_scatter(corr_time, "chan", scatter_dimension=0, tiled=True)
    weight = skip_weight[:, None]
    outputs = conv_time + weight * signal.astype(jnp.float32)
    grad_gating = (cotangent.astype(jnp.float32) * outputs).astype(jnp.bfloat16)
    grad_signal = (back_time + weight * gated_grad.astype(jnp.float32)).astype(jnp.bfloat16)
    normal_scale = 1.0 / math.sqrt(length * peer_count * local_group * lax.axis_size("chan"))
    grad_filters = corr_time * normal_scale
    return (grad_signal, grad_gating, grad_filters)


def per_device(signal, gating, cotangent, filters, skip_weight):
    peers, groups = lax.axis_size("ctx"), lax.axis_size("chan")
    channels, length = signal.shape
    one_each = channels == filters.shape[0] == peers * groups
    piece = length // LANES
    whole_tiles = length % (8 * LANES) == 0 and piece % groups == 0
    if one_each and whole_tiles and (peers * piece) % 16 == 0 and (piece // groups) % TILE == 0:
        return filter_per_device(signal, gating, cotangent, filters, skip_weight)
    return split_transforms(signal, gating, cotangent, filters, skip_weight)


def solution(mesh):
    in_specs = (P("chan", "ctx"), P("chan", "ctx"), P("chan", "ctx"), P(None, "ctx"), P("chan"))
    out_specs = (P("chan", "ctx"), P("chan", "ctx"), P("chan", "ctx"))
    return jax.shard_map(
        per_device, mesh=mesh, in_specs=in_specs, out_specs=out_specs, check_vma=False
    )
```

```python
import functools
import math

import jax
import jax.numpy as jnp
import numpy as np
from jax import lax
from jax.experimental import pallas as pl
from jax.experimental.pallas import tpu as pltpu
from jax.sharding import PartitionSpec as P

LANES = 128
TILE = 2


def split_table(table):
    high = table.astype(jnp.bfloat16)
    low = (table - high.astype(np.float64)).astype(jnp.bfloat16)
    return high, low


def dft_tables(rows):
    height = 2 * rows
    padded = height * LANES
    k1 = np.arange(rows)
    n1 = np.arange(rows)
    n2 = np.arange(LANES)
    outer = np.pi * (np.outer(2 * k1 + 1, n1) % (2 * height)) / height
    high, low = split_table(np.concatenate([np.cos(outer), -np.sin(outer)], axis=0))
    first = np.concatenate([high, low], axis=1)
    turn = np.pi * (np.outer(2 * k1 + 1, n2) % (2 * padded)) / padded
    twiddle = np.stack([np.cos(turn), np.sin(turn)]).astype(np.float32)
    inner = 2.0 * np.pi * (np.outer(n2, n2) % LANES) / LANES
    cosine, sine = np.cos(inner), np.sin(inner)
    second = np.block([[cosine, -sine], [sine, cosine]]).astype(jnp.bfloat16)
    high, low = split_table(np.concatenate([np.cos(outer.T), -np.sin(outer.T)], axis=1) * (2.0 / padded))
    last = np.concatenate([high, low], axis=0)
    return first, twiddle, second, last


def dot(left, right):
    return jnp.dot(left, right, preferred_element_type=jnp.float32)


def slot_order(peers, groups):
    if peers % 2 or groups % 2:
        return list(range(peers * groups))
    return [
        (high * 2 + low) * groups + (plane * 2 + core)
        for plane in range(groups // 2)
        for low in range(2)
        for high in [0, *reversed(range(1, peers // 2))]
        for core in range(2)
    ]


def spectral_kernel(
    groups, peers, scale, got_ref, first_ref, twiddle_ref, second_ref, last_ref, out_ref
):
    piece = out_ref.shape[1] // 3
    taps = piece // groups
    rows = peers * piece
    kept = twiddle_ref.shape[1]
    count = 2 * groups
    order = slot_order(peers, groups)
    slots = [order.index(device) for device in range(peers * groups)]
    got = got_ref[...].astype(jnp.float32).reshape(peers * groups, -1, LANES)
    got = [got[slot] for slot in slots]

    def gather(group, start):
        parts = [got[peer * groups + group][start : start + piece] for peer in range(peers)]
        return jnp.concatenate(parts, axis=0).astype(jnp.bfloat16)

    cosine, sine = twiddle_ref[0], twiddle_ref[1]
    second = second_ref[...]

    def first_stage(values):
        return dot(first_ref[...], jnp.concatenate([values, values], axis=0))

    def turn_forward(stage):
        parts = []
        for at in range(0, stage.shape[1], LANES):
            real, imag = stage[:kept, at : at + LANES], stage[kept:, at : at + LANES]
            turned = jnp.concatenate([real * cosine + imag * sine, imag * cosine - real * sine], axis=1)
            parts.append(turned.astype(jnp.bfloat16))
        return parts

    def second_stage(parts):
        both = dot(jnp.concatenate(parts, axis=0), second)
        cuts = [both[at : at + kept] for at in range(0, both.shape[0], kept)]
        return [(cut[:, :LANES], cut[:, LANES:]) for cut in cuts]

    def swapped(real, imag):
        return jnp.concatenate([imag, real], axis=1).astype(jnp.bfloat16)

    def last_stage(swapped_pairs):
        parts = []
        for imag, real in swapped_pairs:
            turned = jnp.concatenate([real * cosine - imag * sine, imag * cosine + real * sine], axis=0)
            parts.append(turned.astype(jnp.bfloat16))
        both = dot(last_ref[...], jnp.concatenate(parts, axis=1))
        return both[:rows] + both[rows:]

    taps_in = jnp.concatenate([part[2 * piece : 2 * piece + taps] for part in got], axis=0).astype(jnp.bfloat16)
    signal_in = jnp.concatenate([gather(group, 0) for group in range(groups)] + [taps_in], axis=1)
    grad_in = jnp.concatenate([gather(group, piece) for group in range(groups)], axis=1)
    signal_stage = first_stage(signal_in)
    grad_stage = first_stage(grad_in)
    forward = second_stage(turn_forward(signal_stage) + turn_forward(grad_stage))
    signals, (tap_real, tap_imag), grads = forward[:groups], forward[groups], forward[groups + 1 :]
    conv_parts = [swapped(r * tap_real - i * tap_imag, r * tap_imag + i * tap_real) for r, i in signals]
    back_parts = [swapped(tap_real * r + tap_imag * i, tap_real * i - tap_imag * r) for r, i in grads]
    corr_real = sum(sr * gr + si * gi for (sr, si), (gr, gi) in zip(signals, grads)) * scale
    corr_imag = sum(sr * gi - si * gr for (sr, si), (gr, gi) in zip(signals, grads)) * scale
    result = last_stage(second_stage(conv_parts + back_parts + [swapped(corr_real, corr_imag)]))
    for peer in range(peers):
        piece_rows = result[peer * piece : (peer + 1) * piece]
        for group in range(groups):
            cut = lambda sequence: piece_rows[:, sequence * LANES : (sequence + 1) * LANES]
            message = jnp.concatenate([cut(group), cut(groups + group), cut(count)], axis=0)
            out_ref[slots[peer * groups + group]] = message.astype(jnp.bfloat16)


def spectral_products(got, piece, groups, peers, scale):
    rows = peers * piece
    tables = dft_tables(rows)
    vmem = pl.BlockSpec(memory_space=pltpu.VMEM)
    return pl.pallas_call(
        functools.partial(spectral_kernel, groups, peers, scale),
        out_shape=jax.ShapeDtypeStruct((got.shape[0], 3 * piece, LANES), jnp.bfloat16),
        in_specs=[vmem] * 5,
        out_specs=vmem,
        compiler_params=pltpu.CompilerParams(vmem_limit_bytes=24 * 2**20),
        name="spectral_products",
    )(got, *[jnp.asarray(table) for table in tables])


def tile_rows(values):
    return values.reshape(values.shape[0], values.shape[1] // LANES, LANES)


def pack_kernel(
    groups,
    signal_hbm,
    gating_hbm,
    cotangent_hbm,
    filters_hbm,
    weight_hbm,
    message_ref,
    column_ref,
    signal_ref,
    gating_ref,
    cotangent_ref,
    taps_ref,
    weight_ref,
    sems,
):
    channels, length = signal_ref.shape
    share = length // groups
    start = pl.multiple_of(lax.axis_index("chan") * share, share)
    copies = [
        pltpu.make_async_copy(source, target, sems.at[at])
        for at, (source, target) in enumerate(
            [
                (cotangent_hbm, cotangent_ref),
                (gating_hbm, gating_ref),
                (signal_hbm, signal_ref),
                (filters_hbm.at[:, pl.ds(start, share)], taps_ref),
                (weight_hbm, weight_ref),
            ]
        )
    ]
    for copy in (copies[2], *copies[:2], *copies[3:]):
        copy.start()
    cotangent_copy, gating_copy, signal_copy, taps_copy, weight_copy = copies
    at = length // (TILE * LANES)

    def put(first, stop, values):
        rows = tile_rows(values).reshape(channels, stop - first, TILE, LANES)
        message_ref[:, first:stop] = rows.astype(jnp.bfloat16)

    signal_copy.wait()
    put(0, at, signal_ref[...].astype(jnp.float32))
    cotangent_copy.wait()
    gating_copy.wait()
    put(at, 2 * at, cotangent_ref[...].astype(jnp.float32) * gating_ref[...].astype(jnp.float32))
    taps_copy.wait()
    put(2 * at, message_ref.shape[1], taps_ref[...])
    weight_copy.wait()
    square = (channels, channels)
    diagonal = lax.broadcasted_iota(jnp.int32, square, 0) == lax.broadcasted_iota(jnp.int32, square, 1)
    weight = jnp.sum(jnp.where(diagonal, jnp.broadcast_to(weight_ref[...], square), 0.0), axis=1, keepdims=True)
    column_ref[...] = jnp.broadcast_to(weight, column_ref.shape)


def pack(signal, gating, cotangent, filters, skip_weight, groups):
    channels, length = signal.shape
    vmem = pl.BlockSpec(memory_space=pltpu.VMEM)
    operands = (signal, gating, cotangent, filters, skip_weight[None, :])
    return pl.pallas_call(
        functools.partial(pack_kernel, groups),
        out_shape=(
            jax.ShapeDtypeStruct((channels, (2 * length + length // groups) // (TILE * LANES), TILE, LANES), jnp.bfloat16),
            jax.ShapeDtypeStruct((channels, LANES), jnp.float32),
        ),
        in_specs=[pl.BlockSpec(memory_space=pltpu.HBM)] * 5,
        out_specs=(vmem, vmem),
        scratch_shapes=[pltpu.VMEM(signal.shape, jnp.bfloat16)] * 3
        + [
            pltpu.VMEM((filters.shape[0], length // groups), jnp.float32),
            pltpu.VMEM((1, channels), jnp.float32),
            pltpu.SemaphoreType.DMA((5,)),
        ],
        compiler_params=pltpu.CompilerParams(vmem_limit_bytes=16 * 2**20),
        name="pack",
    )(*[pltpu.with_memory_space_constraint(operand, pltpu.HBM) for operand in operands])


def finish_kernel(groups, home_ref, signal_ref, gating_ref, cotangent_ref, column_ref, signal_out, gating_out, filters_out):
    channels, length = signal_ref.shape
    piece = length // LANES
    share = channels // groups
    home = home_ref[...].astype(jnp.float32).reshape(channels, 3 * length)
    cotangent = cotangent_ref[...].astype(jnp.float32)
    gated = (cotangent * gating_ref[...].astype(jnp.float32)).astype(jnp.bfloat16).astype(jnp.float32)
    weight = column_ref[:, :1]
    outputs = home[:, :length] + weight * signal_ref[...].astype(jnp.float32)
    gating_out[...] = (cotangent * outputs).astype(jnp.bfloat16)
    signal_out[...] = (home[:, length : 2 * length] + weight * gated).astype(jnp.bfloat16)
    first = pl.multiple_of(lax.axis_index("chan") * share, share)
    corr = home_ref[pl.ds(first, share), 2 * piece :, :].astype(jnp.float32)
    filters_out[...] = corr.reshape(share, length)


def finish(home, signal, gating, cotangent, column, groups):
    channels, length = signal.shape
    vmem = pl.BlockSpec(memory_space=pltpu.VMEM)
    return pl.pallas_call(
        functools.partial(finish_kernel, groups),
        out_shape=(
            jax.ShapeDtypeStruct(signal.shape, jnp.bfloat16),
            jax.ShapeDtypeStruct(signal.shape, jnp.bfloat16),
            jax.ShapeDtypeStruct((channels // groups, length), jnp.float32),
        ),
        in_specs=[vmem] * 5,
        out_specs=(vmem,) * 3,
        compiler_params=pltpu.CompilerParams(vmem_limit_bytes=16 * 2**20),
        name="finish",
    )(home, signal, gating, cotangent, column)


def filter_per_device(signal, gating, cotangent, filters, skip_weight):
    peers = lax.axis_size("ctx")
    groups = lax.axis_size("chan")
    message, column = pack(signal, gating, cotangent, filters, skip_weight, groups)
    exchange = functools.partial(
        lax.all_to_all,
        axis_name=("ctx", "chan"),
        split_axis=0,
        concat_axis=0,
        axis_index_groups=[slot_order(peers, groups)],
        tiled=True,
    )
    got = exchange(message)
    scale = 1.0 / math.sqrt(signal.shape[1] * peers * groups)
    result = spectral_products(got, signal.shape[1] // LANES, groups, peers, scale)
    home = exchange(result)
    return finish(home, signal, gating, cotangent, column, groups)


def product(form, left, right):
    return jnp.einsum(
        form, left, right, precision=lax.Precision.HIGHEST, preferred_element_type=jnp.float32
    )


def phases(left_idx, right_idx, period):
    joined = left_idx[:, None] * right_idx[None, :] % period
    return joined.astype(jnp.float32) * (2.0 * math.pi / period)


def indices(total):
    return jnp.arange(total, dtype=jnp.int32)


def turn_forward(real_part, imag_part, angles):
    cosine = jnp.cos(angles)
    sine_part = jnp.sin(angles)
    return (real_part * cosine + imag_part * sine_part, imag_part * cosine - real_part * sine_part)


def turn_back(real_part, imag_part, angles):
    cosine = jnp.cos(angles)
    sine_part = jnp.sin(angles)
    return (real_part * cosine - imag_part * sine_part, imag_part * cosine + real_part * sine_part)


def first_pass(blocks, position, peer_count):
    height, length = blocks.shape
    piece_len = length // peer_count
    padded = 2 * peer_count * length
    shaped = blocks.reshape(height, peer_count, piece_len)
    angles = phases(indices(peer_count), indices(2 * peer_count), 2 * peer_count)
    real_part = product("rdm,dk->rmk", shaped, jnp.cos(angles))
    imag_part = -product("rdm,dk->rmk", shaped, jnp.sin(angles))
    offsets = position * piece_len + indices(piece_len)
    real_part, imag_part = turn_forward(
        real_part, imag_part, phases(offsets, indices(2 * peer_count), padded)
    )
    return jnp.stack([real_part, imag_part])


def second_pass(columns, peer_count):
    height, piece_len = (columns.shape[1], columns.shape[2])
    length = piece_len * peer_count
    real_part = columns[0].reshape(height, piece_len, peer_count, 2)
    imag_part = columns[1].reshape(height, piece_len, peer_count, 2)
    angles = phases(indices(peer_count), indices(peer_count), peer_count)
    cosine = jnp.cos(angles)
    sine_part = jnp.sin(angles)
    real_one = product("rmeb,ea->rbma", real_part, cosine) + product(
        "rmeb,ea->rbma", imag_part, sine_part
    )
    imag_one = product("rmeb,ea->rbma", imag_part, cosine) - product(
        "rmeb,ea->rbma", real_part, sine_part
    )
    real_one, imag_one = turn_forward(
        real_one, imag_one, phases(indices(piece_len), indices(peer_count), length)
    )
    angles = phases(indices(piece_len), indices(piece_len), piece_len)
    cosine = jnp.cos(angles)
    sine_part = jnp.sin(angles)
    real_two = product("rbma,mc->rbca", real_one, cosine) + product(
        "rbma,mc->rbca", imag_one, sine_part
    )
    imag_two = product("rbma,mc->rbca", imag_one, cosine) - product(
        "rbma,mc->rbca", real_one, sine_part
    )
    return jnp.stack([real_two.reshape(height, 2, length), imag_two.reshape(height, 2, length)])


def inverse_first(spectrum, position, peer_count):
    height, length = (spectrum.shape[1], spectrum.shape[3])
    piece_len = length // peer_count
    padded = 2 * peer_count * length
    real_part = spectrum[0].reshape(height, 2, piece_len, peer_count)
    imag_part = spectrum[1].reshape(height, 2, piece_len, peer_count)
    angles = phases(indices(piece_len), indices(piece_len), piece_len)
    cosine = jnp.cos(angles)
    sine_part = jnp.sin(angles)
    real_one = product("rbca,cm->rbma", real_part, cosine) - product(
        "rbca,cm->rbma", imag_part, sine_part
    )
    imag_one = product("rbca,cm->rbma", imag_part, cosine) + product(
        "rbca,cm->rbma", real_part, sine_part
    )
    real_one, imag_one = turn_back(
        real_one, imag_one, phases(indices(piece_len), indices(peer_count), length)
    )
    angles = phases(indices(peer_count), indices(peer_count), peer_count)
    cosine = jnp.cos(angles)
    sine_part = jnp.sin(angles)
    real_two = product("rbma,ae->rmeb", real_one, cosine) - product(
        "rbma,ae->rmeb", imag_one, sine_part
    )
    imag_two = product("rbma,ae->rmeb", imag_one, cosine) + product(
        "rbma,ae->rmeb", real_one, sine_part
    )
    offsets = (indices(peer_count)[None, :] * piece_len + indices(piece_len)[:, None]).reshape(-1)
    freq_bins = 2 * position + indices(2)
    angles = phases(offsets, freq_bins, padded).reshape(piece_len, peer_count, 2)
    real_two, imag_two = turn_back(real_two, imag_two, angles)
    return jnp.stack(
        [
            real_two.reshape(height, piece_len, 2 * peer_count),
            imag_two.reshape(height, piece_len, 2 * peer_count),
        ]
    )


def inverse_second(received, peer_count):
    height, piece_len = (received.shape[1], received.shape[2])
    length = piece_len * peer_count
    padded = 2 * peer_count * length
    angles = phases(indices(2 * peer_count), indices(peer_count), 2 * peer_count)
    signal_out = product("rmk,kd->rdm", received[0], jnp.cos(angles)) - product(
        "rmk,kd->rdm", received[1], jnp.sin(angles)
    )
    return (signal_out / padded).reshape(height, length)


def split_transforms(signal, gating, cotangent, filters, skip_weight):
    peer_count = lax.axis_size("ctx")
    position = lax.axis_index("ctx")
    channels, length = signal.shape
    count_filters = filters.shape[0]
    local_group = channels // count_filters
    gated_grad = (cotangent.astype(jnp.float32) * gating.astype(jnp.float32)).astype(jnp.bfloat16)
    signal_blocks, gated_blocks = (
        lax.all_to_all(signal, "ctx", split_axis=1, concat_axis=1, tiled=True),
        lax.all_to_all(gated_grad, "ctx", split_axis=1, concat_axis=1, tiled=True),
    )
    tap_blocks = lax.all_to_all(filters, "ctx", split_axis=1, concat_axis=1, tiled=True)
    signal_cols, gated_cols, tap_cols = (
        lax.all_to_all(
            first_pass(signal_blocks.astype(jnp.float32), position, peer_count),
            "ctx",
            split_axis=3,
            concat_axis=3,
            tiled=True,
        ),
        lax.all_to_all(
            first_pass(gated_blocks.astype(jnp.float32), position, peer_count),
            "ctx",
            split_axis=3,
            concat_axis=3,
            tiled=True,
        ),
        lax.all_to_all(
            first_pass(tap_blocks, position, peer_count),
            "ctx",
            split_axis=3,
            concat_axis=3,
            tiled=True,
        ),
    )
    signal_spec = second_pass(signal_cols, peer_count).reshape(
        2, local_group, count_filters, 2, length
    )
    gated_spec = second_pass(gated_cols, peer_count).reshape(
        2, local_group, count_filters, 2, length
    )
    tap_spec = second_pass(tap_cols, peer_count)
    tap_real, tap_imag = (tap_spec[0], tap_spec[1])
    sig_real, sig_imag = (signal_spec[0], signal_spec[1])
    gated_real, gated_imag = (gated_spec[0], gated_spec[1])
    forward_spec = jnp.stack(
        [sig_real * tap_real - sig_imag * tap_imag, sig_real * tap_imag + sig_imag * tap_real]
    ).reshape(2, channels, 2, length)
    back_spec = jnp.stack(
        [
            tap_real * gated_real + tap_imag * gated_imag,
            tap_real * gated_imag - tap_imag * gated_real,
        ]
    ).reshape(2, channels, 2, length)
    corr_spec = jnp.stack(
        [
            jnp.sum(sig_real * gated_real + sig_imag * gated_imag, axis=0),
            jnp.sum(sig_real * gated_imag - sig_imag * gated_real, axis=0),
        ]
    )
    forward_cols, back_cols, corr_cols = (
        lax.all_to_all(
            inverse_first(forward_spec, position, peer_count),
            "ctx",
            split_axis=3,
            concat_axis=3,
            tiled=True,
        ),
        lax.all_to_all(
            inverse_first(back_spec, position, peer_count),
            "ctx",
            split_axis=3,
            concat_axis=3,
            tiled=True,
        ),
        lax.all_to_all(
            inverse_first(corr_spec, position, peer_count),
            "ctx",
            split_axis=3,
            concat_axis=3,
            tiled=True,
        ),
    )
    conv_time, back_time, corr_time = (
        lax.all_to_all(
            inverse_second(forward_cols, peer_count), "ctx", split_axis=1, concat_axis=1, tiled=True
        ),
        lax.all_to_all(
            inverse_second(back_cols, peer_count), "ctx", split_axis=1, concat_axis=1, tiled=True
        ),
        lax.all_to_all(
            inverse_second(corr_cols, peer_count), "ctx", split_axis=1, concat_axis=1, tiled=True
        ),
    )
    corr_time = lax.psum_scatter(corr_time, "chan", scatter_dimension=0, tiled=True)
    weight = skip_weight[:, None]
    outputs = conv_time + weight * signal.astype(jnp.float32)
    grad_gating = (cotangent.astype(jnp.float32) * outputs).astype(jnp.bfloat16)
    grad_signal = (back_time + weight * gated_grad.astype(jnp.float32)).astype(jnp.bfloat16)
    normal_scale = 1.0 / math.sqrt(length * peer_count * local_group * lax.axis_size("chan"))
    grad_filters = corr_time * normal_scale
    return (grad_signal, grad_gating, grad_filters)


def per_device(signal, gating, cotangent, filters, skip_weight):
    peers, groups = lax.axis_size("ctx"), lax.axis_size("chan")
    channels, length = signal.shape
    one_each = channels == filters.shape[0] == peers * groups
    piece = length // LANES
    whole_tiles = length % (8 * LANES) == 0 and piece % groups == 0
    if one_each and whole_tiles and (peers * piece) % 16 == 0 and (piece // groups) % TILE == 0:
        return filter_per_device(signal, gating, cotangent, filters, skip_weight)
    return split_transforms(signal, gating, cotangent, filters, skip_weight)


def solution(mesh):
    in_specs = (P("chan", "ctx"), P("chan", "ctx"), P("chan", "ctx"), P(None, "ctx"), P("chan"))
    out_specs = (P("chan", "ctx"), P("chan", "ctx"), P("chan", "ctx"))
    return jax.shard_map(
        per_device, mesh=mesh, in_specs=in_specs, out_specs=out_specs, check_vma=False
    )
```

```python
import functools
import math

import jax
import jax.numpy as jnp
import numpy as np
from jax import lax
from jax.experimental import pallas as pl
from jax.experimental.pallas import tpu as pltpu
from jax.sharding import PartitionSpec as P

LANES = 128
TILE = 2


def split_table(table):
    high = table.astype(jnp.bfloat16)
    low = (table - high.astype(np.float64)).astype(jnp.bfloat16)
    return high, low


def dft_tables(rows):
    height = 2 * rows
    padded = height * LANES
    k1 = np.arange(rows)
    n1 = np.arange(rows)
    n2 = np.arange(LANES)
    outer = np.pi * (np.outer(2 * k1 + 1, n1) % (2 * height)) / height
    high, low = split_table(np.concatenate([np.cos(outer), -np.sin(outer)], axis=0))
    first = high
    turn = np.pi * (np.outer(2 * k1 + 1, n2) % (2 * padded)) / padded
    twiddle = np.stack([np.cos(turn), np.sin(turn)]).astype(np.float32)
    inner = 2.0 * np.pi * (np.outer(n2, n2) % LANES) / LANES
    cosine, sine = np.cos(inner), np.sin(inner)
    second = np.block([[cosine, -sine], [sine, cosine]]).astype(jnp.bfloat16)
    high, low = split_table(np.concatenate([np.cos(outer.T), -np.sin(outer.T)], axis=1) * (2.0 / padded))
    last = high
    return first, twiddle, second, last


def dot(left, right):
    return jnp.dot(left, right, preferred_element_type=jnp.float32)


def slot_order(peers, groups):
    if peers % 2 or groups % 2:
        return list(range(peers * groups))
    return [
        (high * 2 + low) * groups + (plane * 2 + core)
        for plane in range(groups // 2)
        for low in range(2)
        for high in [0, *reversed(range(1, peers // 2))]
        for core in range(2)
    ]


def spectral_kernel(
    groups, peers, scale, got_ref, first_ref, twiddle_ref, second_ref, last_ref, out_ref
):
    piece = out_ref.shape[1] // 3
    taps = piece // groups
    rows = peers * piece
    kept = twiddle_ref.shape[1]
    count = 2 * groups
    order = slot_order(peers, groups)
    slots = [order.index(device) for device in range(peers * groups)]
    got = got_ref[...].astype(jnp.float32).reshape(peers * groups, -1, LANES)
    got = [got[slot] for slot in slots]

    def gather(group, start):
        parts = [got[peer * groups + group][start : start + piece] for peer in range(peers)]
        return jnp.concatenate(parts, axis=0).astype(jnp.bfloat16)

    cosine, sine = twiddle_ref[0], twiddle_ref[1]
    second = second_ref[...]

    def first_stage(values):
        return dot(first_ref[...], values)

    def turn_forward(stage):
        parts = []
        for at in range(0, stage.shape[1], LANES):
            real, imag = stage[:kept, at : at + LANES], stage[kept:, at : at + LANES]
            turned = jnp.concatenate([real * cosine + imag * sine, imag * cosine - real * sine], axis=1)
            parts.append(turned.astype(jnp.bfloat16))
        return parts

    def second_stage(parts):
        both = dot(jnp.concatenate(parts, axis=0), second)
        cuts = [both[at : at + kept] for at in range(0, both.shape[0], kept)]
        return [(cut[:, :LANES], cut[:, LANES:]) for cut in cuts]

    def swapped(real, imag):
        return jnp.concatenate([imag, real], axis=1).astype(jnp.bfloat16)

    def last_stage(swapped_pairs):
        parts = []
        for imag, real in swapped_pairs:
            turned = jnp.concatenate([real * cosine - imag * sine, imag * cosine + real * sine], axis=0)
            parts.append(turned.astype(jnp.bfloat16))
        return dot(last_ref[...], jnp.concatenate(parts, axis=1))

    taps_in = jnp.concatenate([part[2 * piece : 2 * piece + taps] for part in got], axis=0).astype(jnp.bfloat16)
    signal_in = jnp.concatenate([gather(group, 0) for group in range(groups)] + [taps_in], axis=1)
    grad_in = jnp.concatenate([gather(group, piece) for group in range(groups)], axis=1)
    signal_stage = first_stage(signal_in)
    grad_stage = first_stage(grad_in)
    forward = second_stage(turn_forward(signal_stage) + turn_forward(grad_stage))
    signals, (tap_real, tap_imag), grads = forward[:groups], forward[groups], forward[groups + 1 :]
    conv_parts = [swapped(r * tap_real - i * tap_imag, r * tap_imag + i * tap_real) for r, i in signals]
    back_parts = [swapped(tap_real * r + tap_imag * i, tap_real * i - tap_imag * r) for r, i in grads]
    corr_real = sum(sr * gr + si * gi for (sr, si), (gr, gi) in zip(signals, grads)) * scale
    corr_imag = sum(sr * gi - si * gr for (sr, si), (gr, gi) in zip(signals, grads)) * scale
    result = last_stage(second_stage(conv_parts + back_parts + [swapped(corr_real, corr_imag)]))
    for peer in range(peers):
        piece_rows = result[peer * piece : (peer + 1) * piece]
        for group in range(groups):
            cut = lambda sequence: piece_rows[:, sequence * LANES : (sequence + 1) * LANES]
            message = jnp.concatenate([cut(group), cut(groups + group), cut(count)], axis=0)
            out_ref[slots[peer * groups + group]] = message.astype(jnp.bfloat16)


def spectral_products(got, piece, groups, peers, scale):
    rows = peers * piece
    tables = dft_tables(rows)
    vmem = pl.BlockSpec(memory_space=pltpu.VMEM)
    return pl.pallas_call(
        functools.partial(spectral_kernel, groups, peers, scale),
        out_shape=jax.ShapeDtypeStruct((got.shape[0], 3 * piece, LANES), jnp.bfloat16),
        in_specs=[vmem] * 5,
        out_specs=vmem,
        compiler_params=pltpu.CompilerParams(vmem_limit_bytes=24 * 2**20),
        name="spectral_products",
    )(got, *[jnp.asarray(table) for table in tables])


def tile_rows(values):
    return values.reshape(values.shape[0], values.shape[1] // LANES, LANES)


def pack_kernel(
    groups,
    signal_hbm,
    gating_hbm,
    cotangent_hbm,
    filters_hbm,
    weight_hbm,
    message_ref,
    column_ref,
    signal_ref,
    gating_ref,
    cotangent_ref,
    taps_ref,
    weight_ref,
    sems,
):
    channels, length = signal_ref.shape
    share = length // groups
    start = pl.multiple_of(lax.axis_index("chan") * share, share)
    copies = [
        pltpu.make_async_copy(source, target, sems.at[at])
        for at, (source, target) in enumerate(
            [
                (cotangent_hbm, cotangent_ref),
                (gating_hbm, gating_ref),
                (signal_hbm, signal_ref),
                (filters_hbm.at[:, pl.ds(start, share)], taps_ref),
                (weight_hbm, weight_ref),
            ]
        )
    ]
    for copy in (copies[2], *copies[:2], *copies[3:]):
        copy.start()
    cotangent_copy, gating_copy, signal_copy, taps_copy, weight_copy = copies
    at = length // (TILE * LANES)

    def put(first, stop, values):
        rows = tile_rows(values).reshape(channels, stop - first, TILE, LANES)
        message_ref[:, first:stop] = rows.astype(jnp.bfloat16)

    signal_copy.wait()
    put(0, at, signal_ref[...].astype(jnp.float32))
    cotangent_copy.wait()
    gating_copy.wait()
    put(at, 2 * at, cotangent_ref[...].astype(jnp.float32) * gating_ref[...].astype(jnp.float32))
    taps_copy.wait()
    put(2 * at, message_ref.shape[1], taps_ref[...])
    weight_copy.wait()
    square = (channels, channels)
    diagonal = lax.broadcasted_iota(jnp.int32, square, 0) == lax.broadcasted_iota(jnp.int32, square, 1)
    weight = jnp.sum(jnp.where(diagonal, jnp.broadcast_to(weight_ref[...], square), 0.0), axis=1, keepdims=True)
    column_ref[...] = jnp.broadcast_to(weight, column_ref.shape)


def pack(signal, gating, cotangent, filters, skip_weight, groups):
    channels, length = signal.shape
    vmem = pl.BlockSpec(memory_space=pltpu.VMEM)
    operands = (signal, gating, cotangent, filters, skip_weight[None, :])
    return pl.pallas_call(
        functools.partial(pack_kernel, groups),
        out_shape=(
            jax.ShapeDtypeStruct((channels, (2 * length + length // groups) // (TILE * LANES), TILE, LANES), jnp.bfloat16),
            jax.ShapeDtypeStruct((channels, LANES), jnp.float32),
        ),
        in_specs=[pl.BlockSpec(memory_space=pltpu.HBM)] * 5,
        out_specs=(vmem, vmem),
        scratch_shapes=[pltpu.VMEM(signal.shape, jnp.bfloat16)] * 3
        + [
            pltpu.VMEM((filters.shape[0], length // groups), jnp.float32),
            pltpu.VMEM((1, channels), jnp.float32),
            pltpu.SemaphoreType.DMA((5,)),
        ],
        compiler_params=pltpu.CompilerParams(vmem_limit_bytes=16 * 2**20),
        name="pack",
    )(*[pltpu.with_memory_space_constraint(operand, pltpu.HBM) for operand in operands])


def finish_kernel(groups, home_ref, signal_ref, gating_ref, cotangent_ref, column_ref, signal_out, gating_out, filters_out):
    channels, length = signal_ref.shape
    piece = length // LANES
    share = channels // groups
    home = home_ref[...].astype(jnp.float32).reshape(channels, 3 * length)
    cotangent = cotangent_ref[...].astype(jnp.float32)
    gated = (cotangent * gating_ref[...].astype(jnp.float32)).astype(jnp.bfloat16).astype(jnp.float32)
    weight = column_ref[:, :1]
    outputs = home[:, :length] + weight * signal_ref[...].astype(jnp.float32)
    gating_out[...] = (cotangent * outputs).astype(jnp.bfloat16)
    signal_out[...] = (home[:, length : 2 * length] + weight * gated).astype(jnp.bfloat16)
    first = pl.multiple_of(lax.axis_index("chan") * share, share)
    corr = home_ref[pl.ds(first, share), 2 * piece :, :].astype(jnp.float32)
    filters_out[...] = corr.reshape(share, length)


def finish(home, signal, gating, cotangent, column, groups):
    channels, length = signal.shape
    vmem = pl.BlockSpec(memory_space=pltpu.VMEM)
    return pl.pallas_call(
        functools.partial(finish_kernel, groups),
        out_shape=(
            jax.ShapeDtypeStruct(signal.shape, jnp.bfloat16),
            jax.ShapeDtypeStruct(signal.shape, jnp.bfloat16),
            jax.ShapeDtypeStruct((channels // groups, length), jnp.float32),
        ),
        in_specs=[vmem] * 5,
        out_specs=(vmem,) * 3,
        compiler_params=pltpu.CompilerParams(vmem_limit_bytes=16 * 2**20),
        name="finish",
    )(home, signal, gating, cotangent, column)


def filter_per_device(signal, gating, cotangent, filters, skip_weight):
    peers = lax.axis_size("ctx")
    groups = lax.axis_size("chan")
    message, column = pack(signal, gating, cotangent, filters, skip_weight, groups)
    exchange = functools.partial(
        lax.all_to_all,
        axis_name=("ctx", "chan"),
        split_axis=0,
        concat_axis=0,
        axis_index_groups=[slot_order(peers, groups)],
        tiled=True,
    )
    got = exchange(message)
    scale = 1.0 / math.sqrt(signal.shape[1] * peers * groups)
    result = spectral_products(got, signal.shape[1] // LANES, groups, peers, scale)
    home = exchange(result)
    return finish(home, signal, gating, cotangent, column, groups)


def product(form, left, right):
    return jnp.einsum(
        form, left, right, precision=lax.Precision.HIGHEST, preferred_element_type=jnp.float32
    )


def phases(left_idx, right_idx, period):
    joined = left_idx[:, None] * right_idx[None, :] % period
    return joined.astype(jnp.float32) * (2.0 * math.pi / period)


def indices(total):
    return jnp.arange(total, dtype=jnp.int32)


def turn_forward(real_part, imag_part, angles):
    cosine = jnp.cos(angles)
    sine_part = jnp.sin(angles)
    return (real_part * cosine + imag_part * sine_part, imag_part * cosine - real_part * sine_part)


def turn_back(real_part, imag_part, angles):
    cosine = jnp.cos(angles)
    sine_part = jnp.sin(angles)
    return (real_part * cosine - imag_part * sine_part, imag_part * cosine + real_part * sine_part)


def first_pass(blocks, position, peer_count):
    height, length = blocks.shape
    piece_len = length // peer_count
    padded = 2 * peer_count * length
    shaped = blocks.reshape(height, peer_count, piece_len)
    angles = phases(indices(peer_count), indices(2 * peer_count), 2 * peer_count)
    real_part = product("rdm,dk->rmk", shaped, jnp.cos(angles))
    imag_part = -product("rdm,dk->rmk", shaped, jnp.sin(angles))
    offsets = position * piece_len + indices(piece_len)
    real_part, imag_part = turn_forward(
        real_part, imag_part, phases(offsets, indices(2 * peer_count), padded)
    )
    return jnp.stack([real_part, imag_part])


def second_pass(columns, peer_count):
    height, piece_len = (columns.shape[1], columns.shape[2])
    length = piece_len * peer_count
    real_part = columns[0].reshape(height, piece_len, peer_count, 2)
    imag_part = columns[1].reshape(height, piece_len, peer_count, 2)
    angles = phases(indices(peer_count), indices(peer_count), peer_count)
    cosine = jnp.cos(angles)
    sine_part = jnp.sin(angles)
    real_one = product("rmeb,ea->rbma", real_part, cosine) + product(
        "rmeb,ea->rbma", imag_part, sine_part
    )
    imag_one = product("rmeb,ea->rbma", imag_part, cosine) - product(
        "rmeb,ea->rbma", real_part, sine_part
    )
    real_one, imag_one = turn_forward(
        real_one, imag_one, phases(indices(piece_len), indices(peer_count), length)
    )
    angles = phases(indices(piece_len), indices(piece_len), piece_len)
    cosine = jnp.cos(angles)
    sine_part = jnp.sin(angles)
    real_two = product("rbma,mc->rbca", real_one, cosine) + product(
        "rbma,mc->rbca", imag_one, sine_part
    )
    imag_two = product("rbma,mc->rbca", imag_one, cosine) - product(
        "rbma,mc->rbca", real_one, sine_part
    )
    return jnp.stack([real_two.reshape(height, 2, length), imag_two.reshape(height, 2, length)])


def inverse_first(spectrum, position, peer_count):
    height, length = (spectrum.shape[1], spectrum.shape[3])
    piece_len = length // peer_count
    padded = 2 * peer_count * length
    real_part = spectrum[0].reshape(height, 2, piece_len, peer_count)
    imag_part = spectrum[1].reshape(height, 2, piece_len, peer_count)
    angles = phases(indices(piece_len), indices(piece_len), piece_len)
    cosine = jnp.cos(angles)
    sine_part = jnp.sin(angles)
    real_one = product("rbca,cm->rbma", real_part, cosine) - product(
        "rbca,cm->rbma", imag_part, sine_part
    )
    imag_one = product("rbca,cm->rbma", imag_part, cosine) + product(
        "rbca,cm->rbma", real_part, sine_part
    )
    real_one, imag_one = turn_back(
        real_one, imag_one, phases(indices(piece_len), indices(peer_count), length)
    )
    angles = phases(indices(peer_count), indices(peer_count), peer_count)
    cosine = jnp.cos(angles)
    sine_part = jnp.sin(angles)
    real_two = product("rbma,ae->rmeb", real_one, cosine) - product(
        "rbma,ae->rmeb", imag_one, sine_part
    )
    imag_two = product("rbma,ae->rmeb", imag_one, cosine) + product(
        "rbma,ae->rmeb", real_one, sine_part
    )
    offsets = (indices(peer_count)[None, :] * piece_len + indices(piece_len)[:, None]).reshape(-1)
    freq_bins = 2 * position + indices(2)
    angles = phases(offsets, freq_bins, padded).reshape(piece_len, peer_count, 2)
    real_two, imag_two = turn_back(real_two, imag_two, angles)
    return jnp.stack(
        [
            real_two.reshape(height, piece_len, 2 * peer_count),
            imag_two.reshape(height, piece_len, 2 * peer_count),
        ]
    )


def inverse_second(received, peer_count):
    height, piece_len = (received.shape[1], received.shape[2])
    length = piece_len * peer_count
    padded = 2 * peer_count * length
    angles = phases(indices(2 * peer_count), indices(peer_count), 2 * peer_count)
    signal_out = product("rmk,kd->rdm", received[0], jnp.cos(angles)) - product(
        "rmk,kd->rdm", received[1], jnp.sin(angles)
    )
    return (signal_out / padded).reshape(height, length)


def split_transforms(signal, gating, cotangent, filters, skip_weight):
    peer_count = lax.axis_size("ctx")
    position = lax.axis_index("ctx")
    channels, length = signal.shape
    count_filters = filters.shape[0]
    local_group = channels // count_filters
    gated_grad = (cotangent.astype(jnp.float32) * gating.astype(jnp.float32)).astype(jnp.bfloat16)
    signal_blocks, gated_blocks = (
        lax.all_to_all(signal, "ctx", split_axis=1, concat_axis=1, tiled=True),
        lax.all_to_all(gated_grad, "ctx", split_axis=1, concat_axis=1, tiled=True),
    )
    tap_blocks = lax.all_to_all(filters, "ctx", split_axis=1, concat_axis=1, tiled=True)
    signal_cols, gated_cols, tap_cols = (
        lax.all_to_all(
            first_pass(signal_blocks.astype(jnp.float32), position, peer_count),
            "ctx",
            split_axis=3,
            concat_axis=3,
            tiled=True,
        ),
        lax.all_to_all(
            first_pass(gated_blocks.astype(jnp.float32), position, peer_count),
            "ctx",
            split_axis=3,
            concat_axis=3,
            tiled=True,
        ),
        lax.all_to_all(
            first_pass(tap_blocks, position, peer_count),
            "ctx",
            split_axis=3,
            concat_axis=3,
            tiled=True,
        ),
    )
    signal_spec = second_pass(signal_cols, peer_count).reshape(
        2, local_group, count_filters, 2, length
    )
    gated_spec = second_pass(gated_cols, peer_count).reshape(
        2, local_group, count_filters, 2, length
    )
    tap_spec = second_pass(tap_cols, peer_count)
    tap_real, tap_imag = (tap_spec[0], tap_spec[1])
    sig_real, sig_imag = (signal_spec[0], signal_spec[1])
    gated_real, gated_imag = (gated_spec[0], gated_spec[1])
    forward_spec = jnp.stack(
        [sig_real * tap_real - sig_imag * tap_imag, sig_real * tap_imag + sig_imag * tap_real]
    ).reshape(2, channels, 2, length)
    back_spec = jnp.stack(
        [
            tap_real * gated_real + tap_imag * gated_imag,
            tap_real * gated_imag - tap_imag * gated_real,
        ]
    ).reshape(2, channels, 2, length)
    corr_spec = jnp.stack(
        [
            jnp.sum(sig_real * gated_real + sig_imag * gated_imag, axis=0),
            jnp.sum(sig_real * gated_imag - sig_imag * gated_real, axis=0),
        ]
    )
    forward_cols, back_cols, corr_cols = (
        lax.all_to_all(
            inverse_first(forward_spec, position, peer_count),
            "ctx",
            split_axis=3,
            concat_axis=3,
            tiled=True,
        ),
        lax.all_to_all(
            inverse_first(back_spec, position, peer_count),
            "ctx",
            split_axis=3,
            concat_axis=3,
            tiled=True,
        ),
        lax.all_to_all(
            inverse_first(corr_spec, position, peer_count),
            "ctx",
            split_axis=3,
            concat_axis=3,
            tiled=True,
        ),
    )
    conv_time, back_time, corr_time = (
        lax.all_to_all(
            inverse_second(forward_cols, peer_count), "ctx", split_axis=1, concat_axis=1, tiled=True
        ),
        lax.all_to_all(
            inverse_second(back_cols, peer_count), "ctx", split_axis=1, concat_axis=1, tiled=True
        ),
        lax.all_to_all(
            inverse_second(corr_cols, peer_count), "ctx", split_axis=1, concat_axis=1, tiled=True
        ),
    )
    corr_time = lax.psum_scatter(corr_time, "chan", scatter_dimension=0, tiled=True)
    weight = skip_weight[:, None]
    outputs = conv_time + weight * signal.astype(jnp.float32)
    grad_gating = (cotangent.astype(jnp.float32) * outputs).astype(jnp.bfloat16)
    grad_signal = (back_time + weight * gated_grad.astype(jnp.float32)).astype(jnp.bfloat16)
    normal_scale = 1.0 / math.sqrt(length * peer_count * local_group * lax.axis_size("chan"))
    grad_filters = corr_time * normal_scale
    return (grad_signal, grad_gating, grad_filters)


def per_device(signal, gating, cotangent, filters, skip_weight):
    peers, groups = lax.axis_size("ctx"), lax.axis_size("chan")
    channels, length = signal.shape
    one_each = channels == filters.shape[0] == peers * groups
    piece = length // LANES
    whole_tiles = length % (8 * LANES) == 0 and piece % groups == 0
    if one_each and whole_tiles and (peers * piece) % 16 == 0 and (piece // groups) % TILE == 0:
        return filter_per_device(signal, gating, cotangent, filters, skip_weight)
    return split_transforms(signal, gating, cotangent, filters, skip_weight)


def solution(mesh):
    in_specs = (P("chan", "ctx"), P("chan", "ctx"), P("chan", "ctx"), P(None, "ctx"), P("chan"))
    out_specs = (P("chan", "ctx"), P("chan", "ctx"), P("chan", "ctx"))
    return jax.shard_map(
        per_device, mesh=mesh, in_specs=in_specs, out_specs=out_specs, check_vma=False
    )
```

```python
import functools
import math

import jax
import jax.numpy as jnp
import numpy as np
from jax import lax
from jax.experimental import pallas as pl
from jax.experimental.pallas import tpu as pltpu
from jax.sharding import PartitionSpec as P

LANES = 128
TILE = 2


def split_table(table):
    high = table.astype(jnp.bfloat16)
    low = (table - high.astype(np.float64)).astype(jnp.bfloat16)
    return high, low


def dft_tables(rows):
    height = 2 * rows
    padded = height * LANES
    k1 = np.arange(rows)
    n1 = np.arange(rows)
    n2 = np.arange(LANES)
    outer = np.pi * (np.outer(2 * k1 + 1, n1) % (2 * height)) / height
    high, low = split_table(np.concatenate([np.cos(outer), -np.sin(outer)], axis=0))
    first = np.concatenate([high, low], axis=1)
    turn = np.pi * (np.outer(2 * k1 + 1, n2) % (2 * padded)) / padded
    twiddle = np.stack([np.cos(turn), np.sin(turn)]).astype(np.float32)
    inner = 2.0 * np.pi * (np.outer(n2, n2) % LANES) / LANES
    cosine, sine = np.cos(inner), np.sin(inner)
    second = np.block([[cosine, -sine], [sine, cosine]]).astype(jnp.bfloat16)
    high, low = split_table(np.concatenate([np.cos(outer.T), -np.sin(outer.T)], axis=1) * (2.0 / padded))
    last = np.concatenate([high, low], axis=0)
    return first, twiddle, second, last


def dot(left, right):
    return jnp.dot(left, right, preferred_element_type=jnp.float32)


def slot_order(peers, groups):
    if peers % 2 or groups % 2:
        return list(range(peers * groups))
    outer = list(reversed(range(peers // 2)))
    return [
        (high * 2 + low) * groups + (plane * 2 + core)
        for plane in range(groups // 2)
        for low in range(2)
        for high in [*outer[-2:], *outer[:-2]]
        for core in range(2)
    ]


def spectral_kernel(
    groups, peers, scale, got_ref, first_ref, twiddle_ref, second_ref, last_ref, out_ref
):
    piece = out_ref.shape[1] // 3
    taps = piece // groups
    rows = peers * piece
    kept = twiddle_ref.shape[1]
    count = 2 * groups
    order = slot_order(peers, groups)
    slots = [order.index(device) for device in range(peers * groups)]
    got = got_ref[...].astype(jnp.float32).reshape(peers * groups, -1, LANES)
    got = [got[slot] for slot in slots]

    def gather(group, start):
        parts = [got[peer * groups + group][start : start + piece] for peer in range(peers)]
        return jnp.concatenate(parts, axis=0).astype(jnp.bfloat16)

    cosine, sine = twiddle_ref[0], twiddle_ref[1]
    second = second_ref[...]

    def first_stage(values):
        return dot(first_ref[...], jnp.concatenate([values, values], axis=0))

    def turn_forward(stage):
        parts = []
        for at in range(0, stage.shape[1], LANES):
            real, imag = stage[:kept, at : at + LANES], stage[kept:, at : at + LANES]
            turned = jnp.concatenate([real * cosine + imag * sine, imag * cosine - real * sine], axis=1)
            parts.append(turned.astype(jnp.bfloat16))
        return parts

    def second_stage(parts):
        both = dot(jnp.concatenate(parts, axis=0), second)
        cuts = [both[at : at + kept] for at in range(0, both.shape[0], kept)]
        return [(cut[:, :LANES], cut[:, LANES:]) for cut in cuts]

    def swapped(real, imag):
        return jnp.concatenate([imag, real], axis=1).astype(jnp.bfloat16)

    def last_stage(swapped_pairs):
        parts = []
        for imag, real in swapped_pairs:
            turned = jnp.concatenate([real * cosine - imag * sine, imag * cosine + real * sine], axis=0)
            parts.append(turned.astype(jnp.bfloat16))
        both = dot(last_ref[...], jnp.concatenate(parts, axis=1))
        return both[:rows] + both[rows:]

    taps_in = jnp.concatenate([part[2 * piece : 2 * piece + taps] for part in got], axis=0).astype(jnp.bfloat16)
    signal_in = jnp.concatenate([gather(group, 0) for group in range(groups)] + [taps_in], axis=1)
    grad_in = jnp.concatenate([gather(group, piece) for group in range(groups)], axis=1)
    signal_stage = first_stage(signal_in)
    grad_stage = first_stage(grad_in)
    forward = second_stage(turn_forward(signal_stage) + turn_forward(grad_stage))
    signals, (tap_real, tap_imag), grads = forward[:groups], forward[groups], forward[groups + 1 :]
    conv_parts = [swapped(r * tap_real - i * tap_imag, r * tap_imag + i * tap_real) for r, i in signals]
    back_parts = [swapped(tap_real * r + tap_imag * i, tap_real * i - tap_imag * r) for r, i in grads]
    corr_real = sum(sr * gr + si * gi for (sr, si), (gr, gi) in zip(signals, grads)) * scale
    corr_imag = sum(sr * gi - si * gr for (sr, si), (gr, gi) in zip(signals, grads)) * scale
    result = last_stage(second_stage(conv_parts + back_parts + [swapped(corr_real, corr_imag)]))
    for peer in range(peers):
        piece_rows = result[peer * piece : (peer + 1) * piece]
        for group in range(groups):
            cut = lambda sequence: piece_rows[:, sequence * LANES : (sequence + 1) * LANES]
            message = jnp.concatenate([cut(group), cut(groups + group), cut(count)], axis=0)
            out_ref[slots[peer * groups + group]] = message.astype(jnp.bfloat16)


def spectral_products(got, piece, groups, peers, scale):
    rows = peers * piece
    tables = dft_tables(rows)
    vmem = pl.BlockSpec(memory_space=pltpu.VMEM)
    return pl.pallas_call(
        functools.partial(spectral_kernel, groups, peers, scale),
        out_shape=jax.ShapeDtypeStruct((got.shape[0], 3 * piece, LANES), jnp.bfloat16),
        in_specs=[vmem] * 5,
        out_specs=vmem,
        compiler_params=pltpu.CompilerParams(vmem_limit_bytes=24 * 2**20),
        name="spectral_products",
    )(got, *[jnp.asarray(table) for table in tables])


def tile_rows(values):
    return values.reshape(values.shape[0], values.shape[1] // LANES, LANES)


def pack_kernel(
    groups,
    signal_hbm,
    gating_hbm,
    cotangent_hbm,
    filters_hbm,
    weight_hbm,
    message_ref,
    column_ref,
    signal_ref,
    gating_ref,
    cotangent_ref,
    taps_ref,
    weight_ref,
    sems,
):
    channels, length = signal_ref.shape
    share = length // groups
    start = pl.multiple_of(lax.axis_index("chan") * share, share)
    copies = [
        pltpu.make_async_copy(source, target, sems.at[at])
        for at, (source, target) in enumerate(
            [
                (cotangent_hbm, cotangent_ref),
                (gating_hbm, gating_ref),
                (signal_hbm, signal_ref),
                (filters_hbm.at[:, pl.ds(start, share)], taps_ref),
                (weight_hbm, weight_ref),
            ]
        )
    ]
    for copy in (copies[2], *copies[:2], *copies[3:]):
        copy.start()
    cotangent_copy, gating_copy, signal_copy, taps_copy, weight_copy = copies
    at = length // (TILE * LANES)

    def put(first, stop, values):
        rows = tile_rows(values).reshape(channels, stop - first, TILE, LANES)
        message_ref[:, first:stop] = rows.astype(jnp.bfloat16)

    signal_copy.wait()
    put(0, at, signal_ref[...].astype(jnp.float32))
    cotangent_copy.wait()
    gating_copy.wait()
    put(at, 2 * at, cotangent_ref[...].astype(jnp.float32) * gating_ref[...].astype(jnp.float32))
    taps_copy.wait()
    put(2 * at, message_ref.shape[1], taps_ref[...])
    weight_copy.wait()
    square = (channels, channels)
    diagonal = lax.broadcasted_iota(jnp.int32, square, 0) == lax.broadcasted_iota(jnp.int32, square, 1)
    weight = jnp.sum(jnp.where(diagonal, jnp.broadcast_to(weight_ref[...], square), 0.0), axis=1, keepdims=True)
    column_ref[...] = jnp.broadcast_to(weight, column_ref.shape)


def pack(signal, gating, cotangent, filters, skip_weight, groups):
    channels, length = signal.shape
    vmem = pl.BlockSpec(memory_space=pltpu.VMEM)
    operands = (signal, gating, cotangent, filters, skip_weight[None, :])
    return pl.pallas_call(
        functools.partial(pack_kernel, groups),
        out_shape=(
            jax.ShapeDtypeStruct((channels, (2 * length + length // groups) // (TILE * LANES), TILE, LANES), jnp.bfloat16),
            jax.ShapeDtypeStruct((channels, LANES), jnp.float32),
        ),
        in_specs=[pl.BlockSpec(memory_space=pltpu.HBM)] * 5,
        out_specs=(vmem, vmem),
        scratch_shapes=[pltpu.VMEM(signal.shape, jnp.bfloat16)] * 3
        + [
            pltpu.VMEM((filters.shape[0], length // groups), jnp.float32),
            pltpu.VMEM((1, channels), jnp.float32),
            pltpu.SemaphoreType.DMA((5,)),
        ],
        compiler_params=pltpu.CompilerParams(vmem_limit_bytes=16 * 2**20),
        name="pack",
    )(*[pltpu.with_memory_space_constraint(operand, pltpu.HBM) for operand in operands])


def finish_kernel(groups, home_ref, signal_ref, gating_ref, cotangent_ref, column_ref, signal_out, gating_out, filters_out):
    channels, length = signal_ref.shape
    piece = length // LANES
    share = channels // groups
    home = home_ref[...].astype(jnp.float32).reshape(channels, 3 * length)
    cotangent = cotangent_ref[...].astype(jnp.float32)
    gated = (cotangent * gating_ref[...].astype(jnp.float32)).astype(jnp.bfloat16).astype(jnp.float32)
    weight = column_ref[:, :1]
    outputs = home[:, :length] + weight * signal_ref[...].astype(jnp.float32)
    gating_out[...] = (cotangent * outputs).astype(jnp.bfloat16)
    signal_out[...] = (home[:, length : 2 * length] + weight * gated).astype(jnp.bfloat16)
    first = pl.multiple_of(lax.axis_index("chan") * share, share)
    corr = home_ref[pl.ds(first, share), 2 * piece :, :].astype(jnp.float32)
    filters_out[...] = corr.reshape(share, length)


def finish(home, signal, gating, cotangent, column, groups):
    channels, length = signal.shape
    vmem = pl.BlockSpec(memory_space=pltpu.VMEM)
    return pl.pallas_call(
        functools.partial(finish_kernel, groups),
        out_shape=(
            jax.ShapeDtypeStruct(signal.shape, jnp.bfloat16),
            jax.ShapeDtypeStruct(signal.shape, jnp.bfloat16),
            jax.ShapeDtypeStruct((channels // groups, length), jnp.float32),
        ),
        in_specs=[vmem] * 5,
        out_specs=(vmem,) * 3,
        compiler_params=pltpu.CompilerParams(vmem_limit_bytes=16 * 2**20),
        name="finish",
    )(home, signal, gating, cotangent, column)


def filter_per_device(signal, gating, cotangent, filters, skip_weight):
    peers = lax.axis_size("ctx")
    groups = lax.axis_size("chan")
    message, column = pack(signal, gating, cotangent, filters, skip_weight, groups)
    exchange = functools.partial(
        lax.all_to_all,
        axis_name=("ctx", "chan"),
        split_axis=0,
        concat_axis=0,
        axis_index_groups=[slot_order(peers, groups)],
        tiled=True,
    )
    got = exchange(message)
    scale = 1.0 / math.sqrt(signal.shape[1] * peers * groups)
    result = spectral_products(got, signal.shape[1] // LANES, groups, peers, scale)
    home = exchange(result)
    return finish(home, signal, gating, cotangent, column, groups)


def product(form, left, right):
    return jnp.einsum(
        form, left, right, precision=lax.Precision.HIGHEST, preferred_element_type=jnp.float32
    )


def phases(left_idx, right_idx, period):
    joined = left_idx[:, None] * right_idx[None, :] % period
    return joined.astype(jnp.float32) * (2.0 * math.pi / period)


def indices(total):
    return jnp.arange(total, dtype=jnp.int32)


def turn_forward(real_part, imag_part, angles):
    cosine = jnp.cos(angles)
    sine_part = jnp.sin(angles)
    return (real_part * cosine + imag_part * sine_part, imag_part * cosine - real_part * sine_part)


def turn_back(real_part, imag_part, angles):
    cosine = jnp.cos(angles)
    sine_part = jnp.sin(angles)
    return (real_part * cosine - imag_part * sine_part, imag_part * cosine + real_part * sine_part)


def first_pass(blocks, position, peer_count):
    height, length = blocks.shape
    piece_len = length // peer_count
    padded = 2 * peer_count * length
    shaped = blocks.reshape(height, peer_count, piece_len)
    angles = phases(indices(peer_count), indices(2 * peer_count), 2 * peer_count)
    real_part = product("rdm,dk->rmk", shaped, jnp.cos(angles))
    imag_part = -product("rdm,dk->rmk", shaped, jnp.sin(angles))
    offsets = position * piece_len + indices(piece_len)
    real_part, imag_part = turn_forward(
        real_part, imag_part, phases(offsets, indices(2 * peer_count), padded)
    )
    return jnp.stack([real_part, imag_part])


def second_pass(columns, peer_count):
    height, piece_len = (columns.shape[1], columns.shape[2])
    length = piece_len * peer_count
    real_part = columns[0].reshape(height, piece_len, peer_count, 2)
    imag_part = columns[1].reshape(height, piece_len, peer_count, 2)
    angles = phases(indices(peer_count), indices(peer_count), peer_count)
    cosine = jnp.cos(angles)
    sine_part = jnp.sin(angles)
    real_one = product("rmeb,ea->rbma", real_part, cosine) + product(
        "rmeb,ea->rbma", imag_part, sine_part
    )
    imag_one = product("rmeb,ea->rbma", imag_part, cosine) - product(
        "rmeb,ea->rbma", real_part, sine_part
    )
    real_one, imag_one = turn_forward(
        real_one, imag_one, phases(indices(piece_len), indices(peer_count), length)
    )
    angles = phases(indices(piece_len), indices(piece_len), piece_len)
    cosine = jnp.cos(angles)
    sine_part = jnp.sin(angles)
    real_two = product("rbma,mc->rbca", real_one, cosine) + product(
        "rbma,mc->rbca", imag_one, sine_part
    )
    imag_two = product("rbma,mc->rbca", imag_one, cosine) - product(
        "rbma,mc->rbca", real_one, sine_part
    )
    return jnp.stack([real_two.reshape(height, 2, length), imag_two.reshape(height, 2, length)])


def inverse_first(spectrum, position, peer_count):
    height, length = (spectrum.shape[1], spectrum.shape[3])
    piece_len = length // peer_count
    padded = 2 * peer_count * length
    real_part = spectrum[0].reshape(height, 2, piece_len, peer_count)
    imag_part = spectrum[1].reshape(height, 2, piece_len, peer_count)
    angles = phases(indices(piece_len), indices(piece_len), piece_len)
    cosine = jnp.cos(angles)
    sine_part = jnp.sin(angles)
    real_one = product("rbca,cm->rbma", real_part, cosine) - product(
        "rbca,cm->rbma", imag_part, sine_part
    )
    imag_one = product("rbca,cm->rbma", imag_part, cosine) + product(
        "rbca,cm->rbma", real_part, sine_part
    )
    real_one, imag_one = turn_back(
        real_one, imag_one, phases(indices(piece_len), indices(peer_count), length)
    )
    angles = phases(indices(peer_count), indices(peer_count), peer_count)
    cosine = jnp.cos(angles)
    sine_part = jnp.sin(angles)
    real_two = product("rbma,ae->rmeb", real_one, cosine) - product(
        "rbma,ae->rmeb", imag_one, sine_part
    )
    imag_two = product("rbma,ae->rmeb", imag_one, cosine) + product(
        "rbma,ae->rmeb", real_one, sine_part
    )
    offsets = (indices(peer_count)[None, :] * piece_len + indices(piece_len)[:, None]).reshape(-1)
    freq_bins = 2 * position + indices(2)
    angles = phases(offsets, freq_bins, padded).reshape(piece_len, peer_count, 2)
    real_two, imag_two = turn_back(real_two, imag_two, angles)
    return jnp.stack(
        [
            real_two.reshape(height, piece_len, 2 * peer_count),
            imag_two.reshape(height, piece_len, 2 * peer_count),
        ]
    )


def inverse_second(received, peer_count):
    height, piece_len = (received.shape[1], received.shape[2])
    length = piece_len * peer_count
    padded = 2 * peer_count * length
    angles = phases(indices(2 * peer_count), indices(peer_count), 2 * peer_count)
    signal_out = product("rmk,kd->rdm", received[0], jnp.cos(angles)) - product(
        "rmk,kd->rdm", received[1], jnp.sin(angles)
    )
    return (signal_out / padded).reshape(height, length)


def split_transforms(signal, gating, cotangent, filters, skip_weight):
    peer_count = lax.axis_size("ctx")
    position = lax.axis_index("ctx")
    channels, length = signal.shape
    count_filters = filters.shape[0]
    local_group = channels // count_filters
    gated_grad = (cotangent.astype(jnp.float32) * gating.astype(jnp.float32)).astype(jnp.bfloat16)
    signal_blocks, gated_blocks = (
        lax.all_to_all(signal, "ctx", split_axis=1, concat_axis=1, tiled=True),
        lax.all_to_all(gated_grad, "ctx", split_axis=1, concat_axis=1, tiled=True),
    )
    tap_blocks = lax.all_to_all(filters, "ctx", split_axis=1, concat_axis=1, tiled=True)
    signal_cols, gated_cols, tap_cols = (
        lax.all_to_all(
            first_pass(signal_blocks.astype(jnp.float32), position, peer_count),
            "ctx",
            split_axis=3,
            concat_axis=3,
            tiled=True,
        ),
        lax.all_to_all(
            first_pass(gated_blocks.astype(jnp.float32), position, peer_count),
            "ctx",
            split_axis=3,
            concat_axis=3,
            tiled=True,
        ),
        lax.all_to_all(
            first_pass(tap_blocks, position, peer_count),
            "ctx",
            split_axis=3,
            concat_axis=3,
            tiled=True,
        ),
    )
    signal_spec = second_pass(signal_cols, peer_count).reshape(
        2, local_group, count_filters, 2, length
    )
    gated_spec = second_pass(gated_cols, peer_count).reshape(
        2, local_group, count_filters, 2, length
    )
    tap_spec = second_pass(tap_cols, peer_count)
    tap_real, tap_imag = (tap_spec[0], tap_spec[1])
    sig_real, sig_imag = (signal_spec[0], signal_spec[1])
    gated_real, gated_imag = (gated_spec[0], gated_spec[1])
    forward_spec = jnp.stack(
        [sig_real * tap_real - sig_imag * tap_imag, sig_real * tap_imag + sig_imag * tap_real]
    ).reshape(2, channels, 2, length)
    back_spec = jnp.stack(
        [
            tap_real * gated_real + tap_imag * gated_imag,
            tap_real * gated_imag - tap_imag * gated_real,
        ]
    ).reshape(2, channels, 2, length)
    corr_spec = jnp.stack(
        [
            jnp.sum(sig_real * gated_real + sig_imag * gated_imag, axis=0),
            jnp.sum(sig_real * gated_imag - sig_imag * gated_real, axis=0),
        ]
    )
    forward_cols, back_cols, corr_cols = (
        lax.all_to_all(
            inverse_first(forward_spec, position, peer_count),
            "ctx",
            split_axis=3,
            concat_axis=3,
            tiled=True,
        ),
        lax.all_to_all(
            inverse_first(back_spec, position, peer_count),
            "ctx",
            split_axis=3,
            concat_axis=3,
            tiled=True,
        ),
        lax.all_to_all(
            inverse_first(corr_spec, position, peer_count),
            "ctx",
            split_axis=3,
            concat_axis=3,
            tiled=True,
        ),
    )
    conv_time, back_time, corr_time = (
        lax.all_to_all(
            inverse_second(forward_cols, peer_count), "ctx", split_axis=1, concat_axis=1, tiled=True
        ),
        lax.all_to_all(
            inverse_second(back_cols, peer_count), "ctx", split_axis=1, concat_axis=1, tiled=True
        ),
        lax.all_to_all(
            inverse_second(corr_cols, peer_count), "ctx", split_axis=1, concat_axis=1, tiled=True
        ),
    )
    corr_time = lax.psum_scatter(corr_time, "chan", scatter_dimension=0, tiled=True)
    weight = skip_weight[:, None]
    outputs = conv_time + weight * signal.astype(jnp.float32)
    grad_gating = (cotangent.astype(jnp.float32) * outputs).astype(jnp.bfloat16)
    grad_signal = (back_time + weight * gated_grad.astype(jnp.float32)).astype(jnp.bfloat16)
    normal_scale = 1.0 / math.sqrt(length * peer_count * local_group * lax.axis_size("chan"))
    grad_filters = corr_time * normal_scale
    return (grad_signal, grad_gating, grad_filters)


def per_device(signal, gating, cotangent, filters, skip_weight):
    peers, groups = lax.axis_size("ctx"), lax.axis_size("chan")
    channels, length = signal.shape
    one_each = channels == filters.shape[0] == peers * groups
    piece = length // LANES
    whole_tiles = length % (8 * LANES) == 0 and piece % groups == 0
    if one_each and whole_tiles and (peers * piece) % 16 == 0 and (piece // groups) % TILE == 0:
        return filter_per_device(signal, gating, cotangent, filters, skip_weight)
    return split_transforms(signal, gating, cotangent, filters, skip_weight)


def solution(mesh):
    in_specs = (P("chan", "ctx"), P("chan", "ctx"), P("chan", "ctx"), P(None, "ctx"), P("chan"))
    out_specs = (P("chan", "ctx"), P("chan", "ctx"), P("chan", "ctx"))
    return jax.shard_map(
        per_device, mesh=mesh, in_specs=in_specs, out_specs=out_specs, check_vma=False
    )
```
